32 devices in a mesh: dp: 8 (over z, y), mp: 4 (over x, core).
Axes of the slice: x: 2, y: 2, z: 4, core: 2. Of those that a mesh axis runs over, the one named last changes fastest.
Arguments:
- byte_embeds: bfloat16 [4, 4096, 1024], P('mp', 'dp'), may hold values from -6 to 6
- lengths: int32 [4], replicated, may hold values from 3585 to 4096, as said below
- patch_in: bfloat16 [8388608], P(('dp', 'mp')), may hold values from -0.0625 to 0.0625
- mixer_in: bfloat16 [4489216], P(('dp', 'mp')), may hold values from -0.1875 to 0.1875
- mixer_out: bfloat16 [2097152], P(('dp', 'mp')), may hold values from -0.125 to 0.125
- patch_out: bfloat16 [8388608], P(('dp', 'mp')), may hold values from -0.1875 to 0.1875
- attend_in: bfloat16 [3145728], P(('dp', 'mp')), may hold values from -0.1875 to 0.1875
- attend_out: bfloat16 [1048576], P(('dp', 'mp')), may hold values from -0.375 to 0.375
- gate_weight: bfloat16 [1024, 4096], P('dp', 'mp'), may hold values from -0.1875 to 0.1875
- up_weight: bfloat16 [1024, 4096], P('dp', 'mp'), may hold values from -0.1875 to 0.1875
- down_weight: bfloat16 [4096, 1024], P('mp', 'dp'), may hold values from -0.09375 to 0.09375
- norm_global: float32 [1024], replicated, may hold values from 0.25 to 1.75
- conv_weight: float32 [4, 2304], replicated, may hold values from -3 to 3
- conv_bias: float32 [2304], replicated, may hold values from -3 to 3
- step_bias: float32 [32], replicated, may hold values from -1 to 1
- decay_rate: float32 [32], replicated, may hold values from -8 to -1
- skip_gain: float32 [32], replicated, may hold values from 0.5 to 1.5
- norm_gated: float32 [2048], replicated, may hold values from 0.25 to 1.75
- norm_attend: float32 [1024], replicated, may hold values from 0.25 to 1.75
- norm_feed: float32 [1024], replicated, may hold values from 0.25 to 1.75
- cotangent: bfloat16 [4, 4096, 1024], P('mp', 'dp'), may hold values from -6 to 6
Outputs:
- out_bytes: bfloat16 [4, 4096, 1024], P('mp', 'dp')
- grad_bytes: bfloat16 [4, 4096, 1024], P('mp', 'dp')
- grad_patch_in: float32 [8388608], P(('dp', 'mp'))
- grad_mixer_in: float32 [4489216], P(('dp', 'mp'))
- grad_mixer_out: float32 [2097152], P(('dp', 'mp'))
- grad_patch_out: float32 [8388608], P(('dp', 'mp'))
- grad_attend_in: float32 [3145728], P(('dp', 'mp'))
- grad_attend_out: float32 [1048576], P(('dp', 'mp'))
- grad_gate: float32 [1024, 4096], P('dp', 'mp')
- grad_up: float32 [1024, 4096], P('dp', 'mp')
- grad_down: float32 [4096, 1024], P('mp', 'dp')
- grad_norm_global: float32 [1024], replicated
- grad_conv_weight: float32 [4, 2304], replicated
- grad_conv_bias: float32 [2304], replicated
- grad_step_bias: float32 [32], replicated
- grad_decay_rate: float32 [32], replicated
- grad_skip_gain: float32 [32], replicated
- grad_norm_gated: float32 [2048], replicated
- grad_norm_attend: float32 [1024], replicated
- grad_norm_feed: float32 [1024], replicated
The draws below stay inside these ranges and needn't reach their ends.
Inputs may be any that keep to these rules, and one draw needn't show every extreme that they name: `lengths`: every sequence uses more than its first (7) * 512 bytes; one sequence uses all 4096.
All inputs are finite; a program needn't handle non-finite values.
Results may differ from the reference program's by a relative error of at most 0.024.
Values may be sent and summed in bfloat16 or wider, within the bound.
A program may use at most 448 MiB of HBM per device.

```python
import jax
import jax.numpy as jnp
from jax import lax

D = 1024
PATCH = 8
INNER = 2048
HEADS_M = 32
STATE = 128
CONV = 4
HEADS_A = 16
FF = 4096
PATCH_DEV = 64
HEAD_M = 64
HEAD_A = 64
CONV_CH = 2304
PROJ = 4384
BYTE_DEV = 512
SEQ_BYTES = 4096
GROUPS = 4
N_DP = 8
N_MP = 4


def draw_lengths(key, part):
    first, second = jax.random.split(jax.random.fold_in(key, 11))
    least = (N_DP - 1) * BYTE_DEV + 1
    most = N_DP * BYTE_DEV
    values = jax.random.randint(first, (N_MP,), least, most + 1)
    chosen = jax.random.randint(second, (), 0, N_MP)
    return jnp.where(jnp.arange(N_MP) == chosen, most, values).astype(jnp.int32)


def level_of(own_key, dims, cuts, low, top_value):
    level, own = 1.0, jax.random.fold_in(own_key, 6)
    for position, parts in cuts:
        steps = jnp.exp(jax.random.uniform(jax.random.fold_in(own, position), (parts,), jnp.float32, low / len(cuts), top_value / len(cuts)))
        level = level * jnp.repeat(steps, dims[position] // parts).reshape([-1 if axis == position else 1 for axis in range(len(dims))])
    return level


def centred(stream_key, shape, scale, most, shards=(), held_as=jnp.bfloat16):
    values = scale * jax.random.normal(stream_key, shape, jnp.float32)
    if shards:
        values = values * level_of(stream_key, shape, shards, -0.22, 0.18)
    return jnp.clip(values, -most, most).astype(held_as)


def setup_inputs(seed: int = 0) -> dict:
    streams_of = jax.random.split(jax.random.key(seed), 22)
    byte_embeds = centred(streams_of[0], (GROUPS, SEQ_BYTES, D), 1.0, 6.0, ((0, 4), (1, 8)))
    lengths = draw_lengths(jax.random.fold_in(streams_of[21], 71), 0)
    patch_in = centred(streams_of[2], (8 * D * D,), (8 * D) ** -0.5, 0.0625, ((0, 32),))
    mixer_in = centred(streams_of[3], (D * PROJ,), D ** -0.5, 0.1875, ((0, 32),))
    mixer_out = centred(streams_of[4], (INNER * D,), INNER ** -0.5, 0.125, ((0, 32),))
    patch_out = centred(streams_of[5], (8 * D * D,), D ** -0.5, 0.1875, ((0, 32),))
    attend_in = centred(streams_of[6], (3 * D * D,), D ** -0.5, 0.1875, ((0, 32),))
    attend_out = centred(streams_of[7], (D * D,), (D // 4) ** -0.5, 0.375, ((0, 32),))
    gate_weight = centred(streams_of[8], (D, FF), D ** -0.5, 0.1875, ((0, 8), (1, 4)))
    up_weight = centred(streams_of[9], (D, FF), D ** -0.5, 0.1875, ((0, 8), (1, 4)))
    down_weight = centred(streams_of[10], (FF, D), FF ** -0.5, 0.09375, ((0, 4), (1, 8)))
    norm_global = jnp.clip(1.0 + 0.15 * jax.random.normal(streams_of[11], (D,), jnp.float32), 0.25, 1.75)
    conv_weight = centred(streams_of[12], (CONV, CONV_CH), CONV ** -0.5, 3.0, (), jnp.float32)
    conv_bias = centred(streams_of[13], (CONV_CH,), 0.5, 3.0, (), jnp.float32)
    step_bias = jnp.clip(jax.random.uniform(streams_of[14], (HEADS_M,), jnp.float32, -1.0, 1.0), -1.0, 1.0)
    decay_rate = jnp.clip(jax.random.uniform(streams_of[15], (HEADS_M,), jnp.float32, -8.0, -1.0), -8.0, -1.0)
    skip_gain = jnp.clip(jax.random.uniform(streams_of[16], (HEADS_M,), jnp.float32, 0.5, 1.5), 0.5, 1.5)
    norm_gated = jnp.clip(1.0 + 0.15 * jax.random.normal(streams_of[17], (INNER,), jnp.float32), 0.25, 1.75)
    norm_attend = jnp.clip(1.0 + 0.15 * jax.random.normal(streams_of[18], (D,), jnp.float32), 0.25, 1.75)
    norm_feed = jnp.clip(1.0 + 0.15 * jax.random.normal(streams_of[19], (D,), jnp.float32), 0.25, 1.75)
    cotangent = centred(streams_of[20], (GROUPS, SEQ_BYTES, D), 1.0, 6.0, ((0, 4), (1, 8)))
    return {"byte_embeds": byte_embeds, "lengths": lengths, "patch_in": patch_in, "mixer_in": mixer_in, "mixer_out": mixer_out, "patch_out": patch_out, "attend_in": attend_in, "attend_out": attend_out, "gate_weight": gate_weight, "up_weight": up_weight, "down_weight": down_weight, "norm_global": norm_global, "conv_weight": conv_weight, "conv_bias": conv_bias, "step_bias": step_bias, "decay_rate": decay_rate, "skip_gain": skip_gain, "norm_gated": norm_gated, "norm_attend": norm_attend, "norm_feed": norm_feed, "cotangent": cotangent}


HIGH = lax.Precision.HIGHEST
EPSILON = 1e-05

@jax.custom_vjp
def low(v):
    return lax.optimization_barrier(v.astype(jnp.bfloat16)).astype(jnp.float32)

@jax.custom_vjp
def low_back(v):
    return v

def low_keep(v):
    return (low(v), None)

def low_pass(kept, grad):
    return (grad,)

def back_keep(v):
    return (v, None)

def back_low(kept, grad):
    return (low(grad),)
low.defvjp(low_keep, low_pass)
low_back.defvjp(back_keep, back_low)

def dot_high(left, right):
    return jnp.dot(left, right, precision=HIGH, preferred_element_type=jnp.float32)

def root_norm(values, gain):
    return values * lax.rsqrt(lax.optimization_barrier(jnp.mean(values * values, axis=-1, keepdims=True)) + EPSILON) * gain

def convolve(extended, conv_weight, conv_bias):
    count = extended.shape[0] - (CONV - 1)
    total = conv_bias + conv_weight[0] * extended[0:count]
    for shift in range(1, CONV):
        total = total + conv_weight[shift] * extended[shift:shift + count]
    return jax.nn.silu(total)

def block_output(heads_x, input_map, output_map, step_size, log_decay, carried):
    count = log_decay.shape[0]
    decay_t = log_decay.T
    spread = decay_t[:, :, None] - decay_t[:, None, :]
    causal = jnp.arange(count)[:, None] >= jnp.arange(count)[None, :]
    factor = jnp.exp(jnp.where(causal[None], spread, -jnp.inf))
    scores = jnp.dot(output_map, input_map.T, precision=HIGH)
    weights = factor * scores[None] * step_size.T[:, None, :]
    inner = jnp.einsum('hts,shp->thp', weights, heads_x, precision=HIGH)
    outer = jnp.einsum('tn,hpn->thp', output_map, carried, precision=HIGH) * jnp.exp(log_decay)[:, :, None]
    return inner + outer

def block_state(heads_x, input_map, step_size, log_decay):
    last = log_decay[-1]
    weight = jnp.exp(last[None, :] - log_decay) * step_size
    own = jnp.einsum('sh,shp,sn->hpn', weight, heads_x, input_map, precision=HIGH)
    return (jnp.exp(last), own)

def patch_attention(attend_proj):
    count = attend_proj.shape[0]
    patches = count // PATCH
    query = attend_proj[:, :D].reshape(patches, PATCH, HEADS_A, HEAD_A)
    keyed = attend_proj[:, D:2 * D].reshape(patches, PATCH, HEADS_A, HEAD_A)
    valued = attend_proj[:, 2 * D:].reshape(patches, PATCH, HEADS_A, HEAD_A)
    scores = jnp.einsum('pihd,pjhd->phij', query, keyed, precision=HIGH) * HEAD_A ** (-0.5)
    causal = jnp.arange(PATCH)[:, None] >= jnp.arange(PATCH)[None, :]
    scores = jnp.where(causal, scores, -jnp.inf)
    top = lax.optimization_barrier(jnp.max(scores, axis=-1, keepdims=True))
    expo = jnp.exp(scores - top)
    probs = expo / lax.optimization_barrier(jnp.sum(expo, axis=-1, keepdims=True))
    result = jnp.einsum('phij,pjhd->pihd', probs, valued, precision=HIGH)
    return result.reshape(count, D)

def group_forward(embeds, keep, weights):
    w_patch_in, w_mixer_in, w_mixer_out, w_patch_out, w_attend, w_attend_out, w_gate, w_up, w_down, norm_global, conv_weight, conv_bias, step_bias, decay_rate, skip_gain, norm_gated, norm_attend, norm_feed = weights
    inputs = embeds * keep
    count = inputs.shape[0]
    patches = count // PATCH
    global_in = low_back(dot_high(inputs.reshape(patches, PATCH * D), w_patch_in))
    normed = low(root_norm(global_in, norm_global))
    projected = low_back(dot_high(normed, w_mixer_in))
    gate_part = projected[:, :INNER]
    conv_input = projected[:, INNER:2 * INNER + 2 * STATE]
    step_raw = projected[:, 2 * INNER + 2 * STATE:]
    extended = jnp.concatenate([jnp.zeros((CONV - 1, CONV_CH), jnp.float32), conv_input], axis=0)
    activated = convolve(extended, conv_weight, conv_bias)
    heads_x = activated[:, :INNER].reshape(patches, HEADS_M, HEAD_M)
    input_map = activated[:, INNER:INNER + STATE]
    output_map = activated[:, INNER + STATE:]
    step_size = jax.nn.softplus(step_raw + step_bias)
    blocks = patches // PATCH_DEV
    rate = jnp.exp(decay_rate)

    def step(carried, item):
        block_x, block_in, block_out, block_step = item
        log_decay = jnp.cumsum(block_step * -rate, axis=0)
        result = block_output(block_x, block_in, block_out, block_step, log_decay, carried)
        decay_all, own = block_state(block_x, block_in, block_step, log_decay)
        return (decay_all[:, None, None] * carried + own, result)
    start = jnp.zeros((HEADS_M, HEAD_M, STATE), jnp.float32)
    items = (heads_x.reshape(blocks, PATCH_DEV, HEADS_M, HEAD_M), input_map.reshape(blocks, PATCH_DEV, STATE), output_map.reshape(blocks, PATCH_DEV, STATE), step_size.reshape(blocks, PATCH_DEV, HEADS_M))
    _, results = lax.scan(jax.checkpoint(step), start, items)
    values = results.reshape(patches, HEADS_M, HEAD_M) + skip_gain[None, :, None] * heads_x
    gated = values.reshape(patches, INNER) * jax.nn.silu(gate_part)
    mixed = low(root_norm(gated, norm_gated))
    global_out = global_in + low_back(dot_high(mixed, w_mixer_out))
    slots = low_back(dot_high(low(global_out), w_patch_out)).reshape(count, D)
    local_in = inputs + slots
    attend_normed = low(root_norm(local_in, norm_attend))
    attend_proj = low_back(dot_high(attend_normed, w_attend))
    attended = low(patch_attention(attend_proj))
    after_attend = local_in + low_back(dot_high(attended, w_attend_out))
    feed_normed = low(root_norm(after_attend, norm_feed))
    gate_value = low_back(dot_high(feed_normed, w_gate))
    up_value = low_back(dot_high(feed_normed, w_up))
    hidden = low(jax.nn.silu(gate_value) * up_value)
    final = after_attend + low_back(dot_high(hidden, w_down))
    return final * keep

def reference(byte_embeds, lengths, patch_in, mixer_in, mixer_out, patch_out, attend_in, attend_out, gate_weight, up_weight, down_weight, norm_global, conv_weight, conv_bias, step_bias, decay_rate, skip_gain, norm_gated, norm_attend, norm_feed, cotangent):
    params = (patch_in.astype(jnp.float32).reshape(PATCH * D, D), mixer_in.astype(jnp.float32).reshape(D, PROJ), mixer_out.astype(jnp.float32).reshape(INNER, D), patch_out.astype(jnp.float32).reshape(D, PATCH * D), attend_in.astype(jnp.float32).reshape(D, 3 * D), attend_out.astype(jnp.float32).reshape(D, D), gate_weight.astype(jnp.float32), up_weight.astype(jnp.float32), down_weight.astype(jnp.float32), norm_global, conv_weight, conv_bias, step_bias, decay_rate, skip_gain, norm_gated, norm_attend, norm_feed)

    def one_group(totals, item):
        embeds, cot, length = item
        keep = (jnp.arange(embeds.shape[0], dtype=jnp.int32) < length).astype(jnp.float32)[:, None]

        def forward(inputs, *weights):
            return group_forward(inputs, keep, weights)
        result, pull = jax.vjp(forward, embeds.astype(jnp.float32), *params)
        grads = pull(cot.astype(jnp.float32))
        totals = tuple((total + grad for total, grad in zip(totals, grads[1:])))
        return (totals, (result.astype(jnp.bfloat16), grads[0].astype(jnp.bfloat16)))
    zeros = tuple((jnp.zeros_like(param) for param in params))
    totals, (results, grad_bytes) = lax.scan(one_group, zeros, (byte_embeds, cotangent, lengths))
    return (results, grad_bytes, totals[0].reshape(-1), totals[1].reshape(-1), totals[2].reshape(-1), totals[3].reshape(-1), totals[4].reshape(-1), totals[5].reshape(-1), totals[6], totals[7], totals[8], totals[9], totals[10], totals[11], totals[12], totals[13], totals[14], totals[15], totals[16], totals[17])
```

```python
import functools

import jax
import jax.numpy as jnp
from jax import lax
from jax.experimental import pallas as pl
from jax.experimental.pallas import tpu as pltpu
from jax.sharding import PartitionSpec as P

D = 1024
PATCH = 8
INNER = 2048
HEADS_M = 32
STATE = 128
CONV = 4
HEADS_A = 16
HEAD_M = 64
HEAD_A = 64
PROJ = 4384
LANE = 128

HIGH = lax.Precision.HIGHEST
EPSILON = 1e-05
BF = jnp.bfloat16
F32 = jnp.float32


def exchange_kernel(plan, sizes, *refs):
    count = len(plan)
    sources, targets = refs[:count], refs[count : 2 * count]
    sems = refs[2 * count :]
    local_sem = sems[0]
    axes = sorted({axis for _, axis in plan})
    me = {axis: lax.axis_index(axis) for axis in axes}
    barrier = pltpu.get_barrier_semaphore()
    total = 0
    for axis in axes:
        for k in range(1, sizes[axis]):
            pl.semaphore_signal(
                barrier,
                inc=1,
                device_id={axis: lax.rem(me[axis] + k, sizes[axis])},
                device_id_type=pl.DeviceIdType.MESH,
            )
        total += sizes[axis] - 1
    pl.semaphore_wait(barrier, total)
    copies = []
    for index, (kind, axis) in enumerate(plan):
        send, recv = sems[1 + 2 * index], sems[2 + 2 * index]
        for k in range(1, sizes[axis]):
            peer = lax.rem(me[axis] + k, sizes[axis])
            source = sources[index].at[peer] if kind == "a2a" else sources[index]
            copy = pltpu.make_async_remote_copy(
                src_ref=source,
                dst_ref=targets[index].at[me[axis]],
                send_sem=send.at[k - 1],
                recv_sem=recv.at[k - 1],
                device_id={axis: peer},
                device_id_type=pl.DeviceIdType.MESH,
            )
            copy.start()
            copies.append(copy)
    own = []
    for index, (kind, axis) in enumerate(plan):
        source = sources[index].at[me[axis]] if kind == "a2a" else sources[index]
        copy = pltpu.make_async_copy(source, targets[index].at[me[axis]], local_sem.at[index])
        copy.start()
        own.append(copy)
    for copy in own:
        copy.wait()
    for copy in copies:
        copy.wait()


def exchange(ident, *steps):
    plan = tuple((kind, axis) for kind, axis, _ in steps)
    arrays = [array for _, _, array in steps]
    sizes = {axis: lax.axis_size(axis) for _, axis in plan}
    shapes = [
        jax.ShapeDtypeStruct(
            array.shape if kind == "a2a" else (sizes[axis],) + array.shape, array.dtype
        )
        for kind, axis, array in steps
    ]
    scratch = [pltpu.SemaphoreType.DMA((len(plan),))]
    for _, axis in plan:
        scratch += [pltpu.SemaphoreType.DMA((sizes[axis] - 1,))] * 2
    return pl.pallas_call(
        functools.partial(exchange_kernel, plan, sizes),
        out_shape=shapes,
        in_specs=[pl.BlockSpec(memory_space=pl.ANY)] * len(plan),
        out_specs=[pl.BlockSpec(memory_space=pl.ANY)] * len(plan),
        scratch_shapes=scratch,
        compiler_params=pltpu.CompilerParams(collective_id=ident, has_side_effects=True),
    )(*arrays)


def product(left, right):
    return jnp.dot(left, right, preferred_element_type=F32)


def left_product(left, right):
    return lax.dot_general(left, right, (((0,), (0,)), ((), ())), preferred_element_type=F32)


def right_product(left, right):
    return lax.dot_general(left, right, (((1,), (1,)), ((), ())), preferred_element_type=F32)


def total(parts):
    return jnp.sum(parts.astype(F32), axis=0)


def root_norm(values, gain):
    return values * lax.rsqrt(jnp.mean(values * values, axis=-1, keepdims=True) + EPSILON) * gain


def convolve(extended, conv_weight, conv_bias):
    count = extended.shape[0] - (CONV - 1)
    summed = conv_bias + conv_weight[0] * extended[0:count]
    for shift in range(1, CONV):
        summed = summed + conv_weight[shift] * extended[shift : shift + count]
    return jax.nn.silu(summed)


def gated_heads(gate_part, conv_input, step_raw, conv_weight, conv_bias, step_bias, decay_rate, skip_gain):
    count, heads = step_raw.shape
    inner = heads * HEAD_M
    extended = jnp.concatenate([jnp.zeros((CONV - 1, conv_input.shape[1]), F32), conv_input], axis=0)
    activated = convolve(extended, conv_weight, conv_bias)
    heads_x = activated[:, :inner].reshape(count, heads, HEAD_M)
    input_map = activated[:, inner : inner + STATE]
    output_map = activated[:, inner + STATE :]
    step_size = jax.nn.softplus(step_raw + step_bias)
    log_decay = jnp.cumsum(step_size * -jnp.exp(decay_rate), axis=0)
    decay_t = log_decay.T
    spread = decay_t[:, :, None] - decay_t[:, None, :]
    causal = jnp.arange(count)[:, None] >= jnp.arange(count)[None, :]
    factor = jnp.exp(jnp.where(causal[None], spread, -jnp.inf))
    scores = jnp.dot(output_map, input_map.T, precision=HIGH)
    weights = factor * scores[None] * step_size.T[:, None, :]
    values = jnp.einsum("hts,shp->thp", weights, heads_x, precision=HIGH)
    values = values + skip_gain[None, :, None] * heads_x
    return values.reshape(count, inner) * jax.nn.silu(gate_part)


def patch_attention(attend_proj):
    count = attend_proj.shape[0]
    patches = count // PATCH
    query = attend_proj[:, :D].reshape(patches, PATCH, HEADS_A, HEAD_A)
    keyed = attend_proj[:, D : 2 * D].reshape(patches, PATCH, HEADS_A, HEAD_A)
    valued = attend_proj[:, 2 * D :].reshape(patches, PATCH, HEADS_A, HEAD_A)
    scores = jnp.einsum("pihd,pjhd->phij", query, keyed, precision=HIGH) * HEAD_A ** (-0.5)
    causal = jnp.arange(PATCH)[:, None] >= jnp.arange(PATCH)[None, :]
    scores = jnp.where(causal, scores, -jnp.inf)
    top = jnp.max(scores, axis=-1, keepdims=True)
    expo = jnp.exp(scores - top)
    probs = expo / jnp.sum(expo, axis=-1, keepdims=True)
    result = jnp.einsum("phij,pjhd->pihd", probs, valued, precision=HIGH)
    return result.reshape(count, D)


def own_columns(array, place, width):
    return lax.dynamic_slice_in_dim(array, place * width, width, axis=-1)


def tucked(row):
    return jnp.pad(row[:, None, :], ((0, 0), (0, 7), (0, -row.shape[1] % LANE)))


def body(
    byte_embeds,
    lengths,
    patch_in,
    mixer_in,
    mixer_out,
    patch_out,
    attend_in,
    attend_out,
    gate_weight,
    up_weight,
    down_weight,
    norm_global,
    conv_weight,
    conv_bias,
    step_bias,
    decay_rate,
    skip_gain,
    norm_gated,
    norm_attend,
    norm_feed,
    cotangent,
):
    n_dp, n_mp = lax.axis_size("dp"), lax.axis_size("mp")
    devices = n_dp * n_mp
    rows = byte_embeds.shape[1]
    patches = rows // PATCH
    count = patches * n_dp
    group = lax.axis_index("mp")
    place = lax.axis_index("dp")
    length = jnp.sum(jnp.where(jnp.arange(lengths.shape[0], dtype=jnp.int32) == group, lengths, 0))
    position = place * rows + jnp.arange(rows, dtype=jnp.int32)
    keep = (position < length).astype(F32)[:, None]
    inputs = byte_embeds[0].astype(F32) * keep

    heads = HEADS_M // n_dp
    inner = heads * HEAD_M
    byte_cols = PATCH * D // n_dp
    k_rows = D // devices
    step_pad = -heads % LANE
    cols = 2 * inner + 2 * STATE + heads + step_pad

    w_attend = lax.all_gather(attend_in, ("dp", "mp"), axis=0, tiled=True).reshape(D, 3 * D)
    w_attend_out = lax.all_gather(attend_out, ("dp", "mp"), axis=0, tiled=True).reshape(D, D)
    w_gate, w_up, w_down = (
        lax.all_gather(gate_weight, "dp", axis=0, tiled=True),
        lax.all_gather(up_weight, "dp", axis=0, tiled=True),
        lax.all_gather(down_weight, "dp", axis=1, tiled=True),
    )
    grad_final = cotangent[0].astype(F32) * keep
    grad_feed_rows = lax.all_gather(grad_final.astype(BF), "mp", axis=0, tiled=True)

    mixer_rows = mixer_in.reshape(k_rows, PROJ)
    shared = mixer_rows[:, 2 * INNER : 2 * INNER + 2 * STATE]
    by_part = jnp.concatenate(
        [
            mixer_rows[:, :INNER].reshape(k_rows, n_dp, inner),
            mixer_rows[:, INNER : 2 * INNER].reshape(k_rows, n_dp, inner),
            jnp.broadcast_to(shared[:, None], (k_rows, n_dp, 2 * STATE)),
            mixer_rows[:, 2 * INNER + 2 * STATE :].reshape(k_rows, n_dp, heads),
            jnp.zeros((k_rows, n_dp, step_pad), BF),
        ],
        axis=2,
    ).transpose(1, 0, 2)
    out_by_part = patch_out.reshape(k_rows, n_dp, byte_cols).transpose(1, 0, 2)
    patch_rows = inputs.astype(BF).reshape(patches, n_dp, byte_cols).transpose(1, 0, 2)
    patch_rows, mixer_cols, out_cols, w_patch_in, w_mixer_out = exchange(
        0,
        ("a2a", "dp", patch_rows),
        ("a2a", "dp", by_part),
        ("a2a", "dp", out_by_part),
        ("ag", "mp", patch_in.reshape(-1, D)),
        ("ag", "mp", mixer_out.reshape(-1, D)),
    )
    patch_rows = patch_rows.reshape(count, byte_cols)
    w_patch_in = w_patch_in.reshape(byte_cols, D)
    w_mixer_out = w_mixer_out.reshape(inner, D)
    parts = product(patch_rows, w_patch_in).astype(BF).reshape(n_dp, patches, D)
    parts, mixer_cols, out_cols = exchange(
        1, ("a2a", "dp", parts), ("ag", "mp", mixer_cols), ("ag", "mp", out_cols)
    )
    w_mixer_in = mixer_cols.transpose(1, 0, 2, 3).reshape(D, cols)
    w_patch_out = out_cols.transpose(1, 0, 2, 3).reshape(D, byte_cols)
    global_in = total(parts)
    (normed,) = exchange(2, ("ag", "dp", root_norm(global_in, norm_global).astype(BF)))
    normed = normed.reshape(count, D)
    projected = product(normed, w_mixer_in)

    def own_conv(array):
        return jnp.concatenate(
            [own_columns(array[..., :INNER], place, inner), array[..., INNER:]], axis=-1
        )

    gated, pull_heads = jax.vjp(
        gated_heads,
        projected[:, :inner],
        projected[:, inner : 2 * inner + 2 * STATE],
        projected[:, 2 * inner + 2 * STATE : 2 * inner + 2 * STATE + heads],
        own_conv(conv_weight),
        own_conv(conv_bias),
        own_columns(step_bias, place, heads),
        own_columns(decay_rate, place, heads),
        own_columns(skip_gain, place, heads),
    )
    own_gain = own_columns(norm_gated, place, inner)
    squares = jnp.sum(gated * gated, axis=1).reshape(n_dp, patches)
    parts = product((gated * own_gain).astype(BF), w_mixer_out).astype(BF)
    parts, squares = exchange(
        3, ("a2a", "dp", parts.reshape(n_dp, patches, D)), ("a2a", "dp", tucked(squares))
    )
    scale = lax.rsqrt(total(squares)[0, :patches] / INNER + EPSILON)
    unscaled = total(parts)
    global_out = global_in + scale[:, None] * unscaled
    global_low, scales = exchange(
        4, ("ag", "dp", global_out.astype(BF)), ("ag", "dp", tucked(scale[None])[0])
    )
    global_low = global_low.reshape(count, D)
    scales = scales[:, 0, :patches].reshape(count, 1)
    slots = product(global_low, w_patch_out).astype(BF)
    (slots,) = exchange(5, ("a2a", "dp", slots.reshape(n_dp, patches, byte_cols)))
    local_in = inputs + slots.astype(F32).transpose(1, 0, 2).reshape(rows, D)

    attend_low = root_norm(local_in, norm_attend).astype(BF)
    attend_proj = product(attend_low, w_attend)
    attended_low = patch_attention(attend_proj).astype(BF)
    after_attend = local_in + product(attended_low, w_attend_out)
    feed_low = root_norm(after_attend, norm_feed).astype(BF)
    feed_rows = lax.all_gather(feed_low, "mp", axis=0, tiled=True)
    gate_value = product(feed_rows, w_gate)
    up_value = product(feed_rows, w_up)
    sigmoid_gate = jax.nn.sigmoid(gate_value)
    silu_gate = gate_value * sigmoid_gate
    hidden_low = (silu_gate * up_value).astype(BF)
    feed_out = lax.psum_scatter(
        product(hidden_low, w_down).astype(BF), "mp", scatter_dimension=0, tiled=True
    ).astype(F32)
    out_bytes = ((after_attend + feed_out) * keep).astype(BF)[None]

    grad_hidden = right_product(grad_feed_rows, w_down)
    grad_down = left_product(hidden_low, grad_feed_rows)
    grad_gate_low = (
        grad_hidden * up_value * sigmoid_gate * (1.0 + gate_value * (1.0 - sigmoid_gate))
    ).astype(BF)
    grad_up_low = (grad_hidden * silu_gate).astype(BF)
    grad_gate = left_product(feed_rows, grad_gate_low)
    grad_up = left_product(feed_rows, grad_up_low)
    grad_feed_normed = lax.psum_scatter(
        (right_product(grad_gate_low, w_gate) + right_product(grad_up_low, w_up)).astype(BF),
        "mp",
        scatter_dimension=0,
        tiled=True,
    ).astype(F32)
    grad_gate, grad_up, grad_down = (
        lax.psum_scatter(grad_gate.astype(BF), "dp", scatter_dimension=0, tiled=True).astype(F32),
        lax.psum_scatter(grad_up.astype(BF), "dp", scatter_dimension=0, tiled=True).astype(F32),
        lax.psum_scatter(grad_down.astype(BF), "dp", scatter_dimension=1, tiled=True).astype(F32),
    )
    _, pull_feed = jax.vjp(root_norm, after_attend, norm_feed)
    grad_after_norm, grad_norm_feed = pull_feed(grad_feed_normed)
    grad_after = grad_final + grad_after_norm
    grad_attend_low = grad_after.astype(BF)
    grad_attend_out = left_product(attended_low, grad_attend_low)
    grad_attended = right_product(grad_attend_low, w_attend_out)
    _, pull_attend = jax.vjp(patch_attention, attend_proj)
    (grad_proj,) = pull_attend(grad_attended)
    grad_proj_low = grad_proj.astype(BF)
    grad_attend_in = left_product(attend_low, grad_proj_low)
    grad_attend_normed = right_product(grad_proj_low, w_attend)
    _, pull_local = jax.vjp(root_norm, local_in, norm_attend)
    grad_local_norm, grad_norm_attend = pull_local(grad_attend_normed)
    grad_local = grad_after + grad_local_norm

    def owners(grad):
        split = grad.reshape(n_dp, n_mp, -1, grad.shape[-1])
        return split.transpose(1, 0, 2, 3).astype(BF)

    grad_slots = grad_local.astype(BF).reshape(patches, n_dp, byte_cols).transpose(1, 0, 2)
    grad_attend = owners(jnp.concatenate([grad_attend_in, grad_attend_out], axis=1))
    grad_slots, grad_attend = exchange(
        6, ("a2a", "dp", grad_slots), ("a2a", "mp", grad_attend)
    )
    grad_slots = grad_slots.reshape(count, byte_cols)
    grad_patch_out = owners(left_product(global_low, grad_slots))
    parts = right_product(grad_slots, w_patch_out).astype(BF).reshape(n_dp, patches, D)
    parts, grad_attend, grad_patch_out = exchange(
        7,
        ("a2a", "dp", parts),
        ("a2a", "dp", total(grad_attend).astype(BF)),
        ("a2a", "mp", grad_patch_out),
    )
    grad_attend = total(grad_attend)
    grad_global_out = total(parts)
    grad_mixer_low = grad_global_out.astype(BF)
    along = jnp.sum(grad_mixer_low.astype(F32) * unscaled, axis=1)
    grad_mixer_low, alongs, grad_patch_out = exchange(
        8,
        ("ag", "dp", grad_mixer_low),
        ("ag", "dp", tucked(along[None])[0]),
        ("a2a", "dp", total(grad_patch_out).astype(BF)),
    )
    grad_patch_out = grad_patch_out.astype(F32).transpose(1, 0, 2).reshape(-1)
    grad_mixer_low = grad_mixer_low.reshape(count, D)
    alongs = alongs[:, 0, :patches].reshape(count, 1)
    grad_mixer_out = left_product((gated * scales * own_gain).astype(BF), grad_mixer_low).astype(BF)
    grad_mixed = right_product(grad_mixer_low, w_mixer_out)
    grad_norm_gated = jnp.sum(grad_mixed * gated * scales, axis=0)
    grad_gated = scales * own_gain * grad_mixed - gated * (scales**3 * alongs / INNER)
    (
        grad_gate_part,
        grad_conv_input,
        grad_step_raw,
        grad_conv_weight,
        grad_conv_bias,
        grad_step_bias,
        grad_decay_rate,
        grad_skip_gain,
    ) = pull_heads(grad_gated)
    grad_projected = jnp.concatenate(
        [
            grad_gate_part,
            grad_conv_input,
            grad_step_raw,
            jnp.zeros((count, step_pad), F32),
        ],
        axis=1,
    ).astype(BF)
    parts = right_product(grad_projected, w_mixer_in).astype(BF).reshape(n_dp, patches, D)
    grad_mixer_in = owners(left_product(normed, grad_projected))
    parts, grad_mixer_out, grad_mixer_in = exchange(
        9,
        ("a2a", "dp", parts),
        ("a2a", "mp", grad_mixer_out.reshape(n_mp, -1, D)),
        ("a2a", "mp", grad_mixer_in),
    )
    grad_mixer_out = total(grad_mixer_out).reshape(-1)
    _, pull_global = jax.vjp(root_norm, global_in, norm_global)
    grad_global_norm, grad_norm_global = pull_global(total(parts))
    grad_global_low = (grad_global_out + grad_global_norm).astype(BF)

    def all_columns(part, whole):
        return lax.dynamic_update_slice_in_dim(
            jnp.zeros(part.shape[:-1] + (whole,), F32), part, place * part.shape[-1], axis=-1
        )

    small = [
        grad_norm_global,
        jnp.concatenate(
            [all_columns(grad_conv_weight[:, :inner], INNER), grad_conv_weight[:, inner:]], axis=1
        ),
        jnp.concatenate([all_columns(grad_conv_bias[:inner], INNER), grad_conv_bias[inner:]]),
        all_columns(grad_step_bias, HEADS_M),
        all_columns(grad_decay_rate, HEADS_M),
        all_columns(grad_skip_gain, HEADS_M),
        all_columns(grad_norm_gated, INNER),
        grad_norm_attend,
        grad_norm_feed,
    ]
    packed = jnp.concatenate([part.reshape(-1) for part in small])
    packed = jnp.pad(packed, (0, -packed.shape[0] % (8 * LANE))).reshape(-1, LANE)
    grad_global_low, packed, grad_mixer_in = exchange(
        10,
        ("ag", "dp", grad_global_low),
        ("ag", "mp", packed),
        ("a2a", "dp", total(grad_mixer_in).astype(BF)),
    )
    grad_global_low = grad_global_low.reshape(count, D)
    grad_patch_rows = right_product(grad_global_low, w_patch_in).astype(BF)
    grad_patch_in = left_product(patch_rows, grad_global_low).astype(BF)
    grad_patch_rows, grad_patch_in, packed = exchange(
        11,
        ("a2a", "dp", grad_patch_rows.reshape(n_dp, patches, byte_cols)),
        ("a2a", "mp", grad_patch_in.reshape(n_mp, -1, D)),
        ("ag", "dp", total(packed)),
    )
    grad_patch_in = total(grad_patch_in).reshape(-1)
    grad_patch_rows = grad_patch_rows.astype(F32).transpose(1, 0, 2).reshape(rows, D)
    grad_bytes = ((grad_local + grad_patch_rows) * keep).astype(BF)[None]
    grad_mixer_in = grad_mixer_in.astype(F32).transpose(1, 0, 2)
    edges = (inner, 2 * inner, 2 * inner + 2 * STATE, 2 * inner + 2 * STATE + heads)
    grad_mixer_in = jnp.concatenate(
        [
            grad_mixer_in[:, :, : edges[0]].reshape(k_rows, INNER),
            grad_mixer_in[:, :, edges[0] : edges[1]].reshape(k_rows, INNER),
            jnp.sum(grad_mixer_in[:, :, edges[1] : edges[2]], axis=1),
            grad_mixer_in[:, :, edges[2] : edges[3]].reshape(k_rows, HEADS_M),
        ],
        axis=1,
    ).reshape(-1)
    packed = total(packed).reshape(-1)
    summed, start = [], 0
    for part in small:
        summed.append(packed[start : start + part.size].reshape(part.shape))
        start += part.size
    return (
        out_bytes,
        grad_bytes,
        grad_patch_in,
        grad_mixer_in,
        grad_mixer_out,
        grad_patch_out,
        grad_attend[:, : 3 * D].reshape(-1),
        grad_attend[:, 3 * D :].reshape(-1),
        grad_gate,
        grad_up,
        grad_down,
        *summed,
    )


def solution(mesh):
    flat = P(("dp", "mp"))
    split = P("mp", "dp", None)
    return jax.shard_map(
        body,
        mesh=mesh,
        in_specs=(split, P())
        + (flat,) * 6
        + (P("dp", "mp"), P("dp", "mp"), P("mp", "dp"))
        + (P(),) * 9
        + (split,),
        out_specs=(split, split)
        + (flat,) * 6
        + (P("dp", "mp"), P("dp", "mp"), P("mp", "dp"))
        + (P(),) * 9,
        check_vma=False,
    )
```

```python
import functools

import jax
import jax.numpy as jnp
from jax import lax
from jax.experimental import pallas as pl
from jax.experimental.pallas import tpu as pltpu
from jax.sharding import PartitionSpec as P

D = 1024
PATCH = 8
INNER = 2048
HEADS_M = 32
STATE = 128
CONV = 4
HEADS_A = 16
HEAD_M = 64
HEAD_A = 64
PROJ = 4384
LANE = 128
VMEM_LIMIT = 60 * 2**20

HIGH = lax.Precision.HIGHEST
EPSILON = 1e-05
BF = jnp.bfloat16
F32 = jnp.float32


MESH = pl.DeviceIdType.MESH


def greet(axes, me, sizes):
    barrier = pltpu.get_barrier_semaphore()
    arrivals = 0
    for axis in axes:
        for k in range(1, sizes[axis]):
            pl.semaphore_signal(
                barrier,
                inc=1,
                device_id={axis: lax.rem(me[axis] + k, sizes[axis])},
                device_id_type=MESH,
            )
        arrivals += sizes[axis] - 1
    pl.semaphore_wait(barrier, arrivals)


def exchange_kernel(plan, sizes, *refs):
    count = len(plan)
    sources, targets = refs[:count], refs[count : 2 * count]
    sems = refs[2 * count :]
    local_sem = sems[0]
    axes = sorted({axis for _, axis in plan})
    me = {axis: lax.axis_index(axis) for axis in axes}
    greet(axes, me, sizes)

    def slot(index, peer):
        kind = plan[index][0]
        if kind == "a2a":
            return sources[index].at[peer]
        if kind == "a2a1":
            return sources[index].at[:, peer]
        return sources[index]

    copies = []
    relays = []
    for index, (kind, axis) in enumerate(plan):
        send, recv = sems[1 + 2 * index], sems[2 + 2 * index]
        here = me[axis]

        def remote(source, target, number, peer):
            copy = pltpu.make_async_remote_copy(
                src_ref=source,
                dst_ref=target,
                send_sem=send.at[number],
                recv_sem=recv.at[number],
                device_id={axis: peer},
                device_id_type=MESH,
            )
            copy.start()
            return copy

        if kind == "agh":
            core = lax.rem(here, 2)
            chips = sizes[axis] // 2
            twin = here + 1 - 2 * core
            for k in range(1, chips):
                peer = lax.rem(here + 2 * k, sizes[axis])
                came = lax.rem(here + sizes[axis] - 2 * k, sizes[axis])
                copy = remote(sources[index], targets[index].at[here], k, peer)
                relays.append((copy, targets[index].at[came], chips - 1 + k, twin, remote))
            copies.append(remote(sources[index], targets[index].at[here], 0, twin))
        else:
            for k in range(1, sizes[axis]):
                peer = lax.rem(here + k, sizes[axis])
                copies.append(remote(slot(index, peer), targets[index].at[here], k - 1, peer))
    own = []
    for index, (kind, axis) in enumerate(plan):
        here = me[axis]
        copy = pltpu.make_async_copy(
            slot(index, here), targets[index].at[here], local_sem.at[index]
        )
        copy.start()
        own.append(copy)
    for copy, block, number, twin, remote in relays:
        copy.wait_recv()
        copies.append(remote(block, block, number, twin))
    for copy in own:
        copy.wait()
    for copy in copies:
        copy.wait()
    for copy, *_ in relays:
        copy.wait_send()


def exchange(ident, *steps):
    plan = tuple((kind, axis) for kind, axis, _ in steps)
    arrays = [array for _, _, array in steps]
    sizes = {axis: lax.axis_size(axis) for _, axis in plan}
    shapes = []
    moved = 0
    for kind, axis, array in steps:
        shape = array.shape
        if kind in ("ag", "agh"):
            shape = (sizes[axis],) + shape
        elif kind == "a2a1":
            shape = (shape[1], shape[0]) + shape[2:]
        shapes.append(jax.ShapeDtypeStruct(shape, array.dtype))
        moved += shapes[-1].size * array.dtype.itemsize
    scratch = [pltpu.SemaphoreType.DMA((len(plan),))]
    for _, axis in plan:
        scratch += [pltpu.SemaphoreType.DMA((sizes[axis] - 1,))] * 2
    return pl.pallas_call(
        functools.partial(exchange_kernel, plan, sizes),
        out_shape=shapes,
        in_specs=[pl.BlockSpec(memory_space=pl.ANY)] * len(plan),
        out_specs=[pl.BlockSpec(memory_space=pl.ANY)] * len(plan),
        scratch_shapes=scratch,
        compiler_params=pltpu.CompilerParams(collective_id=ident, has_side_effects=True),
        cost_estimate=pl.CostEstimate(flops=0, bytes_accessed=64 * moved, transcendentals=0),
    )(*arrays)


def attend_forward_kernel(
    local_ref, gain_ref, feed_gain_ref, w_ref, low_ref, qkv_ref, attended_ref, after_ref, feed_ref
):
    rows = local_ref.shape[0]
    step = min(rows, 256)
    mask = patch_mask(LANE)
    first = lax.broadcasted_iota(jnp.int32, (LANE, LANE), 1) < HEAD_A

    def some(index, _):
        at = pl.ds(pl.multiple_of(index * step, step), step)
        local = local_ref[at, :]
        low = root_norm(local, gain_ref[...]).astype(BF)
        low_ref[at, :] = low
        qkv_ref[at, :] = product(low, w_ref[:, : 3 * D]).astype(BF)

        def heads(inner, _):
            within = pl.ds(pl.multiple_of(index * step + inner * LANE, LANE), LANE)
            for pair in range(D // LANE):
                lanes = slice(pair * LANE, (pair + 1) * LANE)
                query = qkv_ref[within, lanes]
                keyed = qkv_ref[within, D + pair * LANE : D + (pair + 1) * LANE]
                valued = qkv_ref[within, 2 * D + pair * LANE : 2 * D + (pair + 1) * LANE]
                results = []
                for half in (first, ~first):
                    probs = patch_probs(jnp.where(half, query, 0), keyed, mask)
                    results.append(product(probs.astype(BF), valued))
                attended_ref[within, lanes] = jnp.where(first, results[0], results[1]).astype(BF)
            return 0

        lax.fori_loop(0, step // LANE, heads, 0)
        after = local + product(attended_ref[at, :], w_ref[:, 3 * D :])
        after_ref[at, :] = after
        feed_ref[at, :] = root_norm(after, feed_gain_ref[...]).astype(BF)
        return 0

    lax.fori_loop(0, rows // step, some, 0)


def patch_mask(count):
    row = lax.broadcasted_iota(jnp.int32, (count, count), 0)
    column = lax.broadcasted_iota(jnp.int32, (count, count), 1)
    return (row // PATCH == column // PATCH) & (column <= row)


def patch_probs(query, keyed, mask):
    scores = jnp.where(mask, right_product(query, keyed) * HEAD_A ** (-0.5), -1e30)
    expo = jnp.exp(scores - jnp.max(scores, axis=-1, keepdims=True))
    return expo / jnp.sum(expo, axis=-1, keepdims=True)


def attend_forward(local_in, norm_attend, norm_feed, w_attend):
    rows = local_in.shape[0]
    return pl.pallas_call(
        attend_forward_kernel,
        out_shape=[
            jax.ShapeDtypeStruct((rows, D), BF),
            jax.ShapeDtypeStruct((rows, 3 * D), BF),
            jax.ShapeDtypeStruct((rows, D), BF),
            jax.ShapeDtypeStruct((rows, D), F32),
            jax.ShapeDtypeStruct((rows, D), BF),
        ],
        in_specs=[pl.BlockSpec(memory_space=pltpu.VMEM)] * 4,
        out_specs=[pl.BlockSpec(memory_space=pltpu.VMEM)] * 5,
        compiler_params=pltpu.CompilerParams(vmem_limit_bytes=VMEM_LIMIT),
        cost_estimate=pl.CostEstimate(
            flops=2 * rows * D * 4 * D, bytes_accessed=24 * D * D, transcendentals=rows * 16 * LANE
        ),
    )(local_in, norm_attend[None], norm_feed[None], w_attend)


def norm_back(values, gain, grad):
    scale = lax.rsqrt(jnp.mean(values * values, axis=-1, keepdims=True) + EPSILON)
    scaled = grad * gain
    along = jnp.mean(scaled * values, axis=-1, keepdims=True)
    return scale * scaled - values * (scale * scale * scale * along), grad * values * scale


def attend_backward_kernel(
    grad_feed_ref,
    grad_final_ref,
    local_ref,
    after_ref,
    low_ref,
    qkv_ref,
    attended_ref,
    gain_ref,
    feed_gain_ref,
    w_ref,
    grad_local_ref,
    grad_slots_ref,
    grad_w_ref,
    grad_gain_ref,
    grad_feed_gain_ref,
    grads_ref,
):
    rows = local_ref.shape[0]
    step = min(rows, 256)
    mask = patch_mask(LANE)
    first = lax.broadcasted_iota(jnp.int32, (LANE, LANE), 1) < HEAD_A
    grad_gain_ref[...] = jnp.zeros_like(grad_gain_ref)
    grad_feed_gain_ref[...] = jnp.zeros_like(grad_feed_gain_ref)

    def some(index, _):
        at = pl.ds(pl.multiple_of(index * step, step), step)
        grad_after, gains = norm_back(after_ref[at, :], feed_gain_ref[...], grad_feed_ref[at, :])
        grad_feed_gain_ref[...] += jnp.sum(gains, axis=0, keepdims=True)
        grad_after = grad_after + grad_final_ref[at, :].astype(F32)
        grad_low = grad_after.astype(BF)
        grads_ref[at, 3 * D :] = grad_low
        grad_attended = right_product(grad_low, w_ref[:, 3 * D :]).astype(BF)
        grads_ref[at, :D] = grad_attended

        def heads(inner, _):
            within = pl.ds(pl.multiple_of(index * step + inner * LANE, LANE), LANE)
            for pair in range(D // LANE):
                lanes = slice(pair * LANE, (pair + 1) * LANE)
                query = qkv_ref[within, lanes]
                keyed = qkv_ref[within, D + pair * LANE : D + (pair + 1) * LANE]
                valued = qkv_ref[within, 2 * D + pair * LANE : 2 * D + (pair + 1) * LANE]
                grad = grads_ref[within, lanes]
                parts = []
                for half in (first, ~first):
                    probs = patch_probs(jnp.where(half, query, 0), keyed, mask)
                    grad_probs = right_product(jnp.where(half, grad, 0), valued)
                    inside = jnp.sum(grad_probs * probs, axis=-1, keepdims=True)
                    grad_scores = (probs * (grad_probs - inside) * HEAD_A ** (-0.5)).astype(BF)
                    parts.append(
                        (
                            product(grad_scores, keyed),
                            left_product(grad_scores, query),
                            left_product(probs.astype(BF), grad),
                        )
                    )
                for number in range(3):
                    there = slice(number * D + pair * LANE, number * D + (pair + 1) * LANE)
                    grads_ref[within, there] = jnp.where(
                        first, parts[0][number], parts[1][number]
                    ).astype(BF)
            return 0

        lax.fori_loop(0, step // LANE, heads, 0)
        grad_normed = right_product(grads_ref[at, : 3 * D], w_ref[:, : 3 * D])
        grad_local, gains = norm_back(local_ref[at, :], gain_ref[...], grad_normed)
        grad_gain_ref[...] += jnp.sum(gains, axis=0, keepdims=True)
        grad_local = grad_after + grad_local
        grad_local_ref[at, :] = grad_local
        grad_slots_ref[at, :] = grad_local.astype(BF)
        return 0

    lax.fori_loop(0, rows // step, some, 0)

    def columns(index, _):
        at = pl.ds(pl.multiple_of(index * 256, 256), 256)
        grad_w_ref[at, : 3 * D] = left_product(low_ref[:, at], grads_ref[:, : 3 * D]).astype(BF)
        grad_w_ref[at, 3 * D :] = left_product(attended_ref[:, at], grads_ref[:, 3 * D :]).astype(BF)
        return 0

    lax.fori_loop(0, D // 256, columns, 0)


def attend_backward(grad_feed, grad_final, local_in, after, low, qkv, attended, gain, feed_gain, w):
    rows = local_in.shape[0]
    return pl.pallas_call(
        attend_backward_kernel,
        out_shape=[
            jax.ShapeDtypeStruct((rows, D), F32),
            jax.ShapeDtypeStruct((rows, D), BF),
            jax.ShapeDtypeStruct((D, 4 * D), BF),
            jax.ShapeDtypeStruct((1, D), F32),
            jax.ShapeDtypeStruct((1, D), F32),
        ],
        in_specs=[pl.BlockSpec(memory_space=pltpu.VMEM)] * 10,
        out_specs=[pl.BlockSpec(memory_space=pltpu.VMEM)] * 5,
        scratch_shapes=[pltpu.VMEM((rows, 4 * D), BF)],
        compiler_params=pltpu.CompilerParams(vmem_limit_bytes=VMEM_LIMIT),
        cost_estimate=pl.CostEstimate(
            flops=4 * rows * D * 4 * D, bytes_accessed=40 * D * D, transcendentals=rows * 16 * LANE
        ),
    )(grad_feed, grad_final, local_in, after, low, qkv, attended, gain[None], feed_gain[None], w)


def feed_kernel(
    n_mp,
    x_ref,
    c_ref,
    w_ref,
    out_ref,
    grad_feed_ref,
    grads_ref,
    held,
    hidden,
    grad_gate,
    grad_up,
    grad_held,
    paired,
    arrived,
    staged,
    own_sem,
    stage_sems,
    ag_send,
    ag_recv,
    pair_send,
    pair_recv,
    far_send,
    far_recv,
):
    rows = x_ref.shape[0]
    chips = n_mp // 2
    units = w_ref.shape[-1]
    here = lax.axis_index("mp")
    core = lax.rem(here, 2)
    twin = here + 1 - 2 * core
    step = min(rows, 256)
    greet(("mp",), {"mp": here}, {"mp": n_mp})

    def block(owner):
        return pl.ds(pl.multiple_of(owner * rows, rows), rows)

    def remote(source, target, send, recv, peer):
        copy = pltpu.make_async_remote_copy(
            src_ref=source,
            dst_ref=target,
            send_sem=send,
            recv_sem=recv,
            device_id={"mp": peer},
            device_id_type=MESH,
        )
        copy.start()
        return copy

    own = pltpu.make_async_copy(x_ref, held.at[block(here)], own_sem)
    own.start()
    far = [lax.rem(here + 2 * k, n_mp) for k in range(chips)]
    came = [lax.rem(here + n_mp - 2 * k, n_mp) for k in range(chips)]
    direct = [
        remote(x_ref, held.at[block(here)], ag_send.at[k], ag_recv.at[k], far[k])
        for k in range(1, chips)
    ]
    near = remote(x_ref, held.at[block(here)], ag_send.at[0], ag_recv.at[0], twin)

    def weight(number):
        return w_ref[:, number].reshape(D, units)

    stored = []

    def rows_of(owner):
        number = len(stored)
        slot = number % 2
        if number >= 2:
            stored[number - 2].wait()

        def some(index, _):
            local = pl.ds(pl.multiple_of(index * step, step), step)
            at = pl.ds(pl.multiple_of(owner * rows + index * step, step), step)
            x = held[at, :]
            gate = product(x, weight(0))
            up = product(x, weight(1))
            sigmoid = jax.nn.sigmoid(gate)
            silu = gate * sigmoid
            low = (silu * up).astype(BF)
            hidden[at, :] = low
            grad_hidden = product(c_ref[at, :], weight(2))
            gate_low = (grad_hidden * up * sigmoid * (1.0 + gate * (1.0 - sigmoid))).astype(BF)
            up_low = (grad_hidden * silu).astype(BF)
            grad_gate[at, :] = gate_low
            grad_up[at, :] = up_low
            staged[slot, local, :] = right_product(low, weight(2)).astype(BF)
            grad_held[at, :] = (
                right_product(gate_low, weight(0)) + right_product(up_low, weight(1))
            ).astype(BF)
            return 0

        lax.fori_loop(0, rows // step, some, 0)
        copy = pltpu.make_async_copy(
            staged.at[slot], out_ref.at[block(owner)], stage_sems.at[number]
        )
        copy.start()
        stored.append(copy)

    def to_twin(owner, number):
        return remote(
            grad_held.at[block(owner)],
            paired.at[number],
            pair_send.at[number],
            pair_recv.at[number],
            twin,
        )

    own.wait()
    rows_of(here)
    near.wait_recv()
    rows_of(twin)
    pairs = [to_twin(twin, 0)]
    relays = []
    for k in range(1, chips):
        direct[k - 1].wait_recv()
        relays.append(
            remote(
                held.at[block(came[k])],
                held.at[block(came[k])],
                ag_send.at[chips - 1 + k],
                ag_recv.at[chips - 1 + k],
                twin,
            )
        )
        rows_of(came[k])
        relays[-1].wait_recv()
        other = came[k] + 1 - 2 * core
        rows_of(other)
        pairs.append(to_twin(other, k))

    def tiles(start, stop):
        def some(index, _):
            at = pl.ds(pl.multiple_of(index * LANE, LANE), LANE)
            x = held[:, at]
            grads_ref[0, at, :] = left_product(x, grad_gate[...]).astype(BF)
            grads_ref[1, at, :] = left_product(x, grad_up[...]).astype(BF)
            grads_ref[2, at, :] = left_product(c_ref[:, at], hidden[...]).astype(BF)
            return 0

        lax.fori_loop(start, stop, some, 0)

    count = D // LANE
    tiles(0, count // 4)
    sends = []
    for k in range(chips):
        pairs[k].wait_recv()
        at = block(came[k])
        grad_held[at, :] = (grad_held[at, :].astype(F32) + paired[k].astype(F32)).astype(BF)
        if k:
            sends.append(
                remote(
                    grad_held.at[at],
                    arrived.at[k - 1],
                    far_send.at[k - 1],
                    far_recv.at[k - 1],
                    came[k],
                )
            )
    tiles(count // 4, count)
    total_here = grad_held[block(here), :].astype(F32)
    for k in range(1, chips):
        sends[k - 1].wait_recv()
        total_here = total_here + arrived[k - 1].astype(F32)
    grad_feed_ref[...] = total_here
    near.wait_send()
    for copy in direct + relays + pairs + sends:
        copy.wait_send()
    for copy in stored[-2:]:
        copy.wait()


def feed_section(ident, feed_low, grad_rows, weights):
    n_mp = lax.axis_size("mp")
    rows = feed_low.shape[0]
    every = rows * n_mp
    chips = n_mp // 2
    units = weights.shape[-1]
    dma = pltpu.SemaphoreType.DMA
    vmem = pl.BlockSpec(memory_space=pltpu.VMEM)
    return pl.pallas_call(
        functools.partial(feed_kernel, n_mp),
        out_shape=[
            jax.ShapeDtypeStruct((every, D), BF),
            jax.ShapeDtypeStruct((rows, D), F32),
            jax.ShapeDtypeStruct((3, D, units), BF),
        ],
        in_specs=[vmem] * 3,
        out_specs=[pl.BlockSpec(memory_space=pl.ANY), vmem, vmem],
        scratch_shapes=[
            pltpu.VMEM((every, D), BF),
            pltpu.VMEM((every, units), BF),
            pltpu.VMEM((every, units), BF),
            pltpu.VMEM((every, units), BF),
            pltpu.VMEM((every, D), BF),
            pltpu.VMEM((chips, rows, D), BF),
            pltpu.VMEM((chips - 1, rows, D), BF),
            pltpu.VMEM((2, rows, D), BF),
            dma,
            dma((n_mp,)),
            dma((n_mp - 1,)),
            dma((n_mp - 1,)),
            dma((chips,)),
            dma((chips,)),
            dma((chips - 1,)),
            dma((chips - 1,)),
        ],
        compiler_params=pltpu.CompilerParams(
            collective_id=ident, has_side_effects=True, vmem_limit_bytes=VMEM_LIMIT
        ),
        cost_estimate=pl.CostEstimate(
            flops=18 * every * D * units, bytes_accessed=30 * D * D, transcendentals=every * units
        ),
    )(feed_low, grad_rows, weights)


def pair_sum_kernel(n_mp, x_ref, out_ref, mine, paired, local_sems, pair_send, pair_recv, far_send, far_recv, own_sem):
    chips = n_mp // 2
    here = lax.axis_index("mp")
    core = lax.rem(here, 2)
    twin = here + 1 - 2 * core
    greet(("mp",), {"mp": here}, {"mp": n_mp})
    owners = [lax.rem(here + 2 * k, n_mp) for k in range(chips)]
    pairs, loads = [], []
    for k in range(chips):
        copy = pltpu.make_async_remote_copy(
            src_ref=x_ref.at[owners[k] + 1 - 2 * core],
            dst_ref=paired.at[k],
            send_sem=pair_send.at[k],
            recv_sem=pair_recv.at[k],
            device_id={"mp": twin},
            device_id_type=MESH,
        )
        copy.start()
        pairs.append(copy)
        copy = pltpu.make_async_copy(x_ref.at[owners[k]], mine.at[k], local_sems.at[k])
        copy.start()
        loads.append(copy)
    sends = []
    for k in list(range(1, chips)) + [0]:
        loads[k].wait()
        pairs[k].wait_recv()
        mine[k] = (mine[k].astype(F32) + paired[k].astype(F32)).astype(BF)
        if k:
            copy = pltpu.make_async_remote_copy(
                src_ref=mine.at[k],
                dst_ref=out_ref.at[k],
                send_sem=far_send.at[k - 1],
                recv_sem=far_recv.at[k - 1],
                device_id={"mp": owners[k]},
                device_id_type=MESH,
            )
        else:
            copy = pltpu.make_async_copy(mine.at[0], out_ref.at[0], own_sem)
        copy.start()
        sends.append(copy)
    for copy in sends:
        copy.wait()
    for copy in pairs:
        copy.wait_send()


def pair_sum(ident, x):
    n_mp = lax.axis_size("mp")
    chips = n_mp // 2
    dma = pltpu.SemaphoreType.DMA
    hbm = pl.BlockSpec(memory_space=pl.ANY)
    return pl.pallas_call(
        functools.partial(pair_sum_kernel, n_mp),
        out_shape=jax.ShapeDtypeStruct((chips,) + x.shape[1:], BF),
        in_specs=[hbm],
        out_specs=hbm,
        scratch_shapes=[
            pltpu.VMEM((chips,) + x.shape[1:], BF),
            pltpu.VMEM((chips,) + x.shape[1:], BF),
            dma((chips,)),
            dma((chips,)),
            dma((chips,)),
            dma((chips - 1,)),
            dma((chips - 1,)),
            dma,
        ],
        compiler_params=pltpu.CompilerParams(
            collective_id=ident, has_side_effects=True, vmem_limit_bytes=VMEM_LIMIT
        ),
        cost_estimate=pl.CostEstimate(flops=0, bytes_accessed=64 * x.size, transcendentals=0),
    )(x)


def product(left, right):
    return jnp.dot(left, right, preferred_element_type=F32)


def left_product(left, right):
    return lax.dot_general(left, right, (((0,), (0,)), ((), ())), preferred_element_type=F32)


def right_product(left, right):
    return lax.dot_general(left, right, (((1,), (1,)), ((), ())), preferred_element_type=F32)


def total(parts):
    return jnp.sum(parts.astype(F32), axis=0)


def root_norm(values, gain):
    return values * lax.rsqrt(jnp.mean(values * values, axis=-1, keepdims=True) + EPSILON) * gain


def convolve(extended, conv_weight, conv_bias):
    count = extended.shape[0] - (CONV - 1)
    summed = conv_bias + conv_weight[0] * extended[0:count]
    for shift in range(1, CONV):
        summed = summed + conv_weight[shift] * extended[shift : shift + count]
    return jax.nn.silu(summed)


def gated_heads(gate_part, conv_input, step_raw, conv_weight, conv_bias, step_bias, decay_rate, skip_gain):
    count, heads = step_raw.shape
    inner = heads * HEAD_M
    extended = jnp.concatenate([jnp.zeros((CONV - 1, conv_input.shape[1]), F32), conv_input], axis=0)
    activated = convolve(extended, conv_weight, conv_bias)
    heads_x = activated[:, :inner].reshape(count, heads, HEAD_M)
    input_map = activated[:, inner : inner + STATE]
    output_map = activated[:, inner + STATE :]
    step_size = jax.nn.softplus(step_raw + step_bias)
    log_decay = jnp.cumsum(step_size * -jnp.exp(decay_rate), axis=0)
    decay_t = log_decay.T
    spread = decay_t[:, :, None] - decay_t[:, None, :]
    causal = jnp.arange(count)[:, None] >= jnp.arange(count)[None, :]
    factor = jnp.exp(jnp.where(causal[None], spread, -jnp.inf))
    scores = jnp.dot(output_map, input_map.T, precision=HIGH)
    weights = factor * scores[None] * step_size.T[:, None, :]
    values = jnp.einsum("hts,shp->thp", weights, heads_x, precision=HIGH)
    values = values + skip_gain[None, :, None] * heads_x
    return values.reshape(count, inner) * jax.nn.silu(gate_part)


def own_columns(array, place, width):
    return lax.dynamic_slice_in_dim(array, place * width, width, axis=-1)


def tucked(row):
    return jnp.pad(row[:, None, :], ((0, 0), (0, 7), (0, -row.shape[1] % LANE)))


def body(
    byte_embeds,
    lengths,
    patch_in,
    mixer_in,
    mixer_out,
    patch_out,
    attend_in,
    attend_out,
    gate_weight,
    up_weight,
    down_weight,
    norm_global,
    conv_weight,
    conv_bias,
    step_bias,
    decay_rate,
    skip_gain,
    norm_gated,
    norm_attend,
    norm_feed,
    cotangent,
):
    n_dp, n_mp = lax.axis_size("dp"), lax.axis_size("mp")
    devices = n_dp * n_mp
    rows = byte_embeds.shape[1]
    patches = rows // PATCH
    count = patches * n_dp
    group = lax.axis_index("mp")
    place = lax.axis_index("dp")
    length = jnp.sum(jnp.where(jnp.arange(lengths.shape[0], dtype=jnp.int32) == group, lengths, 0))
    position = place * rows + jnp.arange(rows, dtype=jnp.int32)
    keep = (position < length).astype(F32)[:, None]
    inputs = byte_embeds[0].astype(F32) * keep

    heads = HEADS_M // n_dp
    inner = heads * HEAD_M
    byte_cols = PATCH * D // n_dp
    k_rows = D // devices
    step_pad = -heads % LANE
    cols = 2 * inner + 2 * STATE + heads + step_pad

    w_attend = lax.all_gather(
        jnp.concatenate([attend_in.reshape(k_rows, -1), attend_out.reshape(k_rows, -1)], axis=1),
        ("dp", "mp"),
        axis=0,
        tiled=True,
    )
    w_feed = lax.all_gather(jnp.stack([gate_weight, up_weight, down_weight.T]), "dp", axis=0)
    grad_final = (cotangent[0].astype(F32) * keep).astype(BF)

    mixer_rows = mixer_in.reshape(k_rows, PROJ)
    shared = mixer_rows[:, 2 * INNER : 2 * INNER + 2 * STATE]
    by_part = jnp.concatenate(
        [
            mixer_rows[:, :INNER].reshape(k_rows, n_dp, inner),
            mixer_rows[:, INNER : 2 * INNER].reshape(k_rows, n_dp, inner),
            jnp.broadcast_to(shared[:, None], (k_rows, n_dp, 2 * STATE)),
            mixer_rows[:, 2 * INNER + 2 * STATE :].reshape(k_rows, n_dp, heads),
            jnp.zeros((k_rows, n_dp, step_pad), BF),
        ],
        axis=2,
    ).transpose(1, 0, 2)
    out_by_part = patch_out.reshape(k_rows, n_dp, byte_cols).transpose(1, 0, 2)
    patch_rows = inputs.astype(BF).reshape(patches, n_dp, byte_cols).transpose(1, 0, 2)
    patch_rows, mixer_cols, out_cols, w_patch_in, w_mixer_out = exchange(
        0,
        ("a2a", "dp", patch_rows),
        ("a2a", "dp", by_part),
        ("a2a", "dp", out_by_part),
        ("ag", "mp", patch_in.reshape(-1, D)),
        ("ag", "mp", mixer_out.reshape(-1, D)),
    )
    patch_rows = patch_rows.reshape(count, byte_cols)
    w_patch_in = w_patch_in.reshape(byte_cols, D)
    w_mixer_out = w_mixer_out.reshape(inner, D)
    parts = product(patch_rows, w_patch_in).astype(BF).reshape(n_dp, patches, D)
    parts, mixer_cols, out_cols = exchange(
        1, ("a2a", "dp", parts), ("ag", "mp", mixer_cols), ("ag", "mp", out_cols)
    )
    w_mixer_in = mixer_cols.transpose(1, 0, 2, 3).reshape(D, cols)
    w_patch_out = out_cols.transpose(1, 0, 2, 3).reshape(D, byte_cols)
    global_in = total(parts)
    (normed,) = exchange(2, ("ag", "dp", root_norm(global_in, norm_global).astype(BF)))
    normed = normed.reshape(count, D)
    projected = product(normed, w_mixer_in)

    def own_conv(array):
        return jnp.concatenate(
            [own_columns(array[..., :INNER], place, inner), array[..., INNER:]], axis=-1
        )

    gated, pull_heads = jax.vjp(
        gated_heads,
        projected[:, :inner],
        projected[:, inner : 2 * inner + 2 * STATE],
        projected[:, 2 * inner + 2 * STATE : 2 * inner + 2 * STATE + heads],
        own_conv(conv_weight),
        own_conv(conv_bias),
        own_columns(step_bias, place, heads),
        own_columns(decay_rate, place, heads),
        own_columns(skip_gain, place, heads),
    )
    own_gain = own_columns(norm_gated, place, inner)
    squares = jnp.sum(gated * gated, axis=1).reshape(n_dp, patches)
    parts = product((gated * own_gain).astype(BF), w_mixer_out).astype(BF)
    parts, squares, grad_feed_rows = exchange(
        3,
        ("a2a", "dp", parts.reshape(n_dp, patches, D)),
        ("a2a", "dp", tucked(squares)),
        ("agh", "mp", grad_final),
    )
    scale = lax.rsqrt(total(squares)[0, :patches] / INNER + EPSILON)
    unscaled = total(parts)
    global_out = global_in + scale[:, None] * unscaled
    global_low, scales = exchange(
        4, ("ag", "dp", global_out.astype(BF)), ("ag", "dp", tucked(scale[None])[0])
    )
    global_low = global_low.reshape(count, D)
    scales = scales[:, 0, :patches].reshape(count, 1)
    slots = product(global_low, w_patch_out).astype(BF)
    (slots,) = exchange(5, ("a2a", "dp", slots.reshape(n_dp, patches, byte_cols)))
    local_in = inputs + slots.astype(F32).transpose(1, 0, 2).reshape(rows, D)

    attend_low, qkv, attended_low, after_attend, feed_low = attend_forward(
        local_in, norm_attend, norm_feed, w_attend
    )
    feed_parts, grad_feed_normed, grad_feed = feed_section(
        12, feed_low, grad_feed_rows.reshape(-1, D), w_feed
    )
    units = grad_feed.shape[-1]
    grad_feed = grad_feed.reshape(3, n_dp, D // n_dp, units).transpose(1, 0, 2, 3)
    grad_feed = lax.psum_scatter(
        grad_feed.reshape(3 * D, units), "dp", scatter_dimension=0, tiled=True
    ).astype(F32)
    grad_gate, grad_up, grad_down = grad_feed.reshape(3, D // n_dp, units)
    grad_down = grad_down.T
    grad_local, grad_slots, grad_attend, grad_norm_attend, grad_norm_feed = attend_backward(
        grad_feed_normed,
        grad_final,
        local_in,
        after_attend,
        attend_low,
        qkv,
        attended_low,
        norm_attend,
        norm_feed,
        w_attend,
    )
    grad_norm_attend, grad_norm_feed = grad_norm_attend[0], grad_norm_feed[0]
    grad_attend = lax.psum_scatter(
        grad_attend, ("dp", "mp"), scatter_dimension=0, tiled=True
    ).astype(F32)
    feed_out = total(pair_sum(13, feed_parts.reshape(n_mp, rows, D)))
    out_bytes = ((after_attend + feed_out) * keep).astype(BF)[None]

    def owners(grad):
        return grad.astype(BF).reshape(n_dp, n_mp, -1, grad.shape[-1])

    grad_slots = grad_slots.reshape(patches, n_dp, byte_cols).transpose(1, 0, 2)
    (grad_slots,) = exchange(6, ("a2a", "dp", grad_slots))
    grad_slots = grad_slots.reshape(count, byte_cols)
    grad_patch_out = owners(left_product(global_low, grad_slots))
    parts = right_product(grad_slots, w_patch_out).astype(BF).reshape(n_dp, patches, D)
    parts, grad_patch_out = exchange(7, ("a2a", "dp", parts), ("a2a1", "mp", grad_patch_out))
    grad_global_out = total(parts)
    grad_mixer_low = grad_global_out.astype(BF)
    along = jnp.sum(grad_mixer_low.astype(F32) * unscaled, axis=1)
    grad_mixer_low, alongs, grad_patch_out = exchange(
        8,
        ("ag", "dp", grad_mixer_low),
        ("ag", "dp", tucked(along[None])[0]),
        ("a2a", "dp", total(grad_patch_out).astype(BF)),
    )
    grad_patch_out = grad_patch_out.astype(F32).transpose(1, 0, 2).reshape(-1)
    grad_mixer_low = grad_mixer_low.reshape(count, D)
    alongs = alongs[:, 0, :patches].reshape(count, 1)
    grad_mixer_out = left_product((gated * scales * own_gain).astype(BF), grad_mixer_low).astype(BF)
    grad_mixed = right_product(grad_mixer_low, w_mixer_out)
    grad_norm_gated = jnp.sum(grad_mixed * gated * scales, axis=0)
    grad_gated = scales * own_gain * grad_mixed - gated * (scales**3 * alongs / INNER)
    (
        grad_gate_part,
        grad_conv_input,
        grad_step_raw,
        grad_conv_weight,
        grad_conv_bias,
        grad_step_bias,
        grad_decay_rate,
        grad_skip_gain,
    ) = pull_heads(grad_gated)
    grad_projected = jnp.concatenate(
        [
            grad_gate_part,
            grad_conv_input,
            grad_step_raw,
            jnp.zeros((count, step_pad), F32),
        ],
        axis=1,
    ).astype(BF)
    parts = right_product(grad_projected, w_mixer_in).astype(BF).reshape(n_dp, patches, D)
    grad_mixer_in = owners(left_product(normed, grad_projected))
    parts, grad_mixer_out, grad_mixer_in = exchange(
        9,
        ("a2a", "dp", parts),
        ("a2a", "mp", grad_mixer_out.reshape(n_mp, -1, D)),
        ("a2a1", "mp", grad_mixer_in),
    )
    grad_mixer_out = total(grad_mixer_out).reshape(-1)
    _, pull_global = jax.vjp(root_norm, global_in, norm_global)
    grad_global_norm, grad_norm_global = pull_global(total(parts))
    grad_global_low = (grad_global_out + grad_global_norm).astype(BF)

    def all_columns(part, whole):
        return lax.dynamic_update_slice_in_dim(
            jnp.zeros(part.shape[:-1] + (whole,), F32), part, place * part.shape[-1], axis=-1
        )

    small = [
        grad_norm_global,
        jnp.concatenate(
            [all_columns(grad_conv_weight[:, :inner], INNER), grad_conv_weight[:, inner:]], axis=1
        ),
        jnp.concatenate([all_columns(grad_conv_bias[:inner], INNER), grad_conv_bias[inner:]]),
        all_columns(grad_step_bias, HEADS_M),
        all_columns(grad_decay_rate, HEADS_M),
        all_columns(grad_skip_gain, HEADS_M),
        all_columns(grad_norm_gated, INNER),
        grad_norm_attend,
        grad_norm_feed,
    ]
    packed = jnp.concatenate([part.reshape(-1) for part in small])
    packed = jnp.pad(packed, (0, -packed.shape[0] % (8 * LANE))).reshape(-1, LANE)
    grad_global_low, packed, grad_mixer_in = exchange(
        10,
        ("ag", "dp", grad_global_low),
        ("ag", "mp", packed),
        ("a2a", "dp", total(grad_mixer_in).astype(BF)),
    )
    grad_global_low = grad_global_low.reshape(count, D)
    grad_patch_rows = right_product(grad_global_low, w_patch_in).astype(BF)
    grad_patch_in = left_product(patch_rows, grad_global_low).astype(BF)
    grad_patch_rows, grad_patch_in, packed = exchange(
        11,
        ("a2a", "dp", grad_patch_rows.reshape(n_dp, patches, byte_cols)),
        ("a2a", "mp", grad_patch_in.reshape(n_mp, -1, D)),
        ("ag", "dp", total(packed)),
    )
    grad_patch_in = total(grad_patch_in).reshape(-1)
    grad_patch_rows = grad_patch_rows.astype(F32).transpose(1, 0, 2).reshape(rows, D)
    grad_bytes = ((grad_local + grad_patch_rows) * keep).astype(BF)[None]
    grad_mixer_in = grad_mixer_in.astype(F32).transpose(1, 0, 2)
    edges = (inner, 2 * inner, 2 * inner + 2 * STATE, 2 * inner + 2 * STATE + heads)
    grad_mixer_in = jnp.concatenate(
        [
            grad_mixer_in[:, :, : edges[0]].reshape(k_rows, INNER),
            grad_mixer_in[:, :, edges[0] : edges[1]].reshape(k_rows, INNER),
            jnp.sum(grad_mixer_in[:, :, edges[1] : edges[2]], axis=1),
            grad_mixer_in[:, :, edges[2] : edges[3]].reshape(k_rows, HEADS_M),
        ],
        axis=1,
    ).reshape(-1)
    packed = total(packed).reshape(-1)
    summed, start = [], 0
    for part in small:
        summed.append(packed[start : start + part.size].reshape(part.shape))
        start += part.size
    return (
        out_bytes,
        grad_bytes,
        grad_patch_in,
        grad_mixer_in,
        grad_mixer_out,
        grad_patch_out,
        grad_attend[:, : 3 * D].reshape(-1),
        grad_attend[:, 3 * D :].reshape(-1),
        grad_gate,
        grad_up,
        grad_down,
        *summed,
    )


def solution(mesh):
    flat = P(("dp", "mp"))
    split = P("mp", "dp", None)
    return jax.shard_map(
        body,
        mesh=mesh,
        in_specs=(split, P())
        + (flat,) * 6
        + (P("dp", "mp"), P("dp", "mp"), P("mp", "dp"))
        + (P(),) * 9
        + (split,),
        out_specs=(split, split)
        + (flat,) * 6
        + (P("dp", "mp"), P("dp", "mp"), P("mp", "dp"))
        + (P(),) * 9,
        check_vma=False,
    )
```

```python
import functools

import jax
import jax.numpy as jnp
from jax import lax
from jax.experimental import pallas as pl
from jax.experimental.pallas import tpu as pltpu
from jax.sharding import PartitionSpec as P

D = 1024
PATCH = 8
INNER = 2048
HEADS_M = 32
STATE = 128
CONV = 4
HEADS_A = 16
HEAD_M = 64
HEAD_A = 64
PROJ = 4384
LANE = 128
VMEM_LIMIT = 60 * 2**20

HIGH = lax.Precision.HIGHEST
EPSILON = 1e-05
BF = jnp.bfloat16
F32 = jnp.float32


MESH = pl.DeviceIdType.MESH


def greet(axes, me, sizes):
    barrier = pltpu.get_barrier_semaphore()
    arrivals = 0
    for axis in axes:
        for k in range(1, sizes[axis]):
            pl.semaphore_signal(
                barrier,
                inc=1,
                device_id={axis: lax.rem(me[axis] + k, sizes[axis])},
                device_id_type=MESH,
            )
        arrivals += sizes[axis] - 1
    pl.semaphore_wait(barrier, arrivals)


def exchange_kernel(plan, sizes, *refs):
    count = len(plan)
    sources, targets = refs[:count], refs[count : 2 * count]
    scratch = list(refs[2 * count :])
    local_sem = scratch.pop(0)
    axes = sorted({axis for _, axis in plan})
    me = {axis: lax.axis_index(axis) for axis in axes}
    greet(axes, me, sizes)

    def slot(index, peer):
        kind = plan[index][0]
        if kind in ("a2a", "sum"):
            return sources[index].at[peer]
        if kind in ("a2a1", "sum1"):
            return sources[index].at[:, peer]
        return sources[index]

    done, later, sent = [], [], []
    for index, (kind, axis) in enumerate(plan):
        send, recv = scratch.pop(0), scratch.pop(0)
        here, size = me[axis], sizes[axis]
        half = size // 2
        twin = here + 1 - 2 * lax.rem(here, 2)
        target = targets[index]

        def remote(source, target, number, peer, send=send, recv=recv, axis=axis):
            copy = pltpu.make_async_remote_copy(
                src_ref=source,
                dst_ref=target,
                send_sem=send.at[number],
                recv_sem=recv.at[number],
                device_id={axis: peer},
                device_id_type=MESH,
            )
            copy.start()
            return copy

        if kind == "agh":
            for k in range(1, half):
                copy = remote(sources[index], target.at[here], k, lax.rem(here + 2 * k, size))
                sent.append(copy)
                came = lax.rem(here + size - 2 * k, size)

                def relay(copy=copy, block=target.at[came], number=half - 1 + k, twin=twin, remote=remote):
                    copy.wait_recv()
                    done.append(remote(block, block, number, twin))

                later.append(relay)
            done.append(remote(sources[index], target.at[here], 0, twin))
        elif kind in ("sum", "sum1"):
            mine, paired, loads = scratch.pop(0), scratch.pop(0), scratch.pop(0)
            for k in list(range(1, half)) + [0]:
                owner = lax.rem(here + 2 * k, size)
                other = owner + 1 - 2 * lax.rem(here, 2)
                copy = remote(slot(index, other), paired.at[k], k, twin)
                sent.append(copy)
                load = pltpu.make_async_copy(slot(index, owner), mine.at[k], loads.at[k])
                load.start()

                def relay(
                    copy=copy, load=load, mine=mine, paired=paired, k=k, owner=owner, half=half,
                    index=index, target=target, remote=remote,
                ):
                    load.wait()
                    copy.wait_recv()
                    mine[k] = (mine[k].astype(F32) + paired[k].astype(F32)).astype(mine.dtype)
                    if k:
                        done.append(remote(mine.at[k], target.at[k], half - 1 + k, owner))
                    else:
                        own = pltpu.make_async_copy(mine.at[0], target.at[0], local_sem.at[index])
                        own.start()
                        done.append(own)

                later.append(relay)
        else:
            for k in range(1, size):
                peer = lax.rem(here + k, size)
                done.append(remote(slot(index, peer), target.at[here], k - 1, peer))
    for index, (kind, axis) in enumerate(plan):
        if kind not in ("sum", "sum1"):
            here = me[axis]
            copy = pltpu.make_async_copy(
                slot(index, here), targets[index].at[here], local_sem.at[index]
            )
            copy.start()
            done.append(copy)
    for relay in later:
        relay()
    for copy in done:
        copy.wait()
    for copy in sent:
        copy.wait_send()


def exchange(ident, *steps):
    plan = tuple((kind, axis) for kind, axis, _ in steps)
    arrays = [array for _, _, array in steps]
    sizes = {axis: lax.axis_size(axis) for _, axis in plan}
    shapes = []
    scratch = [pltpu.SemaphoreType.DMA((len(plan),))]
    moved = 0
    for kind, axis, array in steps:
        shape = array.shape
        size = sizes[axis]
        sems = size - 1
        if kind in ("ag", "agh"):
            shape = (size,) + shape
        elif kind == "a2a1":
            shape = (size, shape[0]) + shape[2:]
        elif kind == "sum":
            shape = (size // 2,) + shape[1:]
        elif kind == "sum1":
            shape = (size // 2, shape[0]) + shape[2:]
        shapes.append(jax.ShapeDtypeStruct(shape, array.dtype))
        moved += shapes[-1].size * array.dtype.itemsize
        scratch += [pltpu.SemaphoreType.DMA((sems,))] * 2
        if kind in ("sum", "sum1"):
            scratch += [pltpu.VMEM(shape, array.dtype)] * 2 + [pltpu.SemaphoreType.DMA((size // 2,))]
    return pl.pallas_call(
        functools.partial(exchange_kernel, plan, sizes),
        out_shape=shapes,
        in_specs=[pl.BlockSpec(memory_space=pl.ANY)] * len(plan),
        out_specs=[pl.BlockSpec(memory_space=pl.ANY)] * len(plan),
        scratch_shapes=scratch,
        compiler_params=pltpu.CompilerParams(
            collective_id=ident, has_side_effects=True, vmem_limit_bytes=VMEM_LIMIT
        ),
        cost_estimate=pl.CostEstimate(flops=0, bytes_accessed=64 * moved, transcendentals=0),
    )(*arrays)


def attend_forward_kernel(
    local_ref, gain_ref, feed_gain_ref, w_ref, low_ref, qkv_ref, attended_ref, after_ref, feed_ref
):
    rows = local_ref.shape[0]
    step = min(rows, 256)
    mask = patch_mask(LANE)
    first = lax.broadcasted_iota(jnp.int32, (LANE, LANE), 1) < HEAD_A

    def some(index, _):
        at = pl.ds(pl.multiple_of(index * step, step), step)
        local = local_ref[at, :]
        low = root_norm(local, gain_ref[...]).astype(BF)
        low_ref[at, :] = low
        qkv_ref[at, :] = product(low, w_ref[:, : 3 * D]).astype(BF)

        def heads(inner, _):
            within = pl.ds(pl.multiple_of(index * step + inner * LANE, LANE), LANE)
            for pair in range(D // LANE):
                lanes = slice(pair * LANE, (pair + 1) * LANE)
                query = qkv_ref[within, lanes]
                keyed = qkv_ref[within, D + pair * LANE : D + (pair + 1) * LANE]
                valued = qkv_ref[within, 2 * D + pair * LANE : 2 * D + (pair + 1) * LANE]
                results = []
                for half in (first, ~first):
                    probs = patch_probs(jnp.where(half, query, 0), keyed, mask)
                    results.append(product(probs.astype(BF), valued))
                attended_ref[within, lanes] = jnp.where(first, results[0], results[1]).astype(BF)
            return 0

        lax.fori_loop(0, step // LANE, heads, 0)
        after = local + product(attended_ref[at, :], w_ref[:, 3 * D :])
        after_ref[at, :] = after
        feed_ref[at, :] = root_norm(after, feed_gain_ref[...]).astype(BF)
        return 0

    lax.fori_loop(0, rows // step, some, 0)


def patch_mask(count):
    row = lax.broadcasted_iota(jnp.int32, (count, count), 0)
    column = lax.broadcasted_iota(jnp.int32, (count, count), 1)
    return (row // PATCH == column // PATCH) & (column <= row)


def patch_probs(query, keyed, mask):
    scores = jnp.where(mask, right_product(query, keyed) * HEAD_A ** (-0.5), -1e30)
    expo = jnp.exp(scores - jnp.max(scores, axis=-1, keepdims=True))
    return expo / jnp.sum(expo, axis=-1, keepdims=True)


def attend_forward(local_in, norm_attend, norm_feed, w_attend):
    rows = local_in.shape[0]
    return pl.pallas_call(
        attend_forward_kernel,
        out_shape=[
            jax.ShapeDtypeStruct((rows, D), BF),
            jax.ShapeDtypeStruct((rows, 3 * D), BF),
            jax.ShapeDtypeStruct((rows, D), BF),
            jax.ShapeDtypeStruct((rows, D), F32),
            jax.ShapeDtypeStruct((rows, D), BF),
        ],
        in_specs=[pl.BlockSpec(memory_space=pltpu.VMEM)] * 4,
        out_specs=[pl.BlockSpec(memory_space=pltpu.VMEM)] * 5,
        compiler_params=pltpu.CompilerParams(vmem_limit_bytes=VMEM_LIMIT),
        cost_estimate=pl.CostEstimate(
            flops=2 * rows * D * 4 * D, bytes_accessed=24 * D * D, transcendentals=rows * 16 * LANE
        ),
    )(local_in, norm_attend[None], norm_feed[None], w_attend)


def norm_back(values, gain, grad):
    scale = lax.rsqrt(jnp.mean(values * values, axis=-1, keepdims=True) + EPSILON)
    scaled = grad * gain
    along = jnp.mean(scaled * values, axis=-1, keepdims=True)
    return scale * scaled - values * (scale * scale * scale * along), grad * values * scale


def attend_backward_kernel(
    grad_feed_ref,
    grad_final_ref,
    local_ref,
    after_ref,
    low_ref,
    qkv_ref,
    attended_ref,
    gain_ref,
    feed_gain_ref,
    w_ref,
    grad_local_ref,
    grad_slots_ref,
    grad_w_ref,
    grad_gain_ref,
    grad_feed_gain_ref,
    grads_ref,
):
    rows = local_ref.shape[0]
    step = min(rows, 256)
    mask = patch_mask(LANE)
    first = lax.broadcasted_iota(jnp.int32, (LANE, LANE), 1) < HEAD_A
    grad_gain_ref[...] = jnp.zeros_like(grad_gain_ref)
    grad_feed_gain_ref[...] = jnp.zeros_like(grad_feed_gain_ref)

    def some(index, _):
        at = pl.ds(pl.multiple_of(index * step, step), step)
        grad_after, gains = norm_back(after_ref[at, :], feed_gain_ref[...], grad_feed_ref[at, :])
        grad_feed_gain_ref[...] += jnp.sum(gains, axis=0, keepdims=True)
        grad_after = grad_after + grad_final_ref[at, :].astype(F32)
        grad_low = grad_after.astype(BF)
        grads_ref[at, 3 * D :] = grad_low
        grad_attended = right_product(grad_low, w_ref[:, 3 * D :]).astype(BF)
        grads_ref[at, :D] = grad_attended

        def heads(inner, _):
            within = pl.ds(pl.multiple_of(index * step + inner * LANE, LANE), LANE)
            for pair in range(D // LANE):
                lanes = slice(pair * LANE, (pair + 1) * LANE)
                query = qkv_ref[within, lanes]
                keyed = qkv_ref[within, D + pair * LANE : D + (pair + 1) * LANE]
                valued = qkv_ref[within, 2 * D + pair * LANE : 2 * D + (pair + 1) * LANE]
                grad = grads_ref[within, lanes]
                parts = []
                for half in (first, ~first):
                    probs = patch_probs(jnp.where(half, query, 0), keyed, mask)
                    grad_probs = right_product(jnp.where(half, grad, 0), valued)
                    inside = jnp.sum(grad_probs * probs, axis=-1, keepdims=True)
                    grad_scores = (probs * (grad_probs - inside) * HEAD_A ** (-0.5)).astype(BF)
                    parts.append(
                        (
                            product(grad_scores, keyed),
                            left_product(grad_scores, query),
                            left_product(probs.astype(BF), grad),
                        )
                    )
                for number in range(3):
                    there = slice(number * D + pair * LANE, number * D + (pair + 1) * LANE)
                    grads_ref[within, there] = jnp.where(
                        first, parts[0][number], parts[1][number]
                    ).astype(BF)
            return 0

        lax.fori_loop(0, step // LANE, heads, 0)
        grad_normed = right_product(grads_ref[at, : 3 * D], w_ref[:, : 3 * D])
        grad_local, gains = norm_back(local_ref[at, :], gain_ref[...], grad_normed)
        grad_gain_ref[...] += jnp.sum(gains, axis=0, keepdims=True)
        grad_local = grad_after + grad_local
        grad_local_ref[at, :] = grad_local
        grad_slots_ref[at, :] = grad_local.astype(BF)
        return 0

    lax.fori_loop(0, rows // step, some, 0)

    def columns(index, _):
        at = pl.ds(pl.multiple_of(index * 256, 256), 256)
        grad_w_ref[at, : 3 * D] = left_product(low_ref[:, at], grads_ref[:, : 3 * D]).astype(BF)
        grad_w_ref[at, 3 * D :] = left_product(attended_ref[:, at], grads_ref[:, 3 * D :]).astype(BF)
        return 0

    lax.fori_loop(0, D // 256, columns, 0)


def attend_backward(grad_feed, grad_final, local_in, after, low, qkv, attended, gain, feed_gain, w):
    rows = local_in.shape[0]
    return pl.pallas_call(
        attend_backward_kernel,
        out_shape=[
            jax.ShapeDtypeStruct((rows, D), F32),
            jax.ShapeDtypeStruct((rows, D), BF),
            jax.ShapeDtypeStruct((D, 4 * D), BF),
            jax.ShapeDtypeStruct((1, D), F32),
            jax.ShapeDtypeStruct((1, D), F32),
        ],
        in_specs=[pl.BlockSpec(memory_space=pltpu.VMEM)] * 10,
        out_specs=[pl.BlockSpec(memory_space=pltpu.VMEM)] * 5,
        scratch_shapes=[pltpu.VMEM((rows, 4 * D), BF)],
        compiler_params=pltpu.CompilerParams(vmem_limit_bytes=VMEM_LIMIT),
        cost_estimate=pl.CostEstimate(
            flops=4 * rows * D * 4 * D, bytes_accessed=40 * D * D, transcendentals=rows * 16 * LANE
        ),
    )(grad_feed, grad_final, local_in, after, low, qkv, attended, gain[None], feed_gain[None], w)


def feed_kernel(
    n_mp,
    x_ref,
    c_ref,
    w_ref,
    out_ref,
    grad_feed_ref,
    grads_ref,
    held,
    hidden,
    grad_gate,
    grad_up,
    grad_held,
    paired,
    arrived,
    staged,
    own_sem,
    stage_sems,
    ag_send,
    ag_recv,
    pair_send,
    pair_recv,
    far_send,
    far_recv,
):
    rows = x_ref.shape[0]
    chips = n_mp // 2
    units = w_ref.shape[-1]
    here = lax.axis_index("mp")
    core = lax.rem(here, 2)
    twin = here + 1 - 2 * core
    pieces = 2
    size = rows // pieces
    greet(("mp",), {"mp": here}, {"mp": n_mp})

    def block(owner):
        return pl.ds(pl.multiple_of(owner * rows, rows), rows)

    def part(owner, piece):
        return pl.ds(pl.multiple_of(owner * rows + piece * size, size), size)

    def remote(source, target, send, recv, peer):
        copy = pltpu.make_async_remote_copy(
            src_ref=source,
            dst_ref=target,
            send_sem=send,
            recv_sem=recv,
            device_id={"mp": peer},
            device_id_type=MESH,
        )
        copy.start()
        return copy

    own = pltpu.make_async_copy(x_ref, held.at[block(here)], own_sem)
    own.start()
    far = [lax.rem(here + 2 * k, n_mp) for k in range(chips)]
    came = [lax.rem(here + n_mp - 2 * k, n_mp) for k in range(chips)]
    direct = {}
    near = remote(x_ref, held.at[block(here)], ag_send.at[0, 0], ag_recv.at[0, 0], twin)
    for piece in range(pieces):
        for k in range(1, chips):
            direct[k, piece] = remote(
                x_ref.at[part(0, piece)],
                held.at[part(here, piece)],
                ag_send.at[k, piece],
                ag_recv.at[k, piece],
                far[k],
            )

    def weight(number):
        return w_ref[:, number].reshape(D, units)

    stored, relays, pairs, sends = [], {}, {}, {}

    def work(owner, piece):
        number = len(stored)
        slot = number % 2
        if number >= 2:
            stored[number - 2].wait()
        at = part(owner, piece)
        x = held[at, :]
        gate = product(x, weight(0))
        up = product(x, weight(1))
        sigmoid = jax.nn.sigmoid(gate)
        silu = gate * sigmoid
        low = (silu * up).astype(BF)
        hidden[at, :] = low
        grad_hidden = product(c_ref[at, :], weight(2))
        gate_low = (grad_hidden * up * sigmoid * (1.0 + gate * (1.0 - sigmoid))).astype(BF)
        up_low = (grad_hidden * silu).astype(BF)
        grad_gate[at, :] = gate_low
        grad_up[at, :] = up_low
        staged[slot] = right_product(low, weight(2)).astype(BF)
        grad_held[at, :] = (
            right_product(gate_low, weight(0)) + right_product(up_low, weight(1))
        ).astype(BF)
        copy = pltpu.make_async_copy(staged.at[slot], out_ref.at[at], stage_sems.at[number])
        copy.start()
        stored.append(copy)

    def relay(k, piece):
        direct[k, piece].wait_recv()
        at = part(came[k], piece)
        relays[k, piece] = remote(
            held.at[at], held.at[at], ag_send.at[chips - 1 + k, piece], ag_recv.at[chips - 1 + k, piece], twin
        )

    def other(k):
        return came[k] + 1 - 2 * core

    def to_twin(k, piece):
        pairs[k, piece] = remote(
            grad_held.at[part(other(k), piece)],
            paired.at[k, part(0, piece)],
            pair_send.at[k, piece],
            pair_recv.at[k, piece],
            twin,
        )

    def onward(k, piece):
        pairs[k, piece].wait_recv()
        at = part(came[k], piece)
        both = grad_held[at, :].astype(F32) + paired[k, part(0, piece), :].astype(F32)
        grad_held[at, :] = both.astype(BF)
        if k:
            sends[k, piece] = remote(
                grad_held.at[at],
                arrived.at[k - 1, part(0, piece)],
                far_send.at[k - 1, piece],
                far_recv.at[k - 1, piece],
                came[k],
            )

    own.wait()
    for piece in range(pieces):
        work(here, piece)
    near.wait_recv()
    for piece in range(pieces):
        for k in range(1, chips):
            relay(k, piece)
        work(twin, piece)
        to_twin(0, piece)
        for k in range(1, chips):
            if piece:
                onward(k, piece - 1)
            relays[k, piece].wait_recv()
            work(other(k), piece)
            to_twin(k, piece)
            work(came[k], piece)

    def tiles(start, stop):
        def some(index, _):
            at = pl.ds(pl.multiple_of(index * LANE, LANE), LANE)
            x = held[:, at]
            grads_ref[0, at, :] = left_product(x, grad_gate[...]).astype(BF)
            grads_ref[1, at, :] = left_product(x, grad_up[...]).astype(BF)
            grads_ref[2, at, :] = left_product(c_ref[:, at], hidden[...]).astype(BF)
            return 0

        lax.fori_loop(start, stop, some, 0)

    for k in range(1, chips):
        onward(k, pieces - 1)
    count = D // LANE
    tiles(0, count)
    for piece in range(pieces):
        onward(0, piece)
    total_here = grad_held[block(here), :].astype(F32)
    for k in range(1, chips):
        for piece in range(pieces):
            sends[k, piece].wait_recv()
        total_here = total_here + arrived[k - 1].astype(F32)
    grad_feed_ref[...] = total_here
    near.wait_send()
    for group in (direct, relays, pairs, sends):
        for copy in group.values():
            copy.wait_send()
    for copy in stored[-2:]:
        copy.wait()


def feed_section(ident, feed_low, grad_rows, weights):
    n_mp = lax.axis_size("mp")
    rows = feed_low.shape[0]
    every = rows * n_mp
    chips = n_mp // 2
    units = weights.shape[-1]
    dma = pltpu.SemaphoreType.DMA
    vmem = pl.BlockSpec(memory_space=pltpu.VMEM)
    return pl.pallas_call(
        functools.partial(feed_kernel, n_mp),
        out_shape=[
            jax.ShapeDtypeStruct((every, D), BF),
            jax.ShapeDtypeStruct((rows, D), F32),
            jax.ShapeDtypeStruct((3, D, units), BF),
        ],
        in_specs=[vmem] * 3,
        out_specs=[pl.BlockSpec(memory_space=pl.ANY), vmem, vmem],
        scratch_shapes=[
            pltpu.VMEM((every, D), BF),
            pltpu.VMEM((every, units), BF),
            pltpu.VMEM((every, units), BF),
            pltpu.VMEM((every, units), BF),
            pltpu.VMEM((every, D), BF),
            pltpu.VMEM((chips, rows, D), BF),
            pltpu.VMEM((chips - 1, rows, D), BF),
            pltpu.VMEM((2, rows // 2, D), BF),
            dma,
            dma((2 * n_mp,)),
            dma((n_mp - 1, 2)),
            dma((n_mp - 1, 2)),
            dma((chips, 2)),
            dma((chips, 2)),
            dma((chips - 1, 2)),
            dma((chips - 1, 2)),
        ],
        compiler_params=pltpu.CompilerParams(
            collective_id=ident, has_side_effects=True, vmem_limit_bytes=VMEM_LIMIT
        ),
        cost_estimate=pl.CostEstimate(
            flops=18 * every * D * units, bytes_accessed=30 * D * D, transcendentals=every * units
        ),
    )(feed_low, grad_rows, weights)


def product(left, right):
    return jnp.dot(left, right, preferred_element_type=F32)


def left_product(left, right):
    return lax.dot_general(left, right, (((0,), (0,)), ((), ())), preferred_element_type=F32)


def right_product(left, right):
    return lax.dot_general(left, right, (((1,), (1,)), ((), ())), preferred_element_type=F32)


def total(parts):
    return jnp.sum(parts.astype(F32), axis=0)


def root_norm(values, gain):
    return values * lax.rsqrt(jnp.mean(values * values, axis=-1, keepdims=True) + EPSILON) * gain


def shifted(values, steps):
    if steps == 0:
        return values
    row = lax.broadcasted_iota(jnp.int32, values.shape, 0)
    return jnp.where(row >= steps, pltpu.roll(values, steps, 0), 0.0)


def lifted(values, steps):
    if steps == 0:
        return values
    count = values.shape[0]
    row = lax.broadcasted_iota(jnp.int32, values.shape, 0)
    return jnp.where(row < count - steps, pltpu.roll(values, count - steps, 0), 0.0)


def running(values, move):
    steps = 1
    while steps < values.shape[0]:
        values = values + move(values, steps)
        steps *= 2
    return values


def softplus(values):
    return jnp.maximum(values, 0.0) + jnp.log1p(jnp.exp(-jnp.abs(values)))


class Mixer:
    def __init__(self, projected, inner, conv_weight, conv_bias, step_bias, decay_rate):
        self.inner = inner
        self.count = projected.shape[0]
        self.width = min(inner, LANE)
        self.per_group = self.width // HEAD_M
        self.tile = min(self.count, 256)
        edge = 2 * inner + 2 * STATE
        self.conv_input = projected[:, inner:edge]
        self.conv_weight = conv_weight
        summed = conv_bias + conv_weight[CONV - 1 : CONV] * self.conv_input
        for shift in range(1, CONV):
            row = CONV - 1 - shift
            summed = summed + conv_weight[row : row + 1] * shifted(self.conv_input, shift)
        self.sigmoid = jax.nn.sigmoid(summed)
        self.summed = summed
        self.activated = summed * self.sigmoid
        self.raw = projected[:, edge:] + step_bias
        self.step = softplus(self.raw)
        self.rate = jnp.exp(decay_rate)
        self.log_decay = running(self.step * -self.rate, shifted)
        self.log_decay_t = self.log_decay.T
        self.step_t = self.step.T
        low = self.activated.astype(BF)
        self.heads_low = low[:, :inner]
        self.input_low = low[:, inner : inner + STATE]
        self.output_low = low[:, inner + STATE :]
        lane = lax.broadcasted_iota(jnp.int32, (1, self.width), 1)
        self.lanes = [lane // HEAD_M == h for h in range(self.per_group)]

    def tiles(self):
        for start in range(0, self.count, self.tile):
            stop = start + self.tile
            scores = right_product(self.output_low[start:stop], self.input_low[:stop])
            row = lax.broadcasted_iota(jnp.int32, scores.shape, 0) + start
            causal = row >= lax.broadcasted_iota(jnp.int32, scores.shape, 1)
            yield start, stop, scores, causal

    def factor(self, head, start, stop, causal):
        spread = self.log_decay[start:stop, head : head + 1] - self.log_decay_t[head : head + 1, :stop]
        return jnp.exp(jnp.where(causal, spread, -1e30))

    def groups(self):
        return range(self.inner // self.width)

    def merged(self, parts):
        if len(parts) == 1:
            return parts[0]
        return jnp.where(self.lanes[0], parts[0], parts[1])


def mixer_forward_kernel(
    inner, normed_ref, w_ref, w_out_ref, conv_weight_ref, conv_bias_ref, step_bias_ref, decay_ref, skip_ref, gain_ref,
    projected_ref, values_ref, parts_ref, squares_ref,
):
    projected_ref[...] = product(normed_ref[...], w_ref[...])
    mixer = Mixer(
        projected_ref[...], inner, conv_weight_ref[...], conv_bias_ref[...], step_bias_ref[...], decay_ref[...]
    )
    for start, stop, scores, causal in mixer.tiles():
        for group in mixer.groups():
            at = slice(group * mixer.width, (group + 1) * mixer.width)
            parts = []
            for h in range(mixer.per_group):
                head = group * mixer.per_group + h
                weights = (
                    mixer.factor(head, start, stop, causal) * scores * mixer.step_t[head : head + 1, :stop]
                )
                parts.append(product(weights.astype(BF), mixer.heads_low[:stop, at]))
            values_ref[start:stop, at] = (
                mixer.merged(parts) + skip_ref[:, at] * mixer.activated[start:stop, at]
            )
    gate = projected_ref[:, :inner]
    gated = values_ref[...] * (gate * jax.nn.sigmoid(gate))
    squares_ref[...] = lax.dot_general(
        jnp.ones((8, inner), F32),
        gated * gated,
        (((1,), (1,)), ((), ())),
        precision=HIGH,
        preferred_element_type=F32,
    )
    parts_ref[...] = product((gated * gain_ref[...]).astype(BF), w_out_ref[...]).astype(BF)


def mixer_backward_kernel(
    inner,
    grad_ref,
    scales_ref,
    alongs_ref,
    normed_ref,
    projected_ref,
    values_ref,
    w_ref,
    w_out_ref,
    conv_weight_ref,
    conv_bias_ref,
    step_bias_ref,
    decay_ref,
    skip_ref,
    gain_ref,
    parts_ref,
    grad_w_ref,
    grad_w_out_ref,
    grad_conv_weight_ref,
    grad_conv_bias_ref,
    grad_heads_ref,
    grad_skip_ref,
    grad_gain_ref,
    grad_act_ref,
    columns_ref,
    grads_ref,
):
    mixer = Mixer(
        projected_ref[...], inner, conv_weight_ref[...], conv_bias_ref[...], step_bias_ref[...], decay_ref[...]
    )
    count = mixer.count
    edge = 2 * inner + 2 * STATE
    gate = projected_ref[:, :inner]
    sigmoid = jax.nn.sigmoid(gate)
    silu = gate * sigmoid
    values = values_ref[...]
    gated = values * silu
    scales = scales_ref[...]
    grad = grad_ref[...]
    grad_w_out_ref[...] = left_product((gated * scales * gain_ref[...]).astype(BF), grad).astype(BF)
    grad_mixed = right_product(grad, w_out_ref[...])
    grad_gain_ref[...] = jnp.sum(grad_mixed * gated * scales, axis=0, keepdims=True)
    grad_gated = scales * gain_ref[...] * grad_mixed - gated * (scales**3 * alongs_ref[...] / INNER)
    grad_values = grad_gated * silu
    grads_ref[:, :inner] = (grad_gated * values * (sigmoid * (1.0 + gate * (1.0 - sigmoid)))).astype(BF)
    heads_x = mixer.activated[:, :inner]
    grad_skip_ref[...] = jnp.sum(grad_values * heads_x, axis=0, keepdims=True)
    grad_act_ref[:, :inner] = grad_values * skip_ref[...]
    grad_act_ref[:, inner:] = jnp.zeros((count, 2 * STATE), F32)
    columns_ref[...] = jnp.zeros_like(columns_ref)
    grad_low = grad_values.astype(BF)
    lane = lax.broadcasted_iota(jnp.int32, (mixer.tile, LANE), 1)
    grad_decays = []
    for start, stop, scores, causal in mixer.tiles():
        grad_scores = jnp.zeros_like(scores)
        grad_decay = jnp.zeros((mixer.tile, LANE), F32)
        for group in mixer.groups():
            at = slice(group * mixer.width, (group + 1) * mixer.width)
            grad_group = grad_low[start:stop, at]
            parts = []
            for h in range(mixer.per_group):
                head = group * mixer.per_group + h
                row = slice(head, head + 1)
                factor = mixer.factor(head, start, stop, causal)
                step = mixer.step_t[row, :stop]
                unstepped = factor * scores
                grad_weights = right_product(
                    jnp.where(mixer.lanes[h], grad_group, 0), mixer.heads_low[:stop, at]
                )
                parts.append(left_product((unstepped * step).astype(BF), grad_group))
                grad_scores = grad_scores + grad_weights * factor * step
                grad_unstepped = grad_weights * unstepped
                columns_ref[row, :stop] += jnp.sum(grad_unstepped, axis=0, keepdims=True)
                summed = jnp.sum(grad_unstepped * step, axis=1, keepdims=True)
                grad_decay = jnp.where(lane == head, summed, grad_decay)
            grad_act_ref[:stop, at] += mixer.merged(parts)
        grad_decays.append(grad_decay)
        low = grad_scores.astype(BF)
        grad_act_ref[:stop, inner : inner + STATE] += left_product(low, mixer.output_low[start:stop])
        grad_act_ref[start:stop, inner + STATE :] += product(low, mixer.input_low[:stop])
    columns = columns_ref[...].T
    grad_decay = jnp.concatenate(grad_decays, axis=0) - mixer.step * columns
    onward = running(grad_decay, lifted)
    grad_step = columns - onward * mixer.rate
    grad_raw = grad_step * jax.nn.sigmoid(mixer.raw)
    grads_ref[:, edge:] = grad_raw.astype(BF)
    grad_heads_ref[0:1] = jnp.sum(grad_raw, axis=0, keepdims=True)
    grad_heads_ref[1:2] = -jnp.sum(onward * mixer.step, axis=0, keepdims=True) * mixer.rate
    grad_summed = grad_act_ref[...] * (mixer.sigmoid * (1.0 + mixer.summed * (1.0 - mixer.sigmoid)))
    grad_conv_bias_ref[...] = jnp.sum(grad_summed, axis=0, keepdims=True)
    grad_conv = jnp.zeros_like(grad_summed)
    for shift in range(CONV):
        row = slice(CONV - 1 - shift, CONV - shift)
        grad_conv = grad_conv + conv_weight_ref[row] * lifted(grad_summed, shift)
        grad_conv_weight_ref[row] = jnp.sum(
            grad_summed * shifted(mixer.conv_input, shift), axis=0, keepdims=True
        )
    grads_ref[:, inner:edge] = grad_conv.astype(BF)
    parts_ref[...] = right_product(grads_ref[...], w_ref[...]).astype(BF)
    grad_w_ref[...] = left_product(normed_ref[...], grads_ref[...]).astype(BF)


def whole_kernel(kernel, shapes, operands, scratch=(), flops=0):
    vmem = pl.BlockSpec(memory_space=pltpu.VMEM)
    moved = sum(x.size * x.dtype.itemsize for x in list(operands) + list(shapes))
    return pl.pallas_call(
        kernel,
        out_shape=shapes,
        in_specs=[vmem] * len(operands),
        out_specs=[vmem] * len(shapes),
        scratch_shapes=list(scratch),
        compiler_params=pltpu.CompilerParams(vmem_limit_bytes=VMEM_LIMIT),
        cost_estimate=pl.CostEstimate(flops=flops, bytes_accessed=3 * moved, transcendentals=0),
    )(*operands)


def own_columns(array, place, width):
    return lax.dynamic_slice_in_dim(array, place * width, width, axis=-1)


def tucked(row):
    return jnp.pad(row[:, None, :], ((0, 0), (0, 7), (0, -row.shape[1] % LANE)))


def body(
    byte_embeds,
    lengths,
    patch_in,
    mixer_in,
    mixer_out,
    patch_out,
    attend_in,
    attend_out,
    gate_weight,
    up_weight,
    down_weight,
    norm_global,
    conv_weight,
    conv_bias,
    step_bias,
    decay_rate,
    skip_gain,
    norm_gated,
    norm_attend,
    norm_feed,
    cotangent,
):
    n_dp, n_mp = lax.axis_size("dp"), lax.axis_size("mp")
    devices = n_dp * n_mp
    rows = byte_embeds.shape[1]
    patches = rows // PATCH
    count = patches * n_dp
    group = lax.axis_index("mp")
    place = lax.axis_index("dp")
    length = jnp.sum(jnp.where(jnp.arange(lengths.shape[0], dtype=jnp.int32) == group, lengths, 0))
    position = place * rows + jnp.arange(rows, dtype=jnp.int32)
    keep = (position < length).astype(F32)[:, None]
    inputs = byte_embeds[0].astype(F32) * keep

    heads = HEADS_M // n_dp
    inner = heads * HEAD_M
    byte_cols = PATCH * D // n_dp
    k_rows = D // devices
    step_pad = -heads % LANE
    cols = 2 * inner + 2 * STATE + heads + step_pad

    w_attend = lax.all_gather(
        jnp.concatenate([attend_in.reshape(k_rows, -1), attend_out.reshape(k_rows, -1)], axis=1),
        ("dp", "mp"),
        axis=0,
        tiled=True,
    )
    w_feed = lax.all_gather(jnp.stack([gate_weight, up_weight, down_weight.T]), "dp", axis=0)
    grad_final = (cotangent[0].astype(F32) * keep).astype(BF)

    mixer_rows = mixer_in.reshape(k_rows, PROJ)
    shared = mixer_rows[:, 2 * INNER : 2 * INNER + 2 * STATE]
    by_part = jnp.concatenate(
        [
            mixer_rows[:, :INNER].reshape(k_rows, n_dp, inner),
            mixer_rows[:, INNER : 2 * INNER].reshape(k_rows, n_dp, inner),
            jnp.broadcast_to(shared[:, None], (k_rows, n_dp, 2 * STATE)),
            mixer_rows[:, 2 * INNER + 2 * STATE :].reshape(k_rows, n_dp, heads),
            jnp.zeros((k_rows, n_dp, step_pad), BF),
        ],
        axis=2,
    ).transpose(1, 0, 2)
    out_by_part = patch_out.reshape(k_rows, n_dp, byte_cols).transpose(1, 0, 2)
    patch_rows = inputs.astype(BF).reshape(patches, n_dp, byte_cols).transpose(1, 0, 2)
    patch_rows, mixer_cols, w_patch_in = exchange(
        0,
        ("a2a", "dp", patch_rows),
        ("a2a", "dp", by_part),
        ("agh", "mp", patch_in.reshape(-1, D)),
    )
    patch_rows = patch_rows.reshape(count, byte_cols)
    w_patch_in = w_patch_in.reshape(byte_cols, D)
    parts = product(patch_rows, w_patch_in).reshape(n_dp, patches, D)
    parts, mixer_cols = exchange(1, ("sum", "dp", parts), ("agh", "mp", mixer_cols))
    w_mixer_in = mixer_cols.transpose(1, 0, 2, 3).reshape(D, cols)
    global_in = total(parts)
    normed, out_cols, w_mixer_out = exchange(
        2,
        ("agh", "dp", root_norm(global_in, norm_global).astype(BF)),
        ("a2a", "dp", out_by_part),
        ("agh", "mp", mixer_out.reshape(-1, D)),
    )
    w_mixer_out = w_mixer_out.reshape(inner, D)
    normed = normed.reshape(count, D)

    def own_conv(array):
        return jnp.concatenate(
            [own_columns(array[..., :INNER], place, inner), array[..., INNER:]], axis=-1
        )

    def own_heads(array):
        return jnp.pad(own_columns(array, place, heads), (0, step_pad))[None]

    own_gain = own_columns(norm_gated, place, inner)[None]
    mixer_params = (
        own_conv(conv_weight),
        own_conv(conv_bias)[None],
        own_heads(step_bias),
        own_heads(decay_rate),
        jnp.repeat(own_columns(skip_gain, place, heads), HEAD_M)[None],
        own_gain,
    )
    projected, values, parts, squares = whole_kernel(
        functools.partial(mixer_forward_kernel, inner),
        [
            jax.ShapeDtypeStruct((count, cols), F32),
            jax.ShapeDtypeStruct((count, inner), F32),
            jax.ShapeDtypeStruct((count, D), BF),
            jax.ShapeDtypeStruct((8, count), F32),
        ],
        (normed, w_mixer_in, w_mixer_out) + mixer_params,
        flops=2 * count * D * (cols + inner),
    )
    squares = squares[0].reshape(n_dp, patches)
    parts, squares, out_cols = exchange(
        3,
        ("sum", "dp", parts.reshape(n_dp, patches, D)),
        ("a2a", "dp", tucked(squares)),
        ("agh", "mp", out_cols),
    )
    scale = lax.rsqrt(total(squares)[0, :patches] / INNER + EPSILON)
    unscaled = total(parts)
    global_out = global_in + scale[:, None] * unscaled
    w_patch_out = out_cols.transpose(1, 0, 2, 3).reshape(D, byte_cols)
    global_low, scales, grad_feed_rows = exchange(
        4,
        ("agh", "dp", global_out.astype(BF)),
        ("agh", "dp", tucked(scale[None])[0]),
        ("agh", "mp", grad_final),
    )
    global_low = global_low.reshape(count, D)
    scales = scales[:, 0, :patches].reshape(count, 1)
    slots = product(global_low, w_patch_out).astype(BF)
    (slots,) = exchange(5, ("a2a", "dp", slots.reshape(n_dp, patches, byte_cols)))
    local_in = inputs + slots.astype(F32).transpose(1, 0, 2).reshape(rows, D)

    attend_low, qkv, attended_low, after_attend, feed_low = attend_forward(
        local_in, norm_attend, norm_feed, w_attend
    )
    feed_parts, grad_feed_normed, grad_feed = feed_section(
        12, feed_low, grad_feed_rows.reshape(-1, D), w_feed
    )
    units = grad_feed.shape[-1]
    grad_feed = grad_feed.reshape(3, n_dp, D // n_dp, units).transpose(1, 0, 2, 3)
    grad_feed = lax.psum_scatter(
        grad_feed.reshape(3 * D, units), "dp", scatter_dimension=0, tiled=True
    ).astype(F32)
    grad_gate, grad_up, grad_down = grad_feed.reshape(3, D // n_dp, units)
    grad_down = grad_down.T
    grad_local, grad_slots, grad_attend, grad_norm_attend, grad_norm_feed = attend_backward(
        grad_feed_normed,
        grad_final,
        local_in,
        after_attend,
        attend_low,
        qkv,
        attended_low,
        norm_attend,
        norm_feed,
        w_attend,
    )
    grad_norm_attend, grad_norm_feed = grad_norm_attend[0], grad_norm_feed[0]
    grad_attend = lax.psum_scatter(
        grad_attend, ("dp", "mp"), scatter_dimension=0, tiled=True
    ).astype(F32)

    def owners(grad):
        return grad.astype(BF).reshape(n_dp, n_mp, -1, grad.shape[-1])

    grad_slots = grad_slots.reshape(patches, n_dp, byte_cols).transpose(1, 0, 2)
    grad_slots, feed_parts = exchange(
        6, ("a2a", "dp", grad_slots), ("sum", "mp", feed_parts.reshape(n_mp, rows, D))
    )
    out_bytes = ((after_attend + total(feed_parts)) * keep).astype(BF)[None]
    grad_slots = grad_slots.reshape(count, byte_cols)
    grad_patch_out = owners(left_product(global_low, grad_slots))
    parts = right_product(grad_slots, w_patch_out).astype(BF).reshape(n_dp, patches, D)
    parts, grad_patch_out = exchange(7, ("sum", "dp", parts), ("sum1", "mp", grad_patch_out))
    grad_global_out = total(parts)
    grad_mixer_low = grad_global_out.astype(BF)
    along = jnp.sum(grad_mixer_low.astype(F32) * unscaled, axis=1)
    grad_mixer_low, alongs, grad_patch_out = exchange(
        8,
        ("agh", "dp", grad_mixer_low),
        ("agh", "dp", tucked(along[None])[0]),
        ("a2a", "dp", total(grad_patch_out).astype(BF)),
    )
    grad_patch_out = grad_patch_out.astype(F32).transpose(1, 0, 2).reshape(-1)
    grad_mixer_low = grad_mixer_low.reshape(count, D)
    alongs = alongs[:, 0, :patches].reshape(count, 1)
    conv_cols = inner + 2 * STATE
    (
        parts,
        grad_mixer_in,
        grad_mixer_out,
        grad_conv_weight,
        grad_conv_bias,
        grad_heads,
        grad_skip,
        grad_norm_gated,
    ) = whole_kernel(
        functools.partial(mixer_backward_kernel, inner),
        [
            jax.ShapeDtypeStruct((count, D), BF),
            jax.ShapeDtypeStruct((D, cols), BF),
            jax.ShapeDtypeStruct((inner, D), BF),
            jax.ShapeDtypeStruct((CONV, conv_cols), F32),
            jax.ShapeDtypeStruct((1, conv_cols), F32),
            jax.ShapeDtypeStruct((2, heads + step_pad), F32),
            jax.ShapeDtypeStruct((1, inner), F32),
            jax.ShapeDtypeStruct((1, inner), F32),
        ],
        (grad_mixer_low, scales, alongs, normed, projected, values, w_mixer_in, w_mixer_out)
        + mixer_params,
        scratch=(
            pltpu.VMEM((count, conv_cols), F32),
            pltpu.VMEM((LANE, count), F32),
            pltpu.VMEM((count, cols), BF),
        ),
        flops=4 * count * D * (cols + inner),
    )
    grad_conv_bias, grad_norm_gated = grad_conv_bias[0], grad_norm_gated[0]
    grad_step_bias, grad_decay_rate = grad_heads[0, :heads], grad_heads[1, :heads]
    grad_skip_gain = jnp.sum(grad_skip.reshape(heads, HEAD_M), axis=1)
    parts = parts.reshape(n_dp, patches, D)
    grad_mixer_in = owners(grad_mixer_in)
    parts, grad_mixer_out, grad_mixer_in = exchange(
        9,
        ("sum", "dp", parts),
        ("sum", "mp", grad_mixer_out.reshape(n_mp, -1, D)),
        ("sum1", "mp", grad_mixer_in),
    )
    grad_mixer_out = total(grad_mixer_out).reshape(-1)
    _, pull_global = jax.vjp(root_norm, global_in, norm_global)
    grad_global_norm, grad_norm_global = pull_global(total(parts))
    grad_global_low = (grad_global_out + grad_global_norm).astype(BF)

    def all_columns(part, whole):
        return lax.dynamic_update_slice_in_dim(
            jnp.zeros(part.shape[:-1] + (whole,), F32), part, place * part.shape[-1], axis=-1
        )

    small = [
        grad_norm_global,
        jnp.concatenate(
            [all_columns(grad_conv_weight[:, :inner], INNER), grad_conv_weight[:, inner:]], axis=1
        ),
        jnp.concatenate([all_columns(grad_conv_bias[:inner], INNER), grad_conv_bias[inner:]]),
        all_columns(grad_step_bias, HEADS_M),
        all_columns(grad_decay_rate, HEADS_M),
        all_columns(grad_skip_gain, HEADS_M),
        all_columns(grad_norm_gated, INNER),
        grad_norm_attend,
        grad_norm_feed,
    ]
    packed = jnp.concatenate([part.reshape(-1) for part in small])
    packed = jnp.pad(packed, (0, -packed.shape[0] % (8 * LANE))).reshape(-1, LANE)
    grad_global_low, packed, grad_mixer_in = exchange(
        10,
        ("agh", "dp", grad_global_low),
        ("agh", "mp", packed),
        ("a2a", "dp", total(grad_mixer_in).astype(BF)),
    )
    grad_global_low = grad_global_low.reshape(count, D)
    grad_patch_rows = right_product(grad_global_low, w_patch_in).astype(BF)
    grad_patch_in = left_product(patch_rows, grad_global_low).astype(BF)
    grad_patch_rows, grad_patch_in, packed = exchange(
        11,
        ("a2a", "dp", grad_patch_rows.reshape(n_dp, patches, byte_cols)),
        ("sum", "mp", grad_patch_in.reshape(n_mp, -1, D)),
        ("agh", "dp", total(packed)),
    )
    grad_patch_in = total(grad_patch_in).reshape(-1)
    grad_patch_rows = grad_patch_rows.astype(F32).transpose(1, 0, 2).reshape(rows, D)
    grad_bytes = ((grad_local + grad_patch_rows) * keep).astype(BF)[None]
    grad_mixer_in = grad_mixer_in.astype(F32).transpose(1, 0, 2)
    edges = (inner, 2 * inner, 2 * inner + 2 * STATE, 2 * inner + 2 * STATE + heads)
    grad_mixer_in = jnp.concatenate(
        [
            grad_mixer_in[:, :, : edges[0]].reshape(k_rows, INNER),
            grad_mixer_in[:, :, edges[0] : edges[1]].reshape(k_rows, INNER),
            jnp.sum(grad_mixer_in[:, :, edges[1] : edges[2]], axis=1),
            grad_mixer_in[:, :, edges[2] : edges[3]].reshape(k_rows, HEADS_M),
        ],
        axis=1,
    ).reshape(-1)
    packed = total(packed).reshape(-1)
    summed, start = [], 0
    for part in small:
        summed.append(packed[start : start + part.size].reshape(part.shape))
        start += part.size
    return (
        out_bytes,
        grad_bytes,
        grad_patch_in,
        grad_mixer_in,
        grad_mixer_out,
        grad_patch_out,
        grad_attend[:, : 3 * D].reshape(-1),
        grad_attend[:, 3 * D :].reshape(-1),
        grad_gate,
        grad_up,
        grad_down,
        *summed,
    )


def solution(mesh):
    flat = P(("dp", "mp"))
    split = P("mp", "dp", None)
    return jax.shard_map(
        body,
        mesh=mesh,
        in_specs=(split, P())
        + (flat,) * 6
        + (P("dp", "mp"), P("dp", "mp"), P("mp", "dp"))
        + (P(),) * 9
        + (split,),
        out_specs=(split, split)
        + (flat,) * 6
        + (P("dp", "mp"), P("dp", "mp"), P("mp", "dp"))
        + (P(),) * 9,
        check_vma=False,
    )
```

```python
import functools

import jax
import jax.numpy as jnp
from jax import lax
from jax.experimental import pallas as pl
from jax.experimental.pallas import tpu as pltpu
from jax.sharding import PartitionSpec as P

D = 1024
PATCH = 8
INNER = 2048
HEADS_M = 32
STATE = 128
CONV = 4
HEADS_A = 16
HEAD_M = 64
HEAD_A = 64
PROJ = 4384
LANE = 128
VMEM_LIMIT = 60 * 2**20

HIGH = lax.Precision.HIGHEST
EPSILON = 1e-05
BF = jnp.bfloat16
F32 = jnp.float32


MESH = pl.DeviceIdType.MESH


def hail(axes, me, sizes):
    barrier = pltpu.get_barrier_semaphore()
    arrivals = 0
    for axis in axes:
        for k in range(1, sizes[axis]):
            pl.semaphore_signal(
                barrier,
                inc=1,
                device_id={axis: lax.rem(me[axis] + k, sizes[axis])},
                device_id_type=MESH,
            )
        arrivals += sizes[axis] - 1
    return arrivals


def greet(axes, me, sizes):
    pl.semaphore_wait(pltpu.get_barrier_semaphore(), hail(axes, me, sizes))


SUMS = ("sum", "sum1")
SPREADS = ("agh", "agh1")
DMA = pltpu.SemaphoreType.DMA


class Transfer:
    def __init__(self, kind, axis, size, source, target, sems, held=()):
        self.kind, self.axis, self.size = kind, axis, size
        self.source, self.target = source, target
        self.send, self.recv, self.local = sems
        self.here = lax.axis_index(axis)
        self.half = size // 2
        self.twin = self.here + 1 - 2 * lax.rem(self.here, 2)
        self.done, self.later, self.sent = [], [], []
        if kind in SUMS:
            self.mine, self.paired, self.loads = held

    def slot(self, peer):
        if callable(self.source):
            return self.source(peer)
        if self.kind in ("a2a", "sum"):
            return self.source.at[peer]
        if self.kind in ("a2a1", "sum1"):
            return self.source.at[:, peer]
        return self.source

    def block(self, peer):
        return self.target.at[:, peer] if self.kind == "agh1" else self.target.at[peer]

    def remote(self, source, target, number, peer):
        copy = pltpu.make_async_remote_copy(
            src_ref=source,
            dst_ref=target,
            send_sem=self.send.at[number],
            recv_sem=self.recv.at[number],
            device_id={self.axis: peer},
            device_id_type=MESH,
        )
        copy.start()
        return copy

    def start(self, keep_own=True):
        here, size, half, target = self.here, self.size, self.half, self.target
        if self.kind in SPREADS:
            for k in range(1, half):
                copy = self.remote(self.source, self.block(here), k, lax.rem(here + 2 * k, size))
                self.sent.append(copy)
                self.later.append((copy, k))
            self.done.append(self.remote(self.source, self.block(here), 0, self.twin))
        elif self.kind in SUMS:
            for k in list(range(1, half)) + [0]:
                owner = lax.rem(here + 2 * k, size)
                other = owner + 1 - 2 * lax.rem(here, 2)
                copy = self.remote(self.slot(other), self.paired.at[k], k, self.twin)
                self.sent.append(copy)
                load = None
                if self.loads is not None:
                    load = pltpu.make_async_copy(self.slot(owner), self.mine.at[k], self.loads.at[k])
                    load.start()
                self.later.append((copy, k, owner, load))
            return self
        else:
            for k in range(1, size):
                peer = lax.rem(here + k, size)
                self.done.append(self.remote(self.slot(peer), target.at[here], k - 1, peer))
        if keep_own:
            copy = pltpu.make_async_copy(self.slot(here), self.block(here), self.local)
            copy.start()
            self.done.append(copy)
        return self

    def relay(self):
        if self.kind in SPREADS:
            for copy, k in self.later:
                copy.wait_recv()
                block = self.block(lax.rem(self.here + self.size - 2 * k, self.size))
                self.done.append(self.remote(block, block, self.half - 1 + k, self.twin))
        elif self.kind in SUMS:
            for copy, k, owner, load in self.later:
                copy.wait_recv()
                if load is not None:
                    load.wait()
                    own = self.mine[k]
                else:
                    own = self.slot(owner)[...]
                self.mine[k] = (own.astype(F32) + self.paired[k].astype(F32)).astype(self.mine.dtype)
                if k:
                    self.done.append(
                        self.remote(self.mine.at[k], self.target.at[k], self.half - 1 + k, owner)
                    )
                elif load is not None:
                    own = pltpu.make_async_copy(self.mine.at[0], self.target.at[0], self.local)
                    own.start()
                    self.done.append(own)
        self.later = []
        return self

    def finish(self):
        for copy in self.done:
            copy.wait()
        for copy in self.sent:
            copy.wait_send()
        self.done, self.sent = [], []
        return self

    def total(self):
        self.relay()
        self.finish()
        summed = self.mine[0].astype(F32)
        for k in range(1, self.half):
            summed = summed + self.target[k].astype(F32)
        return summed


def transfer_sems(size):
    return [DMA((size - 1,)), DMA((size - 1,)), DMA]


def exchange_kernel(plan, sizes, *refs):
    count = len(plan)
    sources, targets = refs[:count], refs[count : 2 * count]
    scratch = list(refs[2 * count :])
    axes = sorted({axis for _, axis in plan})
    greet(axes, {axis: lax.axis_index(axis) for axis in axes}, sizes)
    moves = []
    for (kind, axis), source, target in zip(plan, sources, targets):
        sems = [scratch.pop(0) for _ in range(3)]
        held = [scratch.pop(0) for _ in range(3)] if kind in SUMS else ()
        moves.append(Transfer(kind, axis, sizes[axis], source, target, sems, held).start())
    order = lambda move: (move.kind not in SUMS, move.axis != "mp")
    for move in sorted(moves, key=order):
        move.relay()
    for move in moves:
        move.finish()


def exchange(ident, *steps):
    plan = tuple((kind, axis) for kind, axis, _ in steps)
    arrays = [array for _, _, array in steps]
    sizes = {axis: lax.axis_size(axis) for _, axis in plan}
    shapes = []
    scratch = []
    moved = 0
    for kind, axis, array in steps:
        shape = array.shape
        size = sizes[axis]
        if kind in ("ag", "agh"):
            shape = (size,) + shape
        elif kind == "agh1":
            shape = (shape[0], size) + shape[1:]
        elif kind == "a2a1":
            shape = (size, shape[0]) + shape[2:]
        elif kind == "sum":
            shape = (size // 2,) + shape[1:]
        elif kind == "sum1":
            shape = (size // 2, shape[0]) + shape[2:]
        shapes.append(jax.ShapeDtypeStruct(shape, array.dtype))
        moved += shapes[-1].size * array.dtype.itemsize
        scratch += transfer_sems(size)
        if kind in SUMS:
            scratch += [pltpu.VMEM(shape, array.dtype)] * 2 + [DMA((size // 2,))]
    return pl.pallas_call(
        functools.partial(exchange_kernel, plan, sizes),
        out_shape=shapes,
        in_specs=[pl.BlockSpec(memory_space=pl.ANY)] * len(plan),
        out_specs=[pl.BlockSpec(memory_space=pl.ANY)] * len(plan),
        scratch_shapes=scratch,
        compiler_params=pltpu.CompilerParams(
            collective_id=ident, has_side_effects=True, vmem_limit_bytes=VMEM_LIMIT
        ),
        cost_estimate=pl.CostEstimate(flops=0, bytes_accessed=64 * moved, transcendentals=0),
    )(*arrays)


def attend_forward_kernel(
    global_ref,
    w_out_ref,
    inputs_ref,
    gain_ref,
    feed_gain_ref,
    w_ref,
    local_ref,
    low_ref,
    qkv_ref,
    attended_ref,
    after_ref,
    feed_ref,
    probs_ref,
    leaving_ref,
    slots_ref,
    chunks_ref,
    *sems,
):
    rows = local_ref.shape[0]
    step = min(rows, 256)
    n_dp, patches, byte_cols = slots_ref.shape
    arrivals = hail(("dp",), {"dp": lax.axis_index("dp")}, {"dp": n_dp})
    leaving_ref[...] = product(global_ref[...], w_out_ref[...]).astype(BF).reshape(slots_ref.shape)
    pl.semaphore_wait(pltpu.get_barrier_semaphore(), arrivals)
    Transfer("a2a", "dp", n_dp, leaving_ref, slots_ref, sems).start().finish()
    for byte in range(PATCH):
        for chunk in range(D // LANE):
            column = byte * D + chunk * LANE
            there = slice(column % byte_cols, column % byte_cols + LANE)
            chunks_ref[chunk, pl.ds(byte, patches, stride=PATCH), :] = slots_ref[
                column // byte_cols, :, there
            ].astype(F32)
    mask = patch_mask(LANE)
    first = lax.broadcasted_iota(jnp.int32, (LANE, LANE), 1) < HEAD_A

    def some(index, _):
        at = pl.ds(pl.multiple_of(index * step, step), step)
        chunks = [chunks_ref[chunk, at, :] for chunk in range(D // LANE)]
        local = inputs_ref[at, :].astype(F32) + jnp.concatenate(chunks, axis=1)
        local_ref[at, :] = local
        low = root_norm(local, gain_ref[...]).astype(BF)
        low_ref[at, :] = low
        qkv_ref[at, :] = product(low, w_ref[:, : 3 * D]).astype(BF)

        def heads(inner, _):
            within = pl.ds(pl.multiple_of(index * step + inner * LANE, LANE), LANE)
            pairs = range(D // LANE)
            scores = []
            for pair in pairs:
                query = qkv_ref[within, pair * LANE : (pair + 1) * LANE]
                keyed = qkv_ref[within, D + pair * LANE : D + (pair + 1) * LANE]
                for half in (first, ~first):
                    scores.append(right_product(jnp.where(half, query, 0), keyed))
            probs = []
            for head, score in enumerate(scores):
                probs.append(patch_probs(score, mask).astype(BF))
                probs_ref[head, within, :] = probs[head]
            for pair in pairs:
                valued = qkv_ref[within, 2 * D + pair * LANE : 2 * D + (pair + 1) * LANE]
                attended_ref[within, pair * LANE : (pair + 1) * LANE] = jnp.where(
                    first, product(probs[2 * pair], valued), product(probs[2 * pair + 1], valued)
                ).astype(BF)
            return 0

        lax.fori_loop(0, step // LANE, heads, 0)
        after = local + product(attended_ref[at, :], w_ref[:, 3 * D :])
        after_ref[at, :] = after
        feed_ref[at, :] = root_norm(after, feed_gain_ref[...]).astype(BF)
        return 0

    lax.fori_loop(0, rows // step, some, 0)


def patch_mask(count):
    row = lax.broadcasted_iota(jnp.int32, (count, count), 0)
    column = lax.broadcasted_iota(jnp.int32, (count, count), 1)
    return (row // PATCH == column // PATCH) & (column <= row)


def patch_probs(scores, mask):
    scores = jnp.where(mask, scores * HEAD_A ** (-0.5), -1e30)
    expo = jnp.exp(scores - jnp.max(scores, axis=-1, keepdims=True))
    return expo / jnp.sum(expo, axis=-1, keepdims=True)


def attend_forward(ident, global_low, w_patch_out, inputs_low, norm_attend, norm_feed, w_attend):
    rows = inputs_low.shape[0]
    n_dp = lax.axis_size("dp")
    slots = (n_dp, rows // PATCH, w_patch_out.shape[1])
    return pl.pallas_call(
        attend_forward_kernel,
        out_shape=[
            jax.ShapeDtypeStruct((rows, D), F32),
            jax.ShapeDtypeStruct((rows, D), BF),
            jax.ShapeDtypeStruct((rows, 3 * D), BF),
            jax.ShapeDtypeStruct((rows, D), BF),
            jax.ShapeDtypeStruct((rows, D), F32),
            jax.ShapeDtypeStruct((rows, D), BF),
            jax.ShapeDtypeStruct((HEADS_A, rows, LANE), BF),
        ],
        in_specs=[pl.BlockSpec(memory_space=pltpu.VMEM)] * 6,
        out_specs=[pl.BlockSpec(memory_space=pltpu.VMEM)] * 7,
        scratch_shapes=[
            pltpu.VMEM(slots, BF),
            pltpu.VMEM(slots, BF),
            pltpu.VMEM((D // LANE, rows, LANE), F32),
        ]
        + transfer_sems(n_dp),
        compiler_params=pltpu.CompilerParams(
            collective_id=ident, has_side_effects=True, vmem_limit_bytes=VMEM_LIMIT
        ),
        cost_estimate=pl.CostEstimate(
            flops=2 * rows * D * 4 * D, bytes_accessed=24 * D * D, transcendentals=rows * 16 * LANE
        ),
    )(global_low, w_patch_out, inputs_low, norm_attend[None], norm_feed[None], w_attend)


def norm_back(values, gain, grad):
    scale = lax.rsqrt(jnp.mean(values * values, axis=-1, keepdims=True) + EPSILON)
    scaled = grad * gain
    along = jnp.mean(scaled * values, axis=-1, keepdims=True)
    return scale * scaled - values * (scale * scale * scale * along), grad * values * scale


def attend_backward_kernel(
    grad_feed_ref,
    grad_final_ref,
    local_ref,
    after_ref,
    low_ref,
    qkv_ref,
    attended_ref,
    probs_ref,
    gain_ref,
    feed_gain_ref,
    w_ref,
    grad_local_ref,
    grad_slots_ref,
    grad_w_ref,
    grad_more_ref,
    grad_gain_ref,
    grad_feed_gain_ref,
    grads_ref,
    chunks_ref,
    slots_ref,
    *sems,
):
    rows = local_ref.shape[0]
    step = min(rows, 256)
    n_dp, _, byte_cols = grad_slots_ref.shape
    arrivals = hail(("dp",), {"dp": lax.axis_index("dp")}, {"dp": n_dp})
    first = lax.broadcasted_iota(jnp.int32, (LANE, LANE), 1) < HEAD_A
    grad_gain_ref[...] = jnp.zeros_like(grad_gain_ref)
    grad_feed_gain_ref[...] = jnp.zeros_like(grad_feed_gain_ref)

    def some(index, _):
        at = pl.ds(pl.multiple_of(index * step, step), step)
        grad_after, gains = norm_back(after_ref[at, :], feed_gain_ref[...], grad_feed_ref[at, :])
        grad_feed_gain_ref[...] += jnp.sum(gains, axis=0, keepdims=True)
        grad_after = grad_after + grad_final_ref[at, :].astype(F32)
        grad_low = grad_after.astype(BF)
        grads_ref[at, 3 * D :] = grad_low
        grad_attended = right_product(grad_low, w_ref[:, 3 * D :]).astype(BF)
        grads_ref[at, :D] = grad_attended

        def heads(inner, _):
            within = pl.ds(pl.multiple_of(index * step + inner * LANE, LANE), LANE)
            pairs = range(D // LANE)

            def part(number, pair):
                return slice(number * D + pair * LANE, number * D + (pair + 1) * LANE)

            given = [grads_ref[within, part(0, pair)] for pair in pairs]
            grad_probs = []
            for pair in pairs:
                for half in (first, ~first):
                    grad_probs.append(
                        right_product(jnp.where(half, given[pair], 0), qkv_ref[within, part(2, pair)])
                    )
            grad_scores = []
            for head, grad in enumerate(grad_probs):
                probs = probs_ref[head, within, :].astype(F32)
                inside = jnp.sum(grad * probs, axis=-1, keepdims=True)
                grad_scores.append((probs * (grad - inside) * HEAD_A ** (-0.5)).astype(BF))
            for pair in pairs:
                query, keyed = qkv_ref[within, part(0, pair)], qkv_ref[within, part(1, pair)]
                two = (2 * pair, 2 * pair + 1)
                results = (
                    [product(grad_scores[head], keyed) for head in two],
                    [left_product(grad_scores[head], query) for head in two],
                    [left_product(probs_ref[head, within, :], given[pair]) for head in two],
                )
                for number in range(3):
                    grads_ref[within, part(number, pair)] = jnp.where(first, *results[number]).astype(BF)
            return 0

        lax.fori_loop(0, step // LANE, heads, 0)
        grad_normed = right_product(grads_ref[at, : 3 * D], w_ref[:, : 3 * D])
        grad_local, gains = norm_back(local_ref[at, :], gain_ref[...], grad_normed)
        grad_gain_ref[...] += jnp.sum(gains, axis=0, keepdims=True)
        grad_local = grad_after + grad_local
        grad_local_ref[at, :] = grad_local
        for chunk in range(D // LANE):
            chunks_ref[chunk, at, :] = grad_local[:, chunk * LANE : (chunk + 1) * LANE]
        return 0

    lax.fori_loop(0, rows // step, some, 0)
    for byte in range(PATCH):
        for chunk in range(D // LANE):
            slots_ref[byte, :, chunk * LANE : (chunk + 1) * LANE] = chunks_ref[
                chunk, pl.ds(byte, rows // PATCH, stride=PATCH), :
            ].astype(BF)
    shares = D // byte_cols

    def slot(peer):
        if shares == 1:
            return slots_ref.at[peer]
        column = pl.multiple_of(lax.rem(peer, shares) * byte_cols, byte_cols)
        return slots_ref.at[peer // shares, :, pl.ds(column, byte_cols)]

    pl.semaphore_wait(pltpu.get_barrier_semaphore(), arrivals)
    move = Transfer("a2a", "dp", n_dp, slot, grad_slots_ref, sems).start()

    n_mp, _, k_rows, _ = grad_w_ref.shape
    each = 256 // (n_mp * k_rows)

    def columns(index, _):
        at = pl.ds(pl.multiple_of(index * 256, 256), 256)
        for source, number, there in (
            (low_ref, 0, slice(0, 2 * D)),
            (low_ref, 2, slice(0, D)),
            (attended_ref, 3, slice(D, 2 * D)),
        ):
            width = there.stop - there.start
            target = grad_w_ref if number == 0 else grad_more_ref
            grad = left_product(source[:, at], grads_ref[:, number * D : number * D + width])
            grad = grad.astype(BF)
            for place in range(each):
                for owner in range(n_mp):
                    start = (place * n_mp + owner) * k_rows
                    target[owner, index * each + place, :, there] = grad[start : start + k_rows]
        return 0

    lax.fori_loop(0, D // 256, columns, 0)
    move.finish()


def attend_backward(ident, grad_feed, grad_final, local_in, after, low, qkv, attended, probs, gain, feed_gain, w):
    rows = local_in.shape[0]
    n_dp, n_mp = lax.axis_size("dp"), lax.axis_size("mp")
    vmem = pl.BlockSpec(memory_space=pltpu.VMEM)
    return pl.pallas_call(
        attend_backward_kernel,
        out_shape=[
            jax.ShapeDtypeStruct((rows, D), F32),
            jax.ShapeDtypeStruct((n_dp, rows // PATCH, PATCH * D // n_dp), BF),
            jax.ShapeDtypeStruct((n_mp, n_dp, D // (n_dp * n_mp), 2 * D), BF),
            jax.ShapeDtypeStruct((n_mp, n_dp, D // (n_dp * n_mp), 2 * D), BF),
            jax.ShapeDtypeStruct((1, D), F32),
            jax.ShapeDtypeStruct((1, D), F32),
        ],
        in_specs=[vmem] * 11,
        out_specs=[vmem, pl.BlockSpec(memory_space=pl.ANY)] + [vmem] * 4,
        scratch_shapes=[
            pltpu.VMEM((rows, 4 * D), BF),
            pltpu.VMEM((D // LANE, rows, LANE), F32),
            pltpu.VMEM((PATCH, rows // PATCH, D), BF),
        ]
        + transfer_sems(n_dp),
        compiler_params=pltpu.CompilerParams(
            collective_id=ident, has_side_effects=True, vmem_limit_bytes=VMEM_LIMIT
        ),
        cost_estimate=pl.CostEstimate(
            flops=4 * rows * D * 4 * D, bytes_accessed=40 * D * D, transcendentals=rows * 16 * LANE
        ),
    )(grad_feed, grad_final, local_in, after, low, qkv, attended, probs, gain[None], feed_gain[None], w)


def feed_kernel(
    n_mp,
    x_ref,
    c_ref,
    w_ref,
    out_ref,
    grad_feed_ref,
    grads_ref,
    held,
    hidden,
    grad_gate,
    grad_up,
    grad_held,
    paired,
    arrived,
    staged,
    own_sem,
    stage_sems,
    ag_send,
    ag_recv,
    pair_send,
    pair_recv,
    far_send,
    far_recv,
):
    rows = x_ref.shape[0]
    chips = n_mp // 2
    units = w_ref.shape[-1]
    here = lax.axis_index("mp")
    core = lax.rem(here, 2)
    twin = here + 1 - 2 * core
    pieces = 2
    size = rows // pieces
    greet(("mp",), {"mp": here}, {"mp": n_mp})

    def block(owner):
        return pl.ds(pl.multiple_of(owner * rows, rows), rows)

    def part(owner, piece):
        return pl.ds(pl.multiple_of(owner * rows + piece * size, size), size)

    def remote(source, target, send, recv, peer):
        copy = pltpu.make_async_remote_copy(
            src_ref=source,
            dst_ref=target,
            send_sem=send,
            recv_sem=recv,
            device_id={"mp": peer},
            device_id_type=MESH,
        )
        copy.start()
        return copy

    own = pltpu.make_async_copy(x_ref, held.at[block(here)], own_sem)
    own.start()
    far = [lax.rem(here + 2 * k, n_mp) for k in range(chips)]
    came = [lax.rem(here + n_mp - 2 * k, n_mp) for k in range(chips)]
    direct = {}
    near = remote(x_ref, held.at[block(here)], ag_send.at[0, 0], ag_recv.at[0, 0], twin)
    for piece in range(pieces):
        for k in range(1, chips):
            direct[k, piece] = remote(
                x_ref.at[part(0, piece)],
                held.at[part(here, piece)],
                ag_send.at[k, piece],
                ag_recv.at[k, piece],
                far[k],
            )

    def weight(number):
        return w_ref[:, number].reshape(D, units)

    stored, relays, pairs, sends = [], {}, {}, {}

    def work(owner, piece):
        number = len(stored)
        slot = number % 2
        if number >= 2:
            stored[number - 2].wait()
        at = part(owner, piece)
        x = held[at, :]
        gate = product(x, weight(0))
        up = product(x, weight(1))
        sigmoid = jax.nn.sigmoid(gate)
        silu = gate * sigmoid
        low = (silu * up).astype(BF)
        hidden[at, :] = low
        grad_hidden = product(c_ref[at, :], weight(2))
        gate_low = (grad_hidden * up * sigmoid * (1.0 + gate * (1.0 - sigmoid))).astype(BF)
        up_low = (grad_hidden * silu).astype(BF)
        grad_gate[at, :] = gate_low
        grad_up[at, :] = up_low
        staged[slot] = right_product(low, weight(2)).astype(BF)
        grad_held[at, :] = (
            right_product(gate_low, weight(0)) + right_product(up_low, weight(1))
        ).astype(BF)
        copy = pltpu.make_async_copy(staged.at[slot], out_ref.at[at], stage_sems.at[number])
        copy.start()
        stored.append(copy)

    def relay(k, piece):
        direct[k, piece].wait_recv()
        at = part(came[k], piece)
        relays[k, piece] = remote(
            held.at[at], held.at[at], ag_send.at[chips - 1 + k, piece], ag_recv.at[chips - 1 + k, piece], twin
        )

    def other(k):
        return came[k] + 1 - 2 * core

    def to_twin(k, piece):
        pairs[k, piece] = remote(
            grad_held.at[part(other(k), piece)],
            paired.at[k, part(0, piece)],
            pair_send.at[k, piece],
            pair_recv.at[k, piece],
            twin,
        )

    def onward(k, piece):
        pairs[k, piece].wait_recv()
        at = part(came[k], piece)
        both = grad_held[at, :].astype(F32) + paired[k, part(0, piece), :].astype(F32)
        grad_held[at, :] = both.astype(BF)
        if k:
            sends[k, piece] = remote(
                grad_held.at[at],
                arrived.at[k - 1, part(0, piece)],
                far_send.at[k - 1, piece],
                far_recv.at[k - 1, piece],
                came[k],
            )

    own.wait()
    for piece in range(pieces):
        work(here, piece)
    near.wait_recv()
    for piece in range(pieces):
        for k in range(1, chips):
            relay(k, piece)
        work(twin, piece)
        to_twin(0, piece)
        for k in range(1, chips):
            if piece:
                onward(k, piece - 1)
            relays[k, piece].wait_recv()
            work(other(k), piece)
            to_twin(k, piece)
            work(came[k], piece)

    def tiles(start, stop):
        def some(index, _):
            at = pl.ds(pl.multiple_of(index * LANE, LANE), LANE)
            x = held[:, at]
            each = grads_ref.shape[2]
            owners = pl.ds(index * (LANE // each), LANE // each)

            def store(number, value):
                grads_ref[owners, number] = value.astype(BF).reshape(LANE // each, each, units)

            store(0, left_product(x, grad_gate[...]))
            store(1, left_product(x, grad_up[...]))
            store(2, left_product(c_ref[:, at], hidden[...]))
            return 0

        lax.fori_loop(start, stop, some, 0)

    for k in range(1, chips):
        onward(k, pieces - 1)
    count = D // LANE
    tiles(0, count)
    for piece in range(pieces):
        onward(0, piece)
    total_here = grad_held[block(here), :].astype(F32)
    for k in range(1, chips):
        for piece in range(pieces):
            sends[k, piece].wait_recv()
        total_here = total_here + arrived[k - 1].astype(F32)
    grad_feed_ref[...] = total_here
    near.wait_send()
    for group in (direct, relays, pairs, sends):
        for copy in group.values():
            copy.wait_send()
    for copy in stored[-2:]:
        copy.wait()


def feed_section(ident, feed_low, grad_rows, weights):
    n_mp = lax.axis_size("mp")
    rows = feed_low.shape[0]
    every = rows * n_mp
    chips = n_mp // 2
    units = weights.shape[-1]
    dma = pltpu.SemaphoreType.DMA
    vmem = pl.BlockSpec(memory_space=pltpu.VMEM)
    return pl.pallas_call(
        functools.partial(feed_kernel, n_mp),
        out_shape=[
            jax.ShapeDtypeStruct((every, D), BF),
            jax.ShapeDtypeStruct((rows, D), F32),
            jax.ShapeDtypeStruct(weights.shape, BF),
        ],
        in_specs=[vmem] * 3,
        out_specs=[pl.BlockSpec(memory_space=pl.ANY), vmem, vmem],
        scratch_shapes=[
            pltpu.VMEM((every, D), BF),
            pltpu.VMEM((every, units), BF),
            pltpu.VMEM((every, units), BF),
            pltpu.VMEM((every, units), BF),
            pltpu.VMEM((every, D), BF),
            pltpu.VMEM((chips, rows, D), BF),
            pltpu.VMEM((chips - 1, rows, D), BF),
            pltpu.VMEM((2, rows // 2, D), BF),
            dma,
            dma((2 * n_mp,)),
            dma((n_mp - 1, 2)),
            dma((n_mp - 1, 2)),
            dma((chips, 2)),
            dma((chips, 2)),
            dma((chips - 1, 2)),
            dma((chips - 1, 2)),
        ],
        compiler_params=pltpu.CompilerParams(
            collective_id=ident, has_side_effects=True, vmem_limit_bytes=VMEM_LIMIT
        ),
        cost_estimate=pl.CostEstimate(
            flops=18 * every * D * units, bytes_accessed=30 * D * D, transcendentals=every * units
        ),
    )(feed_low, grad_rows, weights)


def product(left, right):
    return jnp.dot(left, right, preferred_element_type=F32)


def left_product(left, right):
    return lax.dot_general(left, right, (((0,), (0,)), ((), ())), preferred_element_type=F32)


def right_product(left, right):
    return lax.dot_general(left, right, (((1,), (1,)), ((), ())), preferred_element_type=F32)


def total(parts):
    return jnp.sum(parts.astype(F32), axis=0)


def root_norm(values, gain):
    return values * lax.rsqrt(jnp.mean(values * values, axis=-1, keepdims=True) + EPSILON) * gain


def shifted(values, steps):
    if steps == 0:
        return values
    row = lax.broadcasted_iota(jnp.int32, values.shape, 0)
    return jnp.where(row >= steps, pltpu.roll(values, steps, 0), 0.0)


def lifted(values, steps):
    if steps == 0:
        return values
    count = values.shape[0]
    row = lax.broadcasted_iota(jnp.int32, values.shape, 0)
    return jnp.where(row < count - steps, pltpu.roll(values, count - steps, 0), 0.0)


def running(values, move):
    steps = 1
    while steps < values.shape[0]:
        values = values + move(values, steps)
        steps *= 2
    return values


def softplus(values):
    return jnp.maximum(values, 0.0) + jnp.log1p(jnp.exp(-jnp.abs(values)))


class Mixer:
    def __init__(self, projected, inner, conv_weight, conv_bias, step_bias, decay_rate):
        self.inner = inner
        self.count = projected.shape[0]
        self.width = min(inner, LANE)
        self.per_group = self.width // HEAD_M
        self.tile = min(self.count, 256)
        edge = 2 * inner + 2 * STATE
        self.conv_input = projected[:, inner:edge]
        self.conv_weight = conv_weight
        summed = conv_bias + conv_weight[CONV - 1 : CONV] * self.conv_input
        for shift in range(1, CONV):
            row = CONV - 1 - shift
            summed = summed + conv_weight[row : row + 1] * shifted(self.conv_input, shift)
        self.sigmoid = jax.nn.sigmoid(summed)
        self.summed = summed
        self.activated = summed * self.sigmoid
        self.raw = projected[:, edge:] + step_bias
        self.step = softplus(self.raw)
        self.rate = jnp.exp(decay_rate)
        self.log_decay = running(self.step * -self.rate, shifted)
        self.log_decay_t = self.log_decay.T
        self.step_t = self.step.T
        low = self.activated.astype(BF)
        self.heads_low = low[:, :inner]
        self.input_low = low[:, inner : inner + STATE]
        self.output_low = low[:, inner + STATE :]
        lane = lax.broadcasted_iota(jnp.int32, (1, self.width), 1)
        self.lanes = [lane // HEAD_M == h for h in range(self.per_group)]

    def tiles(self):
        for start in range(0, self.count, self.tile):
            stop = start + self.tile
            scores = right_product(self.output_low[start:stop], self.input_low[:stop])
            row = lax.broadcasted_iota(jnp.int32, scores.shape, 0) + start
            causal = row >= lax.broadcasted_iota(jnp.int32, scores.shape, 1)
            yield start, stop, scores, causal

    def factor(self, head, start, stop, causal):
        spread = self.log_decay[start:stop, head : head + 1] - self.log_decay_t[head : head + 1, :stop]
        return jnp.exp(jnp.where(causal, spread, -1e30))

    def groups(self):
        return range(self.inner // self.width)

    def merged(self, parts):
        if len(parts) == 1:
            return parts[0]
        return jnp.where(self.lanes[0], parts[0], parts[1])


def mixer_forward_kernel(
    inner, normed_ref, w_ref, w_out_ref, conv_weight_ref, conv_bias_ref, step_bias_ref, decay_ref, skip_ref, gain_ref,
    projected_ref, values_ref, parts_ref, squares_ref,
):
    projected_ref[...] = product(normed_ref[...], w_ref[...])
    mixer = Mixer(
        projected_ref[...], inner, conv_weight_ref[...], conv_bias_ref[...], step_bias_ref[...], decay_ref[...]
    )
    for start, stop, scores, causal in mixer.tiles():
        for group in mixer.groups():
            at = slice(group * mixer.width, (group + 1) * mixer.width)
            parts = []
            for h in range(mixer.per_group):
                head = group * mixer.per_group + h
                weights = (
                    mixer.factor(head, start, stop, causal) * scores * mixer.step_t[head : head + 1, :stop]
                )
                parts.append(product(weights.astype(BF), mixer.heads_low[:stop, at]))
            values_ref[start:stop, at] = (
                mixer.merged(parts) + skip_ref[:, at] * mixer.activated[start:stop, at]
            )
    gate = projected_ref[:, :inner]
    gated = values_ref[...] * (gate * jax.nn.sigmoid(gate))
    squares_ref[...] = lax.dot_general(
        jnp.ones((8, inner), F32),
        gated * gated,
        (((1,), (1,)), ((), ())),
        precision=HIGH,
        preferred_element_type=F32,
    )
    parts_ref[...] = product((gated * gain_ref[...]).astype(BF), w_out_ref[...]).astype(BF)


def mixer_backward_kernel(
    inner,
    grad_ref,
    scales_ref,
    alongs_ref,
    normed_ref,
    projected_ref,
    values_ref,
    w_ref,
    w_out_ref,
    conv_weight_ref,
    conv_bias_ref,
    step_bias_ref,
    decay_ref,
    skip_ref,
    gain_ref,
    parts_ref,
    grad_w_ref,
    grad_w_out_ref,
    grad_conv_weight_ref,
    grad_conv_bias_ref,
    grad_heads_ref,
    grad_skip_ref,
    grad_gain_ref,
    grad_act_ref,
    columns_ref,
    grads_ref,
):
    mixer = Mixer(
        projected_ref[...], inner, conv_weight_ref[...], conv_bias_ref[...], step_bias_ref[...], decay_ref[...]
    )
    count = mixer.count
    edge = 2 * inner + 2 * STATE
    gate = projected_ref[:, :inner]
    sigmoid = jax.nn.sigmoid(gate)
    silu = gate * sigmoid
    values = values_ref[...]
    gated = values * silu
    scales = scales_ref[...]
    grad = grad_ref[...]
    grad_w_out_ref[...] = left_product((gated * scales * gain_ref[...]).astype(BF), grad).astype(BF)
    grad_mixed = right_product(grad, w_out_ref[...])
    grad_gain_ref[...] = jnp.sum(grad_mixed * gated * scales, axis=0, keepdims=True)
    grad_gated = scales * gain_ref[...] * grad_mixed - gated * (scales**3 * alongs_ref[...] / INNER)
    grad_values = grad_gated * silu
    grads_ref[:, :inner] = (grad_gated * values * (sigmoid * (1.0 + gate * (1.0 - sigmoid)))).astype(BF)
    heads_x = mixer.activated[:, :inner]
    grad_skip_ref[...] = jnp.sum(grad_values * heads_x, axis=0, keepdims=True)
    grad_act_ref[:, :inner] = grad_values * skip_ref[...]
    grad_act_ref[:, inner:] = jnp.zeros((count, 2 * STATE), F32)
    columns_ref[...] = jnp.zeros_like(columns_ref)
    grad_low = grad_values.astype(BF)
    lane = lax.broadcasted_iota(jnp.int32, (mixer.tile, LANE), 1)
    grad_decays = []
    for start, stop, scores, causal in mixer.tiles():
        grad_scores = jnp.zeros_like(scores)
        grad_decay = jnp.zeros((mixer.tile, LANE), F32)
        for group in mixer.groups():
            at = slice(group * mixer.width, (group + 1) * mixer.width)
            grad_group = grad_low[start:stop, at]
            parts = []
            for h in range(mixer.per_group):
                head = group * mixer.per_group + h
                row = slice(head, head + 1)
                factor = mixer.factor(head, start, stop, causal)
                step = mixer.step_t[row, :stop]
                unstepped = factor * scores
                grad_weights = right_product(
                    jnp.where(mixer.lanes[h], grad_group, 0), mixer.heads_low[:stop, at]
                )
                parts.append(left_product((unstepped * step).astype(BF), grad_group))
                grad_scores = grad_scores + grad_weights * factor * step
                grad_unstepped = grad_weights * unstepped
                columns_ref[row, :stop] += jnp.sum(grad_unstepped, axis=0, keepdims=True)
                summed = jnp.sum(grad_unstepped * step, axis=1, keepdims=True)
                grad_decay = jnp.where(lane == head, summed, grad_decay)
            grad_act_ref[:stop, at] += mixer.merged(parts)
        grad_decays.append(grad_decay)
        low = grad_scores.astype(BF)
        grad_act_ref[:stop, inner : inner + STATE] += left_product(low, mixer.output_low[start:stop])
        grad_act_ref[start:stop, inner + STATE :] += product(low, mixer.input_low[:stop])
    columns = columns_ref[...].T
    grad_decay = jnp.concatenate(grad_decays, axis=0) - mixer.step * columns
    onward = running(grad_decay, lifted)
    grad_step = columns - onward * mixer.rate
    grad_raw = grad_step * jax.nn.sigmoid(mixer.raw)
    grads_ref[:, edge:] = grad_raw.astype(BF)
    grad_heads_ref[0:1] = jnp.sum(grad_raw, axis=0, keepdims=True)
    grad_heads_ref[1:2] = -jnp.sum(onward * mixer.step, axis=0, keepdims=True) * mixer.rate
    grad_summed = grad_act_ref[...] * (mixer.sigmoid * (1.0 + mixer.summed * (1.0 - mixer.sigmoid)))
    grad_conv_bias_ref[...] = jnp.sum(grad_summed, axis=0, keepdims=True)
    grad_conv = jnp.zeros_like(grad_summed)
    for shift in range(CONV):
        row = slice(CONV - 1 - shift, CONV - shift)
        grad_conv = grad_conv + conv_weight_ref[row] * lifted(grad_summed, shift)
        grad_conv_weight_ref[row] = jnp.sum(
            grad_summed * shifted(mixer.conv_input, shift), axis=0, keepdims=True
        )
    grads_ref[:, inner:edge] = grad_conv.astype(BF)
    parts_ref[...] = right_product(grads_ref[...], w_ref[...]).astype(BF)
    grad_w_ref[...] = left_product(normed_ref[...], grads_ref[...]).astype(BF)


def whole_kernel(kernel, shapes, operands, scratch=(), flops=0):
    vmem = pl.BlockSpec(memory_space=pltpu.VMEM)
    moved = sum(x.size * x.dtype.itemsize for x in list(operands) + list(shapes))
    return pl.pallas_call(
        kernel,
        out_shape=shapes,
        in_specs=[vmem] * len(operands),
        out_specs=[vmem] * len(shapes),
        scratch_shapes=list(scratch),
        compiler_params=pltpu.CompilerParams(vmem_limit_bytes=VMEM_LIMIT),
        cost_estimate=pl.CostEstimate(flops=flops, bytes_accessed=3 * moved, transcendentals=0),
    )(*operands)


def own_columns(array, place, width):
    return lax.dynamic_slice_in_dim(array, place * width, width, axis=-1)


def tucked(row):
    return jnp.pad(row[:, None, :], ((0, 0), (0, 7), (0, -row.shape[1] % LANE)))


def body(
    byte_embeds,
    lengths,
    patch_in,
    mixer_in,
    mixer_out,
    patch_out,
    attend_in,
    attend_out,
    gate_weight,
    up_weight,
    down_weight,
    norm_global,
    conv_weight,
    conv_bias,
    step_bias,
    decay_rate,
    skip_gain,
    norm_gated,
    norm_attend,
    norm_feed,
    cotangent,
):
    n_dp, n_mp = lax.axis_size("dp"), lax.axis_size("mp")
    devices = n_dp * n_mp
    rows = byte_embeds.shape[1]
    patches = rows // PATCH
    count = patches * n_dp
    group = lax.axis_index("mp")
    place = lax.axis_index("dp")
    length = jnp.sum(jnp.where(jnp.arange(lengths.shape[0], dtype=jnp.int32) == group, lengths, 0))
    position = place * rows + jnp.arange(rows, dtype=jnp.int32)
    keep = (position < length).astype(F32)[:, None]
    inputs = byte_embeds[0].astype(F32) * keep

    heads = HEADS_M // n_dp
    inner = heads * HEAD_M
    byte_cols = PATCH * D // n_dp
    k_rows = D // devices
    step_pad = -heads % LANE
    cols = 2 * inner + 2 * STATE + heads + step_pad

    w_attend = lax.all_gather(
        jnp.concatenate([attend_in.reshape(k_rows, -1), attend_out.reshape(k_rows, -1)], axis=1),
        ("dp", "mp"),
        axis=0,
        tiled=True,
    )
    w_feed = lax.all_gather(jnp.stack([gate_weight, up_weight, down_weight.T]), "dp", axis=0)
    grad_final = (cotangent[0].astype(F32) * keep).astype(BF)

    mixer_rows = mixer_in.reshape(k_rows, PROJ)
    shared = mixer_rows[:, 2 * INNER : 2 * INNER + 2 * STATE]
    by_part = jnp.concatenate(
        [
            mixer_rows[:, :INNER].reshape(k_rows, n_dp, inner),
            mixer_rows[:, INNER : 2 * INNER].reshape(k_rows, n_dp, inner),
            jnp.broadcast_to(shared[:, None], (k_rows, n_dp, 2 * STATE)),
            mixer_rows[:, 2 * INNER + 2 * STATE :].reshape(k_rows, n_dp, heads),
            jnp.zeros((k_rows, n_dp, step_pad), BF),
        ],
        axis=2,
    ).transpose(1, 0, 2)
    out_by_part = patch_out.reshape(k_rows, n_dp, byte_cols).transpose(1, 0, 2)
    patch_rows = inputs.astype(BF).reshape(patches, n_dp, byte_cols).transpose(1, 0, 2)
    patch_rows, mixer_cols, w_patch_in, grad_feed_rows = exchange(
        0,
        ("a2a", "dp", patch_rows),
        ("a2a", "dp", by_part),
        ("agh", "mp", patch_in.reshape(-1, D)),
        ("agh", "mp", grad_final),
    )
    patch_rows = patch_rows.reshape(count, byte_cols)
    w_patch_in = w_patch_in.reshape(byte_cols, D)
    parts = product(patch_rows, w_patch_in).reshape(n_dp, patches, D)
    parts, mixer_cols = exchange(1, ("sum", "dp", parts), ("agh1", "mp", mixer_cols))
    w_mixer_in = mixer_cols.reshape(D, cols)
    global_in = total(parts)
    normed, out_cols, w_mixer_out = exchange(
        2,
        ("agh", "dp", root_norm(global_in, norm_global).astype(BF)),
        ("a2a", "dp", out_by_part),
        ("agh", "mp", mixer_out.reshape(-1, D)),
    )
    w_mixer_out = w_mixer_out.reshape(inner, D)
    normed = normed.reshape(count, D)

    def own_conv(array):
        return jnp.concatenate(
            [own_columns(array[..., :INNER], place, inner), array[..., INNER:]], axis=-1
        )

    def own_heads(array):
        return jnp.pad(own_columns(array, place, heads), (0, step_pad))[None]

    own_gain = own_columns(norm_gated, place, inner)[None]
    mixer_params = (
        own_conv(conv_weight),
        own_conv(conv_bias)[None],
        own_heads(step_bias),
        own_heads(decay_rate),
        jnp.repeat(own_columns(skip_gain, place, heads), HEAD_M)[None],
        own_gain,
    )
    projected, values, parts, squares = whole_kernel(
        functools.partial(mixer_forward_kernel, inner),
        [
            jax.ShapeDtypeStruct((count, cols), F32),
            jax.ShapeDtypeStruct((count, inner), F32),
            jax.ShapeDtypeStruct((count, D), BF),
            jax.ShapeDtypeStruct((8, count), F32),
        ],
        (normed, w_mixer_in, w_mixer_out) + mixer_params,
        flops=2 * count * D * (cols + inner),
    )
    squares = squares[0].reshape(n_dp, patches)
    parts, squares, out_cols = exchange(
        3,
        ("sum", "dp", parts.reshape(n_dp, patches, D)),
        ("a2a", "dp", tucked(squares)),
        ("agh1", "mp", out_cols),
    )
    scale = lax.rsqrt(total(squares)[0, :patches] / INNER + EPSILON)
    unscaled = total(parts)
    global_out = global_in + scale[:, None] * unscaled
    w_patch_out = out_cols.reshape(D, byte_cols)
    global_low, scales = exchange(
        4,
        ("agh", "dp", global_out.astype(BF)),
        ("agh", "dp", tucked(scale[None])[0]),
    )
    global_low = global_low.reshape(count, D)
    scales = scales[:, 0, :patches].reshape(count, 1)
    local_in, attend_low, qkv, attended_low, after_attend, feed_low, probs = attend_forward(
        5, global_low, w_patch_out, inputs.astype(BF), norm_attend, norm_feed, w_attend
    )
    feed_parts, grad_feed_normed, grad_feed = feed_section(
        12, feed_low, grad_feed_rows.reshape(-1, D), w_feed
    )
    units = grad_feed.shape[-1]
    grad_feed = lax.psum_scatter(
        grad_feed.reshape(3 * D, units), "dp", scatter_dimension=0, tiled=True
    ).astype(F32)
    grad_gate, grad_up, grad_down = grad_feed.reshape(3, D // n_dp, units)
    grad_down = grad_down.T
    grad_local, grad_slots, grad_attend, grad_more, grad_norm_attend, grad_norm_feed = attend_backward(
        6,
        grad_feed_normed,
        grad_final,
        local_in,
        after_attend,
        attend_low,
        qkv,
        attended_low,
        probs,
        norm_attend,
        norm_feed,
        w_attend,
    )
    grad_norm_attend, grad_norm_feed = grad_norm_attend[0], grad_norm_feed[0]

    def owners(grad):
        return grad.astype(BF).reshape(n_dp, n_mp, -1, grad.shape[-1])

    grad_slots = grad_slots.reshape(count, byte_cols)
    grad_patch_out = owners(left_product(global_low, grad_slots))
    parts = right_product(grad_slots, w_patch_out).astype(BF).reshape(n_dp, patches, D)
    parts, grad_patch_out, grad_attend = exchange(
        7, ("sum", "dp", parts), ("sum1", "mp", grad_patch_out), ("sum", "mp", grad_attend)
    )
    grad_global_out = total(parts)
    grad_mixer_low = grad_global_out.astype(BF)
    along = jnp.sum(grad_mixer_low.astype(F32) * unscaled, axis=1)
    grad_mixer_low, alongs, grad_patch_out, grad_more = exchange(
        8,
        ("agh", "dp", grad_mixer_low),
        ("agh", "dp", tucked(along[None])[0]),
        ("a2a", "dp", total(grad_patch_out).astype(BF)),
        ("sum", "mp", grad_more),
    )
    grad_mixer_low = grad_mixer_low.reshape(count, D)
    alongs = alongs[:, 0, :patches].reshape(count, 1)
    conv_cols = inner + 2 * STATE
    (
        parts,
        grad_mixer_in,
        grad_mixer_out,
        grad_conv_weight,
        grad_conv_bias,
        grad_heads,
        grad_skip,
        grad_norm_gated,
    ) = whole_kernel(
        functools.partial(mixer_backward_kernel, inner),
        [
            jax.ShapeDtypeStruct((count, D), BF),
            jax.ShapeDtypeStruct((D, cols), BF),
            jax.ShapeDtypeStruct((inner, D), BF),
            jax.ShapeDtypeStruct((CONV, conv_cols), F32),
            jax.ShapeDtypeStruct((1, conv_cols), F32),
            jax.ShapeDtypeStruct((2, heads + step_pad), F32),
            jax.ShapeDtypeStruct((1, inner), F32),
            jax.ShapeDtypeStruct((1, inner), F32),
        ],
        (grad_mixer_low, scales, alongs, normed, projected, values, w_mixer_in, w_mixer_out)
        + mixer_params,
        scratch=(
            pltpu.VMEM((count, conv_cols), F32),
            pltpu.VMEM((LANE, count), F32),
            pltpu.VMEM((count, cols), BF),
        ),
        flops=4 * count * D * (cols + inner),
    )
    grad_conv_bias, grad_norm_gated = grad_conv_bias[0], grad_norm_gated[0]
    grad_step_bias, grad_decay_rate = grad_heads[0, :heads], grad_heads[1, :heads]
    grad_skip_gain = jnp.sum(grad_skip.reshape(heads, HEAD_M), axis=1)
    parts = parts.reshape(n_dp, patches, D)
    grad_mixer_in = owners(grad_mixer_in)
    parts, grad_mixer_out, grad_mixer_in, feed_parts, grad_attend = exchange(
        9,
        ("sum", "dp", parts),
        ("sum", "mp", grad_mixer_out.reshape(n_mp, -1, D)),
        ("sum1", "mp", grad_mixer_in),
        ("sum", "mp", feed_parts.reshape(n_mp, rows, D)),
        ("sum", "dp", total(grad_attend).astype(BF)),
    )
    grad_mixer_out = total(grad_mixer_out).reshape(-1)
    _, pull_global = jax.vjp(root_norm, global_in, norm_global)
    grad_global_norm, grad_norm_global = pull_global(total(parts))
    grad_global_low = (grad_global_out + grad_global_norm).astype(BF)

    def all_columns(part, whole):
        return lax.dynamic_update_slice_in_dim(
            jnp.zeros(part.shape[:-1] + (whole,), F32), part, place * part.shape[-1], axis=-1
        )

    small = [
        grad_norm_global,
        jnp.concatenate(
            [all_columns(grad_conv_weight[:, :inner], INNER), grad_conv_weight[:, inner:]], axis=1
        ),
        jnp.concatenate([all_columns(grad_conv_bias[:inner], INNER), grad_conv_bias[inner:]]),
        all_columns(grad_step_bias, HEADS_M),
        all_columns(grad_decay_rate, HEADS_M),
        all_columns(grad_skip_gain, HEADS_M),
        all_columns(grad_norm_gated, INNER),
        grad_norm_attend,
        grad_norm_feed,
    ]
    packed = jnp.concatenate([part.reshape(-1) for part in small])
    packed = jnp.pad(packed, (0, -packed.shape[0] % (8 * LANE))).reshape(-1, LANE)
    grad_global_low, packed, grad_mixer_in, grad_more = exchange(
        10,
        ("agh", "dp", grad_global_low),
        ("agh", "mp", packed),
        ("a2a", "dp", total(grad_mixer_in).astype(BF)),
        ("sum", "dp", total(grad_more).astype(BF)),
    )
    grad_attend, grad_more = total(grad_attend), total(grad_more)
    grad_global_low = grad_global_low.reshape(count, D)
    grad_patch_rows = right_product(grad_global_low, w_patch_in).astype(BF)
    grad_patch_in = left_product(patch_rows, grad_global_low).astype(BF)
    grad_patch_rows, grad_patch_in, packed = exchange(
        11,
        ("a2a", "dp", grad_patch_rows.reshape(n_dp, patches, byte_cols)),
        ("sum", "mp", grad_patch_in.reshape(n_mp, -1, D)),
        ("agh", "dp", total(packed)),
    )
    grad_patch_in = total(grad_patch_in).reshape(-1)
    grad_patch_rows = grad_patch_rows.astype(F32).transpose(1, 0, 2).reshape(rows, D)
    grad_bytes = ((grad_local + grad_patch_rows) * keep).astype(BF)[None]
    out_bytes = ((after_attend + total(feed_parts)) * keep).astype(BF)[None]
    grad_patch_out = grad_patch_out.astype(F32).transpose(1, 0, 2).reshape(-1)
    grad_mixer_in = grad_mixer_in.astype(F32).transpose(1, 0, 2)
    edges = (inner, 2 * inner, 2 * inner + 2 * STATE, 2 * inner + 2 * STATE + heads)
    grad_mixer_in = jnp.concatenate(
        [
            grad_mixer_in[:, :, : edges[0]].reshape(k_rows, INNER),
            grad_mixer_in[:, :, edges[0] : edges[1]].reshape(k_rows, INNER),
            jnp.sum(grad_mixer_in[:, :, edges[1] : edges[2]], axis=1),
            grad_mixer_in[:, :, edges[2] : edges[3]].reshape(k_rows, HEADS_M),
        ],
        axis=1,
    ).reshape(-1)
    packed = total(packed).reshape(-1)
    summed, start = [], 0
    for part in small:
        summed.append(packed[start : start + part.size].reshape(part.shape))
        start += part.size
    return (
        out_bytes,
        grad_bytes,
        grad_patch_in,
        grad_mixer_in,
        grad_mixer_out,
        grad_patch_out,
        jnp.concatenate([grad_attend, grad_more[:, :D]], axis=1).reshape(-1),
        grad_more[:, D:].reshape(-1),
        grad_gate,
        grad_up,
        grad_down,
        *summed,
    )


def solution(mesh):
    flat = P(("dp", "mp"))
    split = P("mp", "dp", None)
    return jax.shard_map(
        body,
        mesh=mesh,
        in_specs=(split, P())
        + (flat,) * 6
        + (P("dp", "mp"), P("dp", "mp"), P("mp", "dp"))
        + (P(),) * 9
        + (split,),
        out_specs=(split, split)
        + (flat,) * 6
        + (P("dp", "mp"), P("dp", "mp"), P("mp", "dp"))
        + (P(),) * 9,
        check_vma=False,
    )
```

```python
import functools

import jax
import jax.numpy as jnp
from jax import lax
from jax.experimental import pallas as pl
from jax.experimental.pallas import tpu as pltpu
from jax.sharding import PartitionSpec as P

D = 1024
PATCH = 8
INNER = 2048
HEADS_M = 32
STATE = 128
CONV = 4
HEADS_A = 16
HEAD_M = 64
HEAD_A = 64
PROJ = 4384
LANE = 128
VMEM_LIMIT = 60 * 2**20

HIGH = lax.Precision.HIGHEST
EPSILON = 1e-05
BF = jnp.bfloat16
F32 = jnp.float32


MESH = pl.DeviceIdType.MESH


def hail(axes, me, sizes):
    barrier = pltpu.get_barrier_semaphore()
    arrivals = 0
    for axis in axes:
        for k in range(1, sizes[axis]):
            pl.semaphore_signal(
                barrier,
                inc=1,
                device_id={axis: lax.rem(me[axis] + k, sizes[axis])},
                device_id_type=MESH,
            )
        arrivals += sizes[axis] - 1
    return arrivals


def greet(axes, me, sizes):
    pl.semaphore_wait(pltpu.get_barrier_semaphore(), hail(axes, me, sizes))


SUMS = ("sum", "sum1")
SPREADS = ("agh", "agh1")
DMA = pltpu.SemaphoreType.DMA


class Transfer:
    def __init__(self, kind, axis, size, source, target, sems, held=()):
        self.kind, self.axis, self.size = kind, axis, size
        self.source, self.target = source, target
        self.send, self.recv, self.local = sems
        self.here = lax.axis_index(axis)
        self.half = size // 2
        self.twin = self.here + 1 - 2 * lax.rem(self.here, 2)
        self.done, self.later, self.sent = [], [], []
        if kind in SUMS:
            self.mine, self.paired, self.loads = held

    def slot(self, peer):
        if callable(self.source):
            return self.source(peer)
        if self.kind in ("a2a", "sum"):
            return self.source.at[peer]
        if self.kind in ("a2a1", "sum1"):
            return self.source.at[:, peer]
        return self.source

    def block(self, peer):
        return self.target.at[:, peer] if self.kind == "agh1" else self.target.at[peer]

    def remote(self, source, target, number, peer):
        copy = pltpu.make_async_remote_copy(
            src_ref=source,
            dst_ref=target,
            send_sem=self.send.at[number],
            recv_sem=self.recv.at[number],
            device_id={self.axis: peer},
            device_id_type=MESH,
        )
        copy.start()
        return copy

    def start(self, keep_own=True):
        here, size, half, target = self.here, self.size, self.half, self.target
        if self.kind in SPREADS:
            for k in range(1, half):
                copy = self.remote(self.source, self.block(here), k, lax.rem(here + 2 * k, size))
                self.sent.append(copy)
                self.later.append((copy, k))
            self.done.append(self.remote(self.source, self.block(here), 0, self.twin))
        elif self.kind in SUMS:
            for k in list(range(1, half)) + [0]:
                owner = lax.rem(here + 2 * k, size)
                other = owner + 1 - 2 * lax.rem(here, 2)
                copy = self.remote(self.slot(other), self.paired.at[k], k, self.twin)
                self.sent.append(copy)
                load = None
                if self.loads is not None:
                    load = pltpu.make_async_copy(self.slot(owner), self.mine.at[k], self.loads.at[k])
                    load.start()
                self.later.append((copy, k, owner, load))
            return self
        else:
            for k in range(1, size):
                peer = lax.rem(here + k, size)
                self.done.append(self.remote(self.slot(peer), target.at[here], k - 1, peer))
        if keep_own:
            copy = pltpu.make_async_copy(self.slot(here), self.block(here), self.local)
            copy.start()
            self.done.append(copy)
        return self

    def relay(self):
        if self.kind in SPREADS:
            for copy, k in self.later:
                copy.wait_recv()
                block = self.block(lax.rem(self.here + self.size - 2 * k, self.size))
                self.done.append(self.remote(block, block, self.half - 1 + k, self.twin))
        elif self.kind in SUMS:
            for copy, k, owner, load in self.later:
                copy.wait_recv()
                if load is not None:
                    load.wait()
                    own = self.mine[k]
                else:
                    own = self.slot(owner)[...]
                self.mine[k] = (own.astype(F32) + self.paired[k].astype(F32)).astype(self.mine.dtype)
                if k:
                    self.done.append(
                        self.remote(self.mine.at[k], self.target.at[k], self.half - 1 + k, owner)
                    )
                elif load is not None:
                    own = pltpu.make_async_copy(self.mine.at[0], self.target.at[0], self.local)
                    own.start()
                    self.done.append(own)
        self.later = []
        return self

    def finish(self):
        for copy in self.done:
            copy.wait()
        for copy in self.sent:
            copy.wait_send()
        self.done, self.sent = [], []
        return self

    def total(self):
        self.relay()
        self.finish()
        summed = self.mine[0].astype(F32)
        for k in range(1, self.half):
            summed = summed + self.target[k].astype(F32)
        return summed


def transfer_sems(size):
    return [DMA((size - 1,)), DMA((size - 1,)), DMA]


def exchange_kernel(plan, sizes, *refs):
    count = len(plan)
    sources, targets = refs[:count], refs[count : 2 * count]
    scratch = list(refs[2 * count :])
    axes = sorted({axis for _, axis in plan})
    greet(axes, {axis: lax.axis_index(axis) for axis in axes}, sizes)
    moves = []
    for (kind, axis), source, target in zip(plan, sources, targets):
        sems = [scratch.pop(0) for _ in range(3)]
        held = [scratch.pop(0) for _ in range(3)] if kind in SUMS else ()
        moves.append(Transfer(kind, axis, sizes[axis], source, target, sems, held).start())
    order = lambda move: (move.kind not in SUMS, move.axis != "mp")
    for move in sorted(moves, key=order):
        move.relay()
    for move in moves:
        move.finish()


def exchange(ident, *steps):
    plan = tuple((kind, axis) for kind, axis, _ in steps)
    arrays = [array for _, _, array in steps]
    sizes = {axis: lax.axis_size(axis) for _, axis in plan}
    shapes = []
    scratch = []
    moved = 0
    for kind, axis, array in steps:
        shape = array.shape
        size = sizes[axis]
        if kind in ("ag", "agh"):
            shape = (size,) + shape
        elif kind == "agh1":
            shape = (shape[0], size) + shape[1:]
        elif kind == "a2a1":
            shape = (size, shape[0]) + shape[2:]
        elif kind == "sum":
            shape = (size // 2,) + shape[1:]
        elif kind == "sum1":
            shape = (size // 2, shape[0]) + shape[2:]
        shapes.append(jax.ShapeDtypeStruct(shape, array.dtype))
        moved += shapes[-1].size * array.dtype.itemsize
        scratch += transfer_sems(size)
        if kind in SUMS:
            scratch += [pltpu.VMEM(shape, array.dtype)] * 2 + [DMA((size // 2,))]
    return pl.pallas_call(
        functools.partial(exchange_kernel, plan, sizes),
        out_shape=shapes,
        in_specs=[pl.BlockSpec(memory_space=pl.ANY)] * len(plan),
        out_specs=[pl.BlockSpec(memory_space=pl.ANY)] * len(plan),
        scratch_shapes=scratch,
        compiler_params=pltpu.CompilerParams(
            collective_id=ident, has_side_effects=True, vmem_limit_bytes=VMEM_LIMIT
        ),
        cost_estimate=pl.CostEstimate(flops=0, bytes_accessed=64 * moved, transcendentals=0),
    )(*arrays)


def chain_kernel(first, second, inner_steps, forwards, middle, counts, sizes, *refs):
    refs = list(refs)

    def take(count):
        return [refs.pop(0) for _ in range(count)]

    n_given, n_later, n_local, n_made = counts
    sources, given, later = take(len(first)), take(n_given), take(n_later)
    targets = {i: take(1)[0] for i in range(len(first)) if i not in inner_steps}
    local, targets_second, targets_forward = take(n_local), take(len(second)), take(len(forwards))
    axes = sorted({step[1] for step in first + second})
    greet(axes, {axis: lax.axis_index(axis) for axis in axes}, sizes)

    def transfer(kind, axis, source, target):
        sems = take(3)
        held = take(3) if kind in SUMS else ()
        return Transfer(kind, axis, sizes[axis], source, target, sems, held)

    moves = []
    for index, (kind, axis) in enumerate(first):
        target = take(1)[0] if index in inner_steps else targets[index]
        moves.append(transfer(kind, axis, sources[index], target).start())
    made = take(n_made)
    more = []
    for (kind, axis, source), target in zip(second, targets_second):
        source = made[source] if source >= 0 else later[-1 - source]
        more.append(transfer(kind, axis, source, target))
    passed = []
    for target in targets_forward:
        buffer = take(1)[0]
        passed.append((buffer, transfer("a2a", "dp", buffer, target)))
    for move in moves:
        if move.kind in SUMS:
            move.relay()
    extras = [index for index in inner_steps if index and index not in forwards]
    for index in extras:
        moves[index].finish()
    results, kept = middle(moves[0].total(), *[moves[index].target for index in extras], *given)
    for ref, value in zip(made, results):
        ref[...] = value
    for move in more:
        move.start()
    for ref, value in zip(local, kept):
        ref[...] = value
    for index, (buffer, move) in zip(forwards, passed):
        buffer[...] = moves[index].total().astype(BF)
        move.start()
    for move in more:
        if move.kind in SUMS:
            move.relay()
    for move in moves + more:
        move.relay()
    for move in moves + more + [move for _, move in passed]:
        move.finish()


def moved_shape(kind, size, shape):
    if kind in ("ag", "agh"):
        return (size,) + shape
    if kind == "agh1":
        return (shape[0], size) + shape[1:]
    if kind == "a2a1":
        return (size, shape[0]) + shape[2:]
    if kind == "sum":
        return (size // 2,) + shape[1:]
    if kind == "sum1":
        return (size // 2, shape[0]) + shape[2:]
    return shape


def chain(ident, first, middle, given, made, local, second, extras=(), forwards=()):
    sizes = {axis: lax.axis_size(axis) for axis in ("dp", "mp")}
    inner_steps = tuple(sorted({0} | set(extras) | set(forwards)))
    later = [source for _, _, source in second if not isinstance(source, int)]
    plan_second, seen = [], 0
    shapes, local_shapes, second_shapes, scratch = [], list(local), [], []

    def held(kind, axis, shape, dtype):
        scratch.extend(transfer_sems(sizes[axis]))
        if kind in SUMS:
            scratch.extend([pltpu.VMEM(shape, dtype)] * 2 + [DMA((sizes[axis] // 2,))])

    moved = 0
    for index, (kind, axis, array) in enumerate(first):
        shape = moved_shape(kind, sizes[axis], array.shape)
        moved += 2 * array.size
        if index in inner_steps:
            scratch.append(pltpu.VMEM(shape, array.dtype))
        else:
            shapes.append(jax.ShapeDtypeStruct(shape, array.dtype))
        held(kind, axis, shape, array.dtype)
    scratch.extend(pltpu.VMEM(item.shape, item.dtype) for item in made)
    for kind, axis, source in second:
        item = source
        if isinstance(source, int):
            item = made[source]
            plan_second.append((kind, axis, source))
        else:
            seen += 1
            plan_second.append((kind, axis, -seen))
        shape = moved_shape(kind, sizes[axis], item.shape)
        second_shapes.append(jax.ShapeDtypeStruct(shape, item.dtype))
        held(kind, axis, shape, item.dtype)
    forward_shapes = []
    for index in forwards:
        kind, axis, array = first[index]
        shape = moved_shape(kind, sizes[axis], array.shape)[1:]
        forward_shapes.append(jax.ShapeDtypeStruct(shape, BF))
        scratch.append(pltpu.VMEM(shape, BF))
        held("a2a", "dp", shape, BF)
    hbm, vmem = pl.BlockSpec(memory_space=pl.ANY), pl.BlockSpec(memory_space=pltpu.VMEM)
    return pl.pallas_call(
        functools.partial(
            chain_kernel,
            tuple((kind, axis) for kind, axis, _ in first),
            tuple(plan_second),
            inner_steps,
            tuple(forwards),
            middle,
            (len(given), len(later), len(local), len(made)),
            sizes,
        ),
        out_shape=shapes + local_shapes + second_shapes + forward_shapes,
        in_specs=[hbm] * len(first) + [vmem] * len(given) + [hbm] * len(later),
        out_specs=[hbm] * len(shapes)
        + [vmem] * len(local_shapes)
        + [hbm] * (len(second_shapes) + len(forward_shapes)),
        scratch_shapes=scratch,
        compiler_params=pltpu.CompilerParams(
            collective_id=ident, has_side_effects=True, vmem_limit_bytes=VMEM_LIMIT
        ),
        cost_estimate=pl.CostEstimate(flops=0, bytes_accessed=64 * moved, transcendentals=0),
    )(*[array for _, _, array in first], *given, *later)


def norm_step(summed, gain_ref):
    return [root_norm(summed, gain_ref[...]).astype(BF)], [summed]


def mixed_step(summed, squares_ref, global_in_ref):
    squares = squares_ref[0]
    for index in range(1, squares_ref.shape[0]):
        squares = squares + squares_ref[index]
    scale = lax.rsqrt(squares / INNER + EPSILON)
    return [(global_in_ref[...] + scale[:, :1] * summed).astype(BF), scale], [summed]


def grad_mixed_step(summed, unscaled_ref):
    low = summed.astype(BF)
    along = jnp.sum(low.astype(F32) * unscaled_ref[...], axis=1, keepdims=True)
    return [low, jnp.broadcast_to(along, (along.shape[0], LANE))], [summed]


def grad_norm_step(summed, global_in_ref, gain_ref, grad_out_ref):
    grad, gains = norm_back(global_in_ref[...], gain_ref[...], summed)
    gains = jnp.sum(gains, axis=0, keepdims=True)
    return [(grad_out_ref[...] + grad).astype(BF), jnp.broadcast_to(gains, (8, D))], []


def attend_forward_kernel(
    global_ref,
    w_out_ref,
    inputs_ref,
    gain_ref,
    feed_gain_ref,
    w_ref,
    local_ref,
    low_ref,
    qkv_ref,
    attended_ref,
    after_ref,
    feed_ref,
    probs_ref,
    leaving_ref,
    slots_ref,
    chunks_ref,
    *sems,
):
    rows = local_ref.shape[0]
    step = min(rows, 256)
    n_dp, patches, byte_cols = slots_ref.shape
    arrivals = hail(("dp",), {"dp": lax.axis_index("dp")}, {"dp": n_dp})
    leaving_ref[...] = product(global_ref[...], w_out_ref[...]).astype(BF).reshape(slots_ref.shape)
    pl.semaphore_wait(pltpu.get_barrier_semaphore(), arrivals)
    Transfer("a2a", "dp", n_dp, leaving_ref, slots_ref, sems).start().finish()
    for byte in range(PATCH):
        for chunk in range(D // LANE):
            column = byte * D + chunk * LANE
            there = slice(column % byte_cols, column % byte_cols + LANE)
            chunks_ref[chunk, pl.ds(byte, patches, stride=PATCH), :] = slots_ref[
                column // byte_cols, :, there
            ].astype(F32)
    mask = patch_mask(LANE)
    first = lax.broadcasted_iota(jnp.int32, (LANE, LANE), 1) < HEAD_A

    def some(index, _):
        at = pl.ds(pl.multiple_of(index * step, step), step)
        chunks = [chunks_ref[chunk, at, :] for chunk in range(D // LANE)]
        local = inputs_ref[at, :].astype(F32) + jnp.concatenate(chunks, axis=1)
        local_ref[at, :] = local
        low = root_norm(local, gain_ref[...]).astype(BF)
        low_ref[at, :] = low
        qkv_ref[at, :] = product(low, w_ref[:, : 3 * D]).astype(BF)

        def heads(inner, _):
            within = pl.ds(pl.multiple_of(index * step + inner * LANE, LANE), LANE)
            pairs = range(D // LANE)
            scores = []
            for pair in pairs:
                query = qkv_ref[within, pair * LANE : (pair + 1) * LANE]
                keyed = qkv_ref[within, D + pair * LANE : D + (pair + 1) * LANE]
                for half in (first, ~first):
                    scores.append(right_product(jnp.where(half, query, 0), keyed))
            probs = []
            for head, score in enumerate(scores):
                probs.append(patch_probs(score, mask).astype(BF))
                probs_ref[head, within, :] = probs[head]
            for pair in pairs:
                valued = qkv_ref[within, 2 * D + pair * LANE : 2 * D + (pair + 1) * LANE]
                attended_ref[within, pair * LANE : (pair + 1) * LANE] = jnp.where(
                    first, product(probs[2 * pair], valued), product(probs[2 * pair + 1], valued)
                ).astype(BF)
            return 0

        lax.fori_loop(0, step // LANE, heads, 0)
        after = local + product(attended_ref[at, :], w_ref[:, 3 * D :])
        after_ref[at, :] = after
        feed_ref[at, :] = root_norm(after, feed_gain_ref[...]).astype(BF)
        return 0

    lax.fori_loop(0, rows // step, some, 0)


def patch_mask(count):
    row = lax.broadcasted_iota(jnp.int32, (count, count), 0)
    column = lax.broadcasted_iota(jnp.int32, (count, count), 1)
    return (row // PATCH == column // PATCH) & (column <= row)


def patch_probs(scores, mask):
    scores = jnp.where(mask, scores * HEAD_A ** (-0.5), -1e30)
    expo = jnp.exp(scores - jnp.max(scores, axis=-1, keepdims=True))
    return expo / jnp.sum(expo, axis=-1, keepdims=True)


def attend_forward(ident, global_low, w_patch_out, inputs_low, norm_attend, norm_feed, w_attend):
    rows = inputs_low.shape[0]
    n_dp = lax.axis_size("dp")
    slots = (n_dp, rows // PATCH, w_patch_out.shape[1])
    return pl.pallas_call(
        attend_forward_kernel,
        out_shape=[
            jax.ShapeDtypeStruct((rows, D), F32),
            jax.ShapeDtypeStruct((rows, D), BF),
            jax.ShapeDtypeStruct((rows, 3 * D), BF),
            jax.ShapeDtypeStruct((rows, D), BF),
            jax.ShapeDtypeStruct((rows, D), F32),
            jax.ShapeDtypeStruct((rows, D), BF),
            jax.ShapeDtypeStruct((HEADS_A, rows, LANE), BF),
        ],
        in_specs=[pl.BlockSpec(memory_space=pltpu.VMEM)] * 6,
        out_specs=[pl.BlockSpec(memory_space=pltpu.VMEM)] * 7,
        scratch_shapes=[
            pltpu.VMEM(slots, BF),
            pltpu.VMEM(slots, BF),
            pltpu.VMEM((D // LANE, rows, LANE), F32),
        ]
        + transfer_sems(n_dp),
        compiler_params=pltpu.CompilerParams(
            collective_id=ident, has_side_effects=True, vmem_limit_bytes=VMEM_LIMIT
        ),
        cost_estimate=pl.CostEstimate(
            flops=2 * rows * D * 4 * D, bytes_accessed=24 * D * D, transcendentals=rows * 16 * LANE
        ),
    )(global_low, w_patch_out, inputs_low, norm_attend[None], norm_feed[None], w_attend)


def norm_back(values, gain, grad):
    scale = lax.rsqrt(jnp.mean(values * values, axis=-1, keepdims=True) + EPSILON)
    scaled = grad * gain
    along = jnp.mean(scaled * values, axis=-1, keepdims=True)
    return scale * scaled - values * (scale * scale * scale * along), grad * values * scale


def attend_backward_kernel(
    grad_feed_ref,
    grad_final_ref,
    local_ref,
    after_ref,
    low_ref,
    qkv_ref,
    attended_ref,
    probs_ref,
    gain_ref,
    feed_gain_ref,
    w_ref,
    grad_local_ref,
    grad_slots_ref,
    grad_w_ref,
    grad_more_ref,
    grad_gain_ref,
    grad_feed_gain_ref,
    grads_ref,
    chunks_ref,
    slots_ref,
    *sems,
):
    rows = local_ref.shape[0]
    step = min(rows, 256)
    n_dp, _, byte_cols = grad_slots_ref.shape
    arrivals = hail(("dp",), {"dp": lax.axis_index("dp")}, {"dp": n_dp})
    first = lax.broadcasted_iota(jnp.int32, (LANE, LANE), 1) < HEAD_A
    grad_gain_ref[...] = jnp.zeros_like(grad_gain_ref)
    grad_feed_gain_ref[...] = jnp.zeros_like(grad_feed_gain_ref)

    def some(index, _):
        at = pl.ds(pl.multiple_of(index * step, step), step)
        grad_after, gains = norm_back(after_ref[at, :], feed_gain_ref[...], grad_feed_ref[at, :])
        grad_feed_gain_ref[...] += jnp.sum(gains, axis=0, keepdims=True)
        grad_after = grad_after + grad_final_ref[at, :].astype(F32)
        grad_low = grad_after.astype(BF)
        grads_ref[at, 3 * D :] = grad_low
        grad_attended = right_product(grad_low, w_ref[:, 3 * D :]).astype(BF)
        grads_ref[at, :D] = grad_attended

        def heads(inner, _):
            within = pl.ds(pl.multiple_of(index * step + inner * LANE, LANE), LANE)
            pairs = range(D // LANE)

            def part(number, pair):
                return slice(number * D + pair * LANE, number * D + (pair + 1) * LANE)

            given = [grads_ref[within, part(0, pair)] for pair in pairs]
            grad_probs = []
            for pair in pairs:
                for half in (first, ~first):
                    grad_probs.append(
                        right_product(jnp.where(half, given[pair], 0), qkv_ref[within, part(2, pair)])
                    )
            grad_scores = []
            for head, grad in enumerate(grad_probs):
                probs = probs_ref[head, within, :].astype(F32)
                inside = jnp.sum(grad * probs, axis=-1, keepdims=True)
                grad_scores.append((probs * (grad - inside) * HEAD_A ** (-0.5)).astype(BF))
            for pair in pairs:
                query, keyed = qkv_ref[within, part(0, pair)], qkv_ref[within, part(1, pair)]
                two = (2 * pair, 2 * pair + 1)
                results = (
                    [product(grad_scores[head], keyed) for head in two],
                    [left_product(grad_scores[head], query) for head in two],
                    [left_product(probs_ref[head, within, :], given[pair]) for head in two],
                )
                for number in range(3):
                    grads_ref[within, part(number, pair)] = jnp.where(first, *results[number]).astype(BF)
            return 0

        lax.fori_loop(0, step // LANE, heads, 0)
        grad_normed = right_product(grads_ref[at, : 3 * D], w_ref[:, : 3 * D])
        grad_local, gains = norm_back(local_ref[at, :], gain_ref[...], grad_normed)
        grad_gain_ref[...] += jnp.sum(gains, axis=0, keepdims=True)
        grad_local = grad_after + grad_local
        grad_local_ref[at, :] = grad_local
        for chunk in range(D // LANE):
            chunks_ref[chunk, at, :] = grad_local[:, chunk * LANE : (chunk + 1) * LANE]
        return 0

    lax.fori_loop(0, rows // step, some, 0)
    for byte in range(PATCH):
        for chunk in range(D // LANE):
            slots_ref[byte, :, chunk * LANE : (chunk + 1) * LANE] = chunks_ref[
                chunk, pl.ds(byte, rows // PATCH, stride=PATCH), :
            ].astype(BF)
    shares = D // byte_cols

    def slot(peer):
        if shares == 1:
            return slots_ref.at[peer]
        column = pl.multiple_of(lax.rem(peer, shares) * byte_cols, byte_cols)
        return slots_ref.at[peer // shares, :, pl.ds(column, byte_cols)]

    pl.semaphore_wait(pltpu.get_barrier_semaphore(), arrivals)
    move = Transfer("a2a", "dp", n_dp, slot, grad_slots_ref, sems).start()

    n_mp, _, k_rows, _ = grad_w_ref.shape
    each = 256 // (n_mp * k_rows)

    def columns(index, _):
        at = pl.ds(pl.multiple_of(index * 256, 256), 256)
        for source, number, there in (
            (low_ref, 0, slice(0, 2 * D)),
            (low_ref, 2, slice(0, D)),
            (attended_ref, 3, slice(D, 2 * D)),
        ):
            width = there.stop - there.start
            target = grad_w_ref if number == 0 else grad_more_ref
            grad = left_product(source[:, at], grads_ref[:, number * D : number * D + width])
            grad = grad.astype(BF)
            for place in range(each):
                for owner in range(n_mp):
                    start = (place * n_mp + owner) * k_rows
                    target[owner, index * each + place, :, there] = grad[start : start + k_rows]
        return 0

    lax.fori_loop(0, D // 256, columns, 0)
    move.finish()


def attend_backward(ident, grad_feed, grad_final, local_in, after, low, qkv, attended, probs, gain, feed_gain, w):
    rows = local_in.shape[0]
    n_dp, n_mp = lax.axis_size("dp"), lax.axis_size("mp")
    vmem = pl.BlockSpec(memory_space=pltpu.VMEM)
    return pl.pallas_call(
        attend_backward_kernel,
        out_shape=[
            jax.ShapeDtypeStruct((rows, D), F32),
            jax.ShapeDtypeStruct((n_dp, rows // PATCH, PATCH * D // n_dp), BF),
            jax.ShapeDtypeStruct((n_mp, n_dp, D // (n_dp * n_mp), 2 * D), BF),
            jax.ShapeDtypeStruct((n_mp, n_dp, D // (n_dp * n_mp), 2 * D), BF),
            jax.ShapeDtypeStruct((1, D), F32),
            jax.ShapeDtypeStruct((1, D), F32),
        ],
        in_specs=[vmem] * 11,
        out_specs=[vmem, pl.BlockSpec(memory_space=pl.ANY)] + [vmem] * 4,
        scratch_shapes=[
            pltpu.VMEM((rows, 4 * D), BF),
            pltpu.VMEM((D // LANE, rows, LANE), F32),
            pltpu.VMEM((PATCH, rows // PATCH, D), BF),
        ]
        + transfer_sems(n_dp),
        compiler_params=pltpu.CompilerParams(
            collective_id=ident, has_side_effects=True, vmem_limit_bytes=VMEM_LIMIT
        ),
        cost_estimate=pl.CostEstimate(
            flops=4 * rows * D * 4 * D, bytes_accessed=40 * D * D, transcendentals=rows * 16 * LANE
        ),
    )(grad_feed, grad_final, local_in, after, low, qkv, attended, probs, gain[None], feed_gain[None], w)


def feed_kernel(
    n_mp,
    x_ref,
    c_ref,
    w_ref,
    out_ref,
    grad_feed_ref,
    grads_ref,
    held,
    hidden,
    grad_gate,
    grad_up,
    grad_held,
    paired,
    arrived,
    staged,
    own_sem,
    stage_sems,
    ag_send,
    ag_recv,
    pair_send,
    pair_recv,
    far_send,
    far_recv,
):
    rows = x_ref.shape[0]
    chips = n_mp // 2
    units = w_ref.shape[-1]
    here = lax.axis_index("mp")
    core = lax.rem(here, 2)
    twin = here + 1 - 2 * core
    pieces = 2
    size = rows // pieces
    greet(("mp",), {"mp": here}, {"mp": n_mp})

    def block(owner):
        return pl.ds(pl.multiple_of(owner * rows, rows), rows)

    def part(owner, piece):
        return pl.ds(pl.multiple_of(owner * rows + piece * size, size), size)

    def remote(source, target, send, recv, peer):
        copy = pltpu.make_async_remote_copy(
            src_ref=source,
            dst_ref=target,
            send_sem=send,
            recv_sem=recv,
            device_id={"mp": peer},
            device_id_type=MESH,
        )
        copy.start()
        return copy

    own = pltpu.make_async_copy(x_ref, held.at[block(here)], own_sem)
    own.start()
    far = [lax.rem(here + 2 * k, n_mp) for k in range(chips)]
    came = [lax.rem(here + n_mp - 2 * k, n_mp) for k in range(chips)]
    direct = {}
    near = remote(x_ref, held.at[block(here)], ag_send.at[0, 0], ag_recv.at[0, 0], twin)
    for piece in range(pieces):
        for k in range(1, chips):
            direct[k, piece] = remote(
                x_ref.at[part(0, piece)],
                held.at[part(here, piece)],
                ag_send.at[k, piece],
                ag_recv.at[k, piece],
                far[k],
            )

    def weight(number):
        return w_ref[:, number].reshape(D, units)

    stored, relays, pairs, sends = [], {}, {}, {}

    def work(owner, piece):
        number = len(stored)
        slot = number % 2
        if number >= 2:
            stored[number - 2].wait()
        at = part(owner, piece)
        x = held[at, :]
        gate = product(x, weight(0))
        up = product(x, weight(1))
        sigmoid = jax.nn.sigmoid(gate)
        silu = gate * sigmoid
        low = (silu * up).astype(BF)
        hidden[at, :] = low
        grad_hidden = product(c_ref[at, :], weight(2))
        gate_low = (grad_hidden * up * sigmoid * (1.0 + gate * (1.0 - sigmoid))).astype(BF)
        up_low = (grad_hidden * silu).astype(BF)
        grad_gate[at, :] = gate_low
        grad_up[at, :] = up_low
        staged[slot] = right_product(low, weight(2)).astype(BF)
        grad_held[at, :] = (
            right_product(gate_low, weight(0)) + right_product(up_low, weight(1))
        ).astype(BF)
        copy = pltpu.make_async_copy(staged.at[slot], out_ref.at[at], stage_sems.at[number])
        copy.start()
        stored.append(copy)

    def relay(k, piece):
        direct[k, piece].wait_recv()
        at = part(came[k], piece)
        relays[k, piece] = remote(
            held.at[at], held.at[at], ag_send.at[chips - 1 + k, piece], ag_recv.at[chips - 1 + k, piece], twin
        )

    def other(k):
        return came[k] + 1 - 2 * core

    def to_twin(k, piece):
        pairs[k, piece] = remote(
            grad_held.at[part(other(k), piece)],
            paired.at[k, part(0, piece)],
            pair_send.at[k, piece],
            pair_recv.at[k, piece],
            twin,
        )

    def onward(k, piece):
        pairs[k, piece].wait_recv()
        at = part(came[k], piece)
        both = grad_held[at, :].astype(F32) + paired[k, part(0, piece), :].astype(F32)
        grad_held[at, :] = both.astype(BF)
        if k:
            sends[k, piece] = remote(
                grad_held.at[at],
                arrived.at[k - 1, part(0, piece)],
                far_send.at[k - 1, piece],
                far_recv.at[k - 1, piece],
                came[k],
            )

    own.wait()
    for piece in range(pieces):
        work(here, piece)
    near.wait_recv()
    for piece in range(pieces):
        for k in range(1, chips):
            relay(k, piece)
        work(twin, piece)
        to_twin(0, piece)
        for k in range(1, chips):
            if piece:
                onward(k, piece - 1)
            relays[k, piece].wait_recv()
            work(other(k), piece)
            to_twin(k, piece)
            work(came[k], piece)

    def tiles(start, stop):
        def some(index, _):
            at = pl.ds(pl.multiple_of(index * LANE, LANE), LANE)
            x = held[:, at]
            each = grads_ref.shape[2]
            owners = pl.ds(index * (LANE // each), LANE // each)

            def store(number, value):
                grads_ref[owners, number] = value.astype(BF).reshape(LANE // each, each, units)

            store(0, left_product(x, grad_gate[...]))
            store(1, left_product(x, grad_up[...]))
            store(2, left_product(c_ref[:, at], hidden[...]))
            return 0

        lax.fori_loop(start, stop, some, 0)

    for k in range(1, chips):
        onward(k, pieces - 1)
    count = D // LANE
    tiles(0, count)
    for piece in range(pieces):
        onward(0, piece)
    total_here = grad_held[block(here), :].astype(F32)
    for k in range(1, chips):
        for piece in range(pieces):
            sends[k, piece].wait_recv()
        total_here = total_here + arrived[k - 1].astype(F32)
    grad_feed_ref[...] = total_here
    near.wait_send()
    for group in (direct, relays, pairs, sends):
        for copy in group.values():
            copy.wait_send()
    for copy in stored[-2:]:
        copy.wait()


def feed_section(ident, feed_low, grad_rows, weights):
    n_mp = lax.axis_size("mp")
    rows = feed_low.shape[0]
    every = rows * n_mp
    chips = n_mp // 2
    units = weights.shape[-1]
    dma = pltpu.SemaphoreType.DMA
    vmem = pl.BlockSpec(memory_space=pltpu.VMEM)
    return pl.pallas_call(
        functools.partial(feed_kernel, n_mp),
        out_shape=[
            jax.ShapeDtypeStruct((every, D), BF),
            jax.ShapeDtypeStruct((rows, D), F32),
            jax.ShapeDtypeStruct(weights.shape, BF),
        ],
        in_specs=[vmem] * 3,
        out_specs=[pl.BlockSpec(memory_space=pl.ANY), vmem, vmem],
        scratch_shapes=[
            pltpu.VMEM((every, D), BF),
            pltpu.VMEM((every, units), BF),
            pltpu.VMEM((every, units), BF),
            pltpu.VMEM((every, units), BF),
            pltpu.VMEM((every, D), BF),
            pltpu.VMEM((chips, rows, D), BF),
            pltpu.VMEM((chips - 1, rows, D), BF),
            pltpu.VMEM((2, rows // 2, D), BF),
            dma,
            dma((2 * n_mp,)),
            dma((n_mp - 1, 2)),
            dma((n_mp - 1, 2)),
            dma((chips, 2)),
            dma((chips, 2)),
            dma((chips - 1, 2)),
            dma((chips - 1, 2)),
        ],
        compiler_params=pltpu.CompilerParams(
            collective_id=ident, has_side_effects=True, vmem_limit_bytes=VMEM_LIMIT
        ),
        cost_estimate=pl.CostEstimate(
            flops=18 * every * D * units, bytes_accessed=30 * D * D, transcendentals=every * units
        ),
    )(feed_low, grad_rows, weights)


def product(left, right):
    return jnp.dot(left, right, preferred_element_type=F32)


def left_product(left, right):
    return lax.dot_general(left, right, (((0,), (0,)), ((), ())), preferred_element_type=F32)


def right_product(left, right):
    return lax.dot_general(left, right, (((1,), (1,)), ((), ())), preferred_element_type=F32)


def total(parts):
    return jnp.sum(parts.astype(F32), axis=0)


def root_norm(values, gain):
    return values * lax.rsqrt(jnp.mean(values * values, axis=-1, keepdims=True) + EPSILON) * gain


def shifted(values, steps):
    if steps == 0:
        return values
    row = lax.broadcasted_iota(jnp.int32, values.shape, 0)
    return jnp.where(row >= steps, pltpu.roll(values, steps, 0), 0.0)


def lifted(values, steps):
    if steps == 0:
        return values
    count = values.shape[0]
    row = lax.broadcasted_iota(jnp.int32, values.shape, 0)
    return jnp.where(row < count - steps, pltpu.roll(values, count - steps, 0), 0.0)


def running(values, move):
    steps = 1
    while steps < values.shape[0]:
        values = values + move(values, steps)
        steps *= 2
    return values


def softplus(values):
    return jnp.maximum(values, 0.0) + jnp.log1p(jnp.exp(-jnp.abs(values)))


class Mixer:
    def __init__(self, projected, inner, conv_weight, conv_bias, step_bias, decay_rate):
        self.inner = inner
        self.count = projected.shape[0]
        self.width = min(inner, LANE)
        self.per_group = self.width // HEAD_M
        self.tile = min(self.count, 256)
        edge = 2 * inner + 2 * STATE
        self.conv_input = projected[:, inner:edge]
        self.conv_weight = conv_weight
        summed = conv_bias + conv_weight[CONV - 1 : CONV] * self.conv_input
        for shift in range(1, CONV):
            row = CONV - 1 - shift
            summed = summed + conv_weight[row : row + 1] * shifted(self.conv_input, shift)
        self.sigmoid = jax.nn.sigmoid(summed)
        self.summed = summed
        self.activated = summed * self.sigmoid
        self.raw = projected[:, edge:] + step_bias
        self.step = softplus(self.raw)
        self.rate = jnp.exp(decay_rate)
        self.log_decay = running(self.step * -self.rate, shifted)
        self.log_decay_t = self.log_decay.T
        self.step_t = self.step.T
        low = self.activated.astype(BF)
        self.heads_low = low[:, :inner]
        self.input_low = low[:, inner : inner + STATE]
        self.output_low = low[:, inner + STATE :]
        lane = lax.broadcasted_iota(jnp.int32, (1, self.width), 1)
        self.lanes = [lane // HEAD_M == h for h in range(self.per_group)]

    def tiles(self):
        for start in range(0, self.count, self.tile):
            stop = start + self.tile
            scores = right_product(self.output_low[start:stop], self.input_low[:stop])
            row = lax.broadcasted_iota(jnp.int32, scores.shape, 0) + start
            causal = row >= lax.broadcasted_iota(jnp.int32, scores.shape, 1)
            yield start, stop, scores, causal

    def factor(self, head, start, stop, causal):
        spread = self.log_decay[start:stop, head : head + 1] - self.log_decay_t[head : head + 1, :stop]
        return jnp.exp(jnp.where(causal, spread, -1e30))

    def groups(self):
        return range(self.inner // self.width)

    def merged(self, parts):
        if len(parts) == 1:
            return parts[0]
        return jnp.where(self.lanes[0], parts[0], parts[1])


def mixer_forward_kernel(
    inner, normed_ref, w_ref, w_out_ref, conv_weight_ref, conv_bias_ref, step_bias_ref, decay_ref, skip_ref, gain_ref,
    projected_ref, values_ref, parts_ref, squares_ref,
):
    projected_ref[...] = product(normed_ref[...], w_ref[...])
    mixer = Mixer(
        projected_ref[...], inner, conv_weight_ref[...], conv_bias_ref[...], step_bias_ref[...], decay_ref[...]
    )
    for start, stop, scores, causal in mixer.tiles():
        for group in mixer.groups():
            at = slice(group * mixer.width, (group + 1) * mixer.width)
            parts = []
            for h in range(mixer.per_group):
                head = group * mixer.per_group + h
                weights = (
                    mixer.factor(head, start, stop, causal) * scores * mixer.step_t[head : head + 1, :stop]
                )
                parts.append(product(weights.astype(BF), mixer.heads_low[:stop, at]))
            values_ref[start:stop, at] = (
                mixer.merged(parts) + skip_ref[:, at] * mixer.activated[start:stop, at]
            )
    gate = projected_ref[:, :inner]
    gated = values_ref[...] * (gate * jax.nn.sigmoid(gate))
    squares = jnp.sum(gated * gated, axis=1, keepdims=True)
    squares_ref[...] = jnp.broadcast_to(squares, squares_ref.shape)
    parts_ref[...] = product((gated * gain_ref[...]).astype(BF), w_out_ref[...]).astype(BF)


def mixer_backward_kernel(
    inner,
    grad_ref,
    scales_ref,
    alongs_ref,
    normed_ref,
    projected_ref,
    values_ref,
    w_ref,
    w_out_ref,
    conv_weight_ref,
    conv_bias_ref,
    step_bias_ref,
    decay_ref,
    skip_ref,
    gain_ref,
    parts_ref,
    grad_w_ref,
    grad_w_out_ref,
    grad_conv_weight_ref,
    grad_conv_bias_ref,
    grad_heads_ref,
    grad_skip_ref,
    grad_gain_ref,
    grad_act_ref,
    columns_ref,
    grads_ref,
):
    mixer = Mixer(
        projected_ref[...], inner, conv_weight_ref[...], conv_bias_ref[...], step_bias_ref[...], decay_ref[...]
    )
    count = mixer.count
    edge = 2 * inner + 2 * STATE
    gate = projected_ref[:, :inner]
    sigmoid = jax.nn.sigmoid(gate)
    silu = gate * sigmoid
    values = values_ref[...]
    gated = values * silu
    scales = scales_ref[:, :1]
    grad = grad_ref[...]
    grad_w_out_ref[...] = left_product((gated * scales * gain_ref[...]).astype(BF), grad).astype(BF)
    grad_mixed = right_product(grad, w_out_ref[...])
    grad_gain_ref[...] = jnp.sum(grad_mixed * gated * scales, axis=0, keepdims=True)
    grad_gated = scales * gain_ref[...] * grad_mixed - gated * (scales**3 * alongs_ref[:, :1] / INNER)
    grad_values = grad_gated * silu
    grads_ref[:, :inner] = (grad_gated * values * (sigmoid * (1.0 + gate * (1.0 - sigmoid)))).astype(BF)
    heads_x = mixer.activated[:, :inner]
    grad_skip_ref[...] = jnp.sum(grad_values * heads_x, axis=0, keepdims=True)
    grad_act_ref[:, :inner] = grad_values * skip_ref[...]
    grad_act_ref[:, inner:] = jnp.zeros((count, 2 * STATE), F32)
    columns_ref[...] = jnp.zeros_like(columns_ref)
    grad_low = grad_values.astype(BF)
    lane = lax.broadcasted_iota(jnp.int32, (mixer.tile, LANE), 1)
    grad_decays = []
    for start, stop, scores, causal in mixer.tiles():
        grad_scores = jnp.zeros_like(scores)
        grad_decay = jnp.zeros((mixer.tile, LANE), F32)
        for group in mixer.groups():
            at = slice(group * mixer.width, (group + 1) * mixer.width)
            grad_group = grad_low[start:stop, at]
            parts = []
            for h in range(mixer.per_group):
                head = group * mixer.per_group + h
                row = slice(head, head + 1)
                factor = mixer.factor(head, start, stop, causal)
                step = mixer.step_t[row, :stop]
                unstepped = factor * scores
                grad_weights = right_product(
                    jnp.where(mixer.lanes[h], grad_group, 0), mixer.heads_low[:stop, at]
                )
                parts.append(left_product((unstepped * step).astype(BF), grad_group))
                grad_scores = grad_scores + grad_weights * factor * step
                grad_unstepped = grad_weights * unstepped
                columns_ref[row, :stop] += jnp.sum(grad_unstepped, axis=0, keepdims=True)
                summed = jnp.sum(grad_unstepped * step, axis=1, keepdims=True)
                grad_decay = jnp.where(lane == head, summed, grad_decay)
            grad_act_ref[:stop, at] += mixer.merged(parts)
        grad_decays.append(grad_decay)
        low = grad_scores.astype(BF)
        grad_act_ref[:stop, inner : inner + STATE] += left_product(low, mixer.output_low[start:stop])
        grad_act_ref[start:stop, inner + STATE :] += product(low, mixer.input_low[:stop])
    columns = columns_ref[...].T
    grad_decay = jnp.concatenate(grad_decays, axis=0) - mixer.step * columns
    onward = running(grad_decay, lifted)
    grad_step = columns - onward * mixer.rate
    grad_raw = grad_step * jax.nn.sigmoid(mixer.raw)
    grads_ref[:, edge:] = grad_raw.astype(BF)
    grad_heads_ref[0:1] = jnp.sum(grad_raw, axis=0, keepdims=True)
    grad_heads_ref[1:2] = -jnp.sum(onward * mixer.step, axis=0, keepdims=True) * mixer.rate
    grad_summed = grad_act_ref[...] * (mixer.sigmoid * (1.0 + mixer.summed * (1.0 - mixer.sigmoid)))
    grad_conv_bias_ref[...] = jnp.sum(grad_summed, axis=0, keepdims=True)
    grad_conv = jnp.zeros_like(grad_summed)
    for shift in range(CONV):
        row = slice(CONV - 1 - shift, CONV - shift)
        grad_conv = grad_conv + conv_weight_ref[row] * lifted(grad_summed, shift)
        grad_conv_weight_ref[row] = jnp.sum(
            grad_summed * shifted(mixer.conv_input, shift), axis=0, keepdims=True
        )
    grads_ref[:, inner:edge] = grad_conv.astype(BF)
    parts_ref[...] = right_product(grads_ref[...], w_ref[...]).astype(BF)
    grad_w_ref[...] = left_product(normed_ref[...], grads_ref[...]).astype(BF)


def whole_kernel(kernel, shapes, operands, scratch=(), flops=0):
    vmem = pl.BlockSpec(memory_space=pltpu.VMEM)
    moved = sum(x.size * x.dtype.itemsize for x in list(operands) + list(shapes))
    return pl.pallas_call(
        kernel,
        out_shape=shapes,
        in_specs=[vmem] * len(operands),
        out_specs=[vmem] * len(shapes),
        scratch_shapes=list(scratch),
        compiler_params=pltpu.CompilerParams(vmem_limit_bytes=VMEM_LIMIT),
        cost_estimate=pl.CostEstimate(flops=flops, bytes_accessed=3 * moved, transcendentals=0),
    )(*operands)


def own_columns(array, place, width):
    return lax.dynamic_slice_in_dim(array, place * width, width, axis=-1)


def tucked(row):
    return jnp.pad(row[:, None, :], ((0, 0), (0, 7), (0, -row.shape[1] % LANE)))


def body(
    byte_embeds,
    lengths,
    patch_in,
    mixer_in,
    mixer_out,
    patch_out,
    attend_in,
    attend_out,
    gate_weight,
    up_weight,
    down_weight,
    norm_global,
    conv_weight,
    conv_bias,
    step_bias,
    decay_rate,
    skip_gain,
    norm_gated,
    norm_attend,
    norm_feed,
    cotangent,
):
    n_dp, n_mp = lax.axis_size("dp"), lax.axis_size("mp")
    devices = n_dp * n_mp
    rows = byte_embeds.shape[1]
    patches = rows // PATCH
    count = patches * n_dp
    group = lax.axis_index("mp")
    place = lax.axis_index("dp")
    length = jnp.sum(jnp.where(jnp.arange(lengths.shape[0], dtype=jnp.int32) == group, lengths, 0))
    position = place * rows + jnp.arange(rows, dtype=jnp.int32)
    keep = (position < length).astype(F32)[:, None]
    inputs = byte_embeds[0].astype(F32) * keep

    heads = HEADS_M // n_dp
    inner = heads * HEAD_M
    byte_cols = PATCH * D // n_dp
    k_rows = D // devices
    step_pad = -heads % LANE
    cols = 2 * inner + 2 * STATE + heads + step_pad

    w_attend = lax.all_gather(
        jnp.concatenate([attend_in.reshape(k_rows, -1), attend_out.reshape(k_rows, -1)], axis=1),
        ("dp", "mp"),
        axis=0,
        tiled=True,
    )
    w_feed = lax.all_gather(jnp.stack([gate_weight, up_weight, down_weight.T]), "dp", axis=0)
    grad_final = (cotangent[0].astype(F32) * keep).astype(BF)

    mixer_rows = mixer_in.reshape(k_rows, PROJ)
    shared = mixer_rows[:, 2 * INNER : 2 * INNER + 2 * STATE]
    by_part = jnp.concatenate(
        [
            mixer_rows[:, :INNER].reshape(k_rows, n_dp, inner),
            mixer_rows[:, INNER : 2 * INNER].reshape(k_rows, n_dp, inner),
            jnp.broadcast_to(shared[:, None], (k_rows, n_dp, 2 * STATE)),
            mixer_rows[:, 2 * INNER + 2 * STATE :].reshape(k_rows, n_dp, heads),
            jnp.zeros((k_rows, n_dp, step_pad), BF),
        ],
        axis=2,
    ).transpose(1, 0, 2)
    out_by_part = patch_out.reshape(k_rows, n_dp, byte_cols).transpose(1, 0, 2)
    patch_rows = inputs.astype(BF).reshape(patches, n_dp, byte_cols).transpose(1, 0, 2)
    patch_rows, mixer_cols, w_patch_in = exchange(
        0,
        ("a2a", "dp", patch_rows),
        ("a2a", "dp", by_part),
        ("agh", "mp", patch_in.reshape(-1, D)),
    )
    patch_rows = patch_rows.reshape(count, byte_cols)
    w_patch_in = w_patch_in.reshape(byte_cols, D)
    parts = product(patch_rows, w_patch_in).reshape(n_dp, patches, D)
    row, lanes = jax.ShapeDtypeStruct((patches, D), F32), jax.ShapeDtypeStruct((patches, LANE), F32)
    row_low = jax.ShapeDtypeStruct((patches, D), BF)
    mixer_cols, global_in, normed, out_cols, w_mixer_out = chain(
        1,
        [("sum", "dp", parts), ("agh1", "mp", mixer_cols)],
        norm_step,
        [norm_global[None]],
        [row_low],
        [row],
        [("agh", "dp", 0), ("a2a", "dp", out_by_part), ("agh", "mp", mixer_out.reshape(-1, D))],
    )
    w_mixer_in = mixer_cols.reshape(D, cols)
    w_mixer_out = w_mixer_out.reshape(inner, D)
    normed = normed.reshape(count, D)

    def own_conv(array):
        return jnp.concatenate(
            [own_columns(array[..., :INNER], place, inner), array[..., INNER:]], axis=-1
        )

    def own_heads(array):
        return jnp.pad(own_columns(array, place, heads), (0, step_pad))[None]

    own_gain = own_columns(norm_gated, place, inner)[None]
    mixer_params = (
        own_conv(conv_weight),
        own_conv(conv_bias)[None],
        own_heads(step_bias),
        own_heads(decay_rate),
        jnp.repeat(own_columns(skip_gain, place, heads), HEAD_M)[None],
        own_gain,
    )
    projected, values, parts, squares = whole_kernel(
        functools.partial(mixer_forward_kernel, inner),
        [
            jax.ShapeDtypeStruct((count, cols), F32),
            jax.ShapeDtypeStruct((count, inner), F32),
            jax.ShapeDtypeStruct((count, D), BF),
            jax.ShapeDtypeStruct((count, LANE), F32),
        ],
        (normed, w_mixer_in, w_mixer_out) + mixer_params,
        flops=2 * count * D * (cols + inner),
    )
    out_cols, grad_feed_rows, unscaled, global_low, scales = chain(
        3,
        [
            ("sum", "dp", parts.reshape(n_dp, patches, D)),
            ("a2a", "dp", squares.reshape(n_dp, patches, LANE)),
            ("agh1", "mp", out_cols),
            ("agh", "mp", grad_final),
        ],
        mixed_step,
        [global_in],
        [row_low, lanes],
        [row],
        [("agh", "dp", 0), ("agh", "dp", 1)],
        extras=(1,),
    )
    w_patch_out = out_cols.reshape(D, byte_cols)
    global_low = global_low.reshape(count, D)
    scales = scales.reshape(count, LANE)

    local_in, attend_low, qkv, attended_low, after_attend, feed_low, probs = attend_forward(
        5, global_low, w_patch_out, inputs.astype(BF), norm_attend, norm_feed, w_attend
    )
    feed_parts, grad_feed_normed, grad_feed = feed_section(
        12, feed_low, grad_feed_rows.reshape(-1, D), w_feed
    )
    units = grad_feed.shape[-1]
    grad_feed = lax.psum_scatter(
        grad_feed.reshape(3 * D, units), "dp", scatter_dimension=0, tiled=True
    ).astype(F32)
    grad_gate, grad_up, grad_down = grad_feed.reshape(3, D // n_dp, units)
    grad_down = grad_down.T
    grad_local, grad_slots, grad_attend, grad_more, grad_norm_attend, grad_norm_feed = attend_backward(
        6,
        grad_feed_normed,
        grad_final,
        local_in,
        after_attend,
        attend_low,
        qkv,
        attended_low,
        probs,
        norm_attend,
        norm_feed,
        w_attend,
    )
    grad_norm_attend, grad_norm_feed = grad_norm_attend[0], grad_norm_feed[0]

    def owners(grad):
        return grad.astype(BF).reshape(n_dp, n_mp, -1, grad.shape[-1])

    grad_slots = grad_slots.reshape(count, byte_cols)
    grad_patch_out = owners(left_product(global_low, grad_slots))
    parts = right_product(grad_slots, w_patch_out).astype(BF).reshape(n_dp, patches, D)
    grad_attend, grad_global_out, grad_mixer_low, alongs, grad_more, grad_patch_out = chain(
        7,
        [("sum", "dp", parts), ("sum1", "mp", grad_patch_out), ("sum", "mp", grad_attend)],
        grad_mixed_step,
        [unscaled],
        [row_low, lanes],
        [row],
        [("agh", "dp", 0), ("agh", "dp", 1), ("sum", "mp", grad_more)],
        forwards=(1,),
    )
    grad_mixer_low = grad_mixer_low.reshape(count, D)
    alongs = alongs.reshape(count, LANE)
    conv_cols = inner + 2 * STATE
    (
        parts,
        grad_mixer_in,
        grad_mixer_out,
        grad_conv_weight,
        grad_conv_bias,
        grad_heads,
        grad_skip,
        grad_norm_gated,
    ) = whole_kernel(
        functools.partial(mixer_backward_kernel, inner),
        [
            jax.ShapeDtypeStruct((count, D), BF),
            jax.ShapeDtypeStruct((D, cols), BF),
            jax.ShapeDtypeStruct((inner, D), BF),
            jax.ShapeDtypeStruct((CONV, conv_cols), F32),
            jax.ShapeDtypeStruct((1, conv_cols), F32),
            jax.ShapeDtypeStruct((2, heads + step_pad), F32),
            jax.ShapeDtypeStruct((1, inner), F32),
            jax.ShapeDtypeStruct((1, inner), F32),
        ],
        (grad_mixer_low, scales, alongs, normed, projected, values, w_mixer_in, w_mixer_out)
        + mixer_params,
        scratch=(
            pltpu.VMEM((count, conv_cols), F32),
            pltpu.VMEM((LANE, count), F32),
            pltpu.VMEM((count, cols), BF),
        ),
        flops=4 * count * D * (cols + inner),
    )
    grad_conv_bias, grad_norm_gated = grad_conv_bias[0], grad_norm_gated[0]
    grad_step_bias, grad_decay_rate = grad_heads[0, :heads], grad_heads[1, :heads]
    grad_skip_gain = jnp.sum(grad_skip.reshape(heads, HEAD_M), axis=1)
    parts = parts.reshape(n_dp, patches, D)
    grad_mixer_in = owners(grad_mixer_in)
    def all_columns(part, whole):
        return lax.dynamic_update_slice_in_dim(
            jnp.zeros(part.shape[:-1] + (whole,), F32), part, place * part.shape[-1], axis=-1
        )

    small = [
        jnp.concatenate(
            [all_columns(grad_conv_weight[:, :inner], INNER), grad_conv_weight[:, inner:]], axis=1
        ),
        jnp.concatenate([all_columns(grad_conv_bias[:inner], INNER), grad_conv_bias[inner:]]),
        all_columns(grad_step_bias, HEADS_M),
        all_columns(grad_decay_rate, HEADS_M),
        all_columns(grad_skip_gain, HEADS_M),
        all_columns(grad_norm_gated, INNER),
        grad_norm_attend,
        grad_norm_feed,
    ]
    packed = jnp.concatenate([part.reshape(-1) for part in small])
    packed = jnp.pad(packed, (0, -packed.shape[0] % (8 * LANE))).reshape(-1, LANE)
    grad_mixer_out, feed_parts, grad_attend, packed, grad_global_low, gains, grad_more, grad_mixer_in = chain(
        9,
        [
            ("sum", "dp", parts),
            ("sum1", "mp", grad_mixer_in),
            ("sum", "mp", grad_mixer_out.reshape(n_mp, -1, D)),
            ("sum", "mp", feed_parts.reshape(n_mp, rows, D)),
            ("sum", "dp", total(grad_attend).astype(BF)),
            ("agh", "mp", packed),
        ],
        grad_norm_step,
        [global_in, norm_global[None], grad_global_out],
        [row_low, jax.ShapeDtypeStruct((8, D), F32)],
        [],
        [("agh", "dp", 0), ("agh", "mp", 1), ("sum", "dp", total(grad_more).astype(BF))],
        forwards=(1,),
    )
    grad_mixer_out = total(grad_mixer_out).reshape(-1)
    grad_attend, grad_more = total(grad_attend), total(grad_more)
    grad_global_low = grad_global_low.reshape(count, D)
    grad_patch_rows = right_product(grad_global_low, w_patch_in).astype(BF)
    grad_patch_in = left_product(patch_rows, grad_global_low).astype(BF)
    grad_patch_rows, grad_patch_in, packed, gains = exchange(
        11,
        ("a2a", "dp", grad_patch_rows.reshape(n_dp, patches, byte_cols)),
        ("sum", "mp", grad_patch_in.reshape(n_mp, -1, D)),
        ("agh", "dp", total(packed)),
        ("agh", "dp", total(gains)),
    )
    grad_patch_in = total(grad_patch_in).reshape(-1)
    grad_patch_rows = grad_patch_rows.astype(F32).transpose(1, 0, 2).reshape(rows, D)
    grad_bytes = ((grad_local + grad_patch_rows) * keep).astype(BF)[None]
    out_bytes = ((after_attend + total(feed_parts)) * keep).astype(BF)[None]
    grad_patch_out = grad_patch_out.astype(F32).transpose(1, 0, 2).reshape(-1)
    grad_mixer_in = grad_mixer_in.astype(F32).transpose(1, 0, 2)
    edges = (inner, 2 * inner, 2 * inner + 2 * STATE, 2 * inner + 2 * STATE + heads)
    grad_mixer_in = jnp.concatenate(
        [
            grad_mixer_in[:, :, : edges[0]].reshape(k_rows, INNER),
            grad_mixer_in[:, :, edges[0] : edges[1]].reshape(k_rows, INNER),
            jnp.sum(grad_mixer_in[:, :, edges[1] : edges[2]], axis=1),
            grad_mixer_in[:, :, edges[2] : edges[3]].reshape(k_rows, HEADS_M),
        ],
        axis=1,
    ).reshape(-1)
    packed = total(packed).reshape(-1)
    summed, start = [], 0
    for part in small:
        summed.append(packed[start : start + part.size].reshape(part.shape))
        start += part.size
    return (
        out_bytes,
        grad_bytes,
        grad_patch_in,
        grad_mixer_in,
        grad_mixer_out,
        grad_patch_out,
        jnp.concatenate([grad_attend, grad_more[:, :D]], axis=1).reshape(-1),
        grad_more[:, D:].reshape(-1),
        grad_gate,
        grad_up,
        grad_down,
        total(gains)[0],
        *summed,
    )


def solution(mesh):
    flat = P(("dp", "mp"))
    split = P("mp", "dp", None)
    return jax.shard_map(
        body,
        mesh=mesh,
        in_specs=(split, P())
        + (flat,) * 6
        + (P("dp", "mp"), P("dp", "mp"), P("mp", "dp"))
        + (P(),) * 9
        + (split,),
        out_specs=(split, split)
        + (flat,) * 6
        + (P("dp", "mp"), P("dp", "mp"), P("mp", "dp"))
        + (P(),) * 9,
        check_vma=False,
    )
```

```python
import functools

import jax
import jax.numpy as jnp
from jax import lax
from jax.experimental import pallas as pl
from jax.experimental.pallas import tpu as pltpu
from jax.sharding import PartitionSpec as P

D = 1024
PATCH = 8
INNER = 2048
HEADS_M = 32
STATE = 128
CONV = 4
HEADS_A = 16
HEAD_M = 64
HEAD_A = 64
PROJ = 4384
LANE = 128
VMEM_LIMIT = 60 * 2**20

HIGH = lax.Precision.HIGHEST
EPSILON = 1e-05
BF = jnp.bfloat16
F32 = jnp.float32


MESH = pl.DeviceIdType.MESH


def hail(axes, me, sizes):
    barrier = pltpu.get_barrier_semaphore()
    arrivals = 0
    for axis in axes:
        for k in range(1, sizes[axis]):
            pl.semaphore_signal(
                barrier,
                inc=1,
                device_id={axis: lax.rem(me[axis] + k, sizes[axis])},
                device_id_type=MESH,
            )
        arrivals += sizes[axis] - 1
    return arrivals


def greet(axes, me, sizes):
    pl.semaphore_wait(pltpu.get_barrier_semaphore(), hail(axes, me, sizes))


SUMS = ("sum", "sum1")
SPREADS = ("agh", "agh1")
DMA = pltpu.SemaphoreType.DMA


class Transfer:
    def __init__(self, kind, axis, size, source, target, sems, held=()):
        self.kind, self.axis, self.size = kind, axis, size
        self.source, self.target = source, target
        self.send, self.recv, self.local = sems
        self.here = lax.axis_index(axis)
        self.half = size // 2
        self.twin = self.here + 1 - 2 * lax.rem(self.here, 2)
        self.done, self.later, self.sent = [], [], []
        if kind in SUMS:
            self.mine, self.paired, self.loads = held

    def slot(self, peer):
        if callable(self.source):
            return self.source(peer)
        if self.kind in ("a2a", "sum"):
            return self.source.at[peer]
        if self.kind in ("a2a1", "sum1"):
            return self.source.at[:, peer]
        return self.source

    def block(self, peer):
        return self.target.at[:, peer] if self.kind == "agh1" else self.target.at[peer]

    def remote(self, source, target, number, peer):
        copy = pltpu.make_async_remote_copy(
            src_ref=source,
            dst_ref=target,
            send_sem=self.send.at[number],
            recv_sem=self.recv.at[number],
            device_id={self.axis: peer},
            device_id_type=MESH,
        )
        copy.start()
        return copy

    def start(self, keep_own=True):
        here, size, half, target = self.here, self.size, self.half, self.target
        if self.kind in SPREADS:
            for k in range(1, half):
                copy = self.remote(self.source, self.block(here), k, lax.rem(here + 2 * k, size))
                self.sent.append(copy)
                self.later.append((copy, k))
            self.done.append(self.remote(self.source, self.block(here), 0, self.twin))
        elif self.kind in SUMS:
            for k in list(range(1, half)) + [0]:
                owner = lax.rem(here + 2 * k, size)
                other = owner + 1 - 2 * lax.rem(here, 2)
                copy = self.remote(self.slot(other), self.paired.at[k], k, self.twin)
                self.sent.append(copy)
                load = None
                if self.loads is not None:
                    load = pltpu.make_async_copy(self.slot(owner), self.mine.at[k], self.loads.at[k])
                    load.start()
                self.later.append((copy, k, owner, load))
            return self
        else:
            for k in range(1, size):
                peer = lax.rem(here + k, size)
                self.done.append(self.remote(self.slot(peer), target.at[here], k - 1, peer))
        if keep_own:
            copy = pltpu.make_async_copy(self.slot(here), self.block(here), self.local)
            copy.start()
            self.done.append(copy)
        return self

    def relay(self):
        if self.kind in SPREADS:
            for copy, k in self.later:
                copy.wait_recv()
                block = self.block(lax.rem(self.here + self.size - 2 * k, self.size))
                self.done.append(self.remote(block, block, self.half - 1 + k, self.twin))
        elif self.kind in SUMS:
            for copy, k, owner, load in self.later:
                copy.wait_recv()
                if load is not None:
                    load.wait()
                    own = self.mine[k]
                else:
                    own = self.slot(owner)[...]
                self.mine[k] = (own.astype(F32) + self.paired[k].astype(F32)).astype(self.mine.dtype)
                if k:
                    self.done.append(
                        self.remote(self.mine.at[k], self.target.at[k], self.half - 1 + k, owner)
                    )
                elif load is not None:
                    own = pltpu.make_async_copy(self.mine.at[0], self.target.at[0], self.local)
                    own.start()
                    self.done.append(own)
        self.later = []
        return self

    def finish(self):
        for copy in self.done:
            copy.wait()
        for copy in self.sent:
            copy.wait_send()
        self.done, self.sent = [], []
        return self

    def total(self):
        self.relay()
        self.finish()
        summed = self.mine[0].astype(F32)
        for k in range(1, self.half):
            summed = summed + self.target[k].astype(F32)
        return summed


def transfer_sems(size):
    return [DMA((size - 1,)), DMA((size - 1,)), DMA]


def exchange_kernel(plan, sizes, *refs):
    count = len(plan)
    sources, targets = refs[:count], refs[count : 2 * count]
    scratch = list(refs[2 * count :])
    axes = sorted({axis for _, axis in plan})
    greet(axes, {axis: lax.axis_index(axis) for axis in axes}, sizes)
    moves = []
    for (kind, axis), source, target in zip(plan, sources, targets):
        sems = [scratch.pop(0) for _ in range(3)]
        held = [scratch.pop(0) for _ in range(3)] if kind in SUMS else ()
        moves.append(Transfer(kind, axis, sizes[axis], source, target, sems, held).start())
    order = lambda move: (move.kind not in SUMS, move.axis != "mp")
    for move in sorted(moves, key=order):
        move.relay()
    for move in moves:
        move.finish()


def exchange(ident, *steps):
    plan = tuple((kind, axis) for kind, axis, _ in steps)
    arrays = [array for _, _, array in steps]
    sizes = {axis: lax.axis_size(axis) for _, axis in plan}
    shapes = []
    scratch = []
    moved = 0
    for kind, axis, array in steps:
        shape = array.shape
        size = sizes[axis]
        if kind in ("ag", "agh"):
            shape = (size,) + shape
        elif kind == "agh1":
            shape = (shape[0], size) + shape[1:]
        elif kind == "a2a1":
            shape = (size, shape[0]) + shape[2:]
        elif kind == "sum":
            shape = (size // 2,) + shape[1:]
        elif kind == "sum1":
            shape = (size // 2, shape[0]) + shape[2:]
        shapes.append(jax.ShapeDtypeStruct(shape, array.dtype))
        moved += shapes[-1].size * array.dtype.itemsize
        scratch += transfer_sems(size)
        if kind in SUMS:
            scratch += [pltpu.VMEM(shape, array.dtype)] * 2 + [DMA((size // 2,))]
    return pl.pallas_call(
        functools.partial(exchange_kernel, plan, sizes),
        out_shape=shapes,
        in_specs=[pl.BlockSpec(memory_space=pl.ANY)] * len(plan),
        out_specs=[pl.BlockSpec(memory_space=pl.ANY)] * len(plan),
        scratch_shapes=scratch,
        compiler_params=pltpu.CompilerParams(
            collective_id=ident, has_side_effects=True, vmem_limit_bytes=VMEM_LIMIT
        ),
        cost_estimate=pl.CostEstimate(flops=0, bytes_accessed=64 * moved, transcendentals=0),
    )(*arrays)


def chain_kernel(first, second, inner_steps, forwards, middle, counts, sizes, *refs):
    refs = list(refs)

    def take(count):
        return [refs.pop(0) for _ in range(count)]

    n_given, n_later, n_local, n_made = counts
    sources, given, later = take(len(first)), take(n_given), take(n_later)
    targets = {i: take(1)[0] for i in range(len(first)) if i not in inner_steps}
    local, targets_second, targets_forward = take(n_local), take(len(second)), take(len(forwards))
    axes = sorted({step[1] for step in first + second})
    greet(axes, {axis: lax.axis_index(axis) for axis in axes}, sizes)

    def transfer(kind, axis, source, target):
        sems = take(3)
        held = take(3) if kind in SUMS else ()
        return Transfer(kind, axis, sizes[axis], source, target, sems, held)

    moves = []
    for index, (kind, axis) in enumerate(first):
        target = take(1)[0] if index in inner_steps else targets[index]
        moves.append(transfer(kind, axis, sources[index], target).start())
    made = take(n_made)
    more = []
    for (kind, axis, source), target in zip(second, targets_second):
        source = made[source] if source >= 0 else later[-1 - source]
        more.append(transfer(kind, axis, source, target))
    passed = []
    for target in targets_forward:
        buffer = take(1)[0]
        passed.append((buffer, transfer("a2a", "dp", buffer, target)))
    for move in moves:
        if move.kind in SUMS:
            move.relay()
    extras = [index for index in inner_steps if index and index not in forwards]
    for index in extras:
        moves[index].finish()
    results, kept = middle(moves[0].total(), *[moves[index].target for index in extras], *given)
    for ref, value in zip(made, results):
        ref[...] = value
    for move in more:
        move.start()
    for ref, value in zip(local, kept):
        ref[...] = value
    for index, (buffer, move) in zip(forwards, passed):
        buffer[...] = moves[index].total().astype(BF)
        move.start()
    for move in more:
        if move.kind in SUMS:
            move.relay()
    for move in moves + more:
        move.relay()
    for move in moves + more + [move for _, move in passed]:
        move.finish()


def moved_shape(kind, size, shape):
    if kind in ("ag", "agh"):
        return (size,) + shape
    if kind == "agh1":
        return (shape[0], size) + shape[1:]
    if kind == "a2a1":
        return (size, shape[0]) + shape[2:]
    if kind == "sum":
        return (size // 2,) + shape[1:]
    if kind == "sum1":
        return (size // 2, shape[0]) + shape[2:]
    return shape


def chain(ident, first, middle, given, made, local, second, extras=(), forwards=()):
    sizes = {axis: lax.axis_size(axis) for axis in ("dp", "mp")}
    inner_steps = tuple(sorted({0} | set(extras) | set(forwards)))
    later = [source for _, _, source in second if not isinstance(source, int)]
    plan_second, seen = [], 0
    shapes, local_shapes, second_shapes, scratch = [], list(local), [], []

    def held(kind, axis, shape, dtype):
        scratch.extend(transfer_sems(sizes[axis]))
        if kind in SUMS:
            scratch.extend([pltpu.VMEM(shape, dtype)] * 2 + [DMA((sizes[axis] // 2,))])

    moved = 0
    for index, (kind, axis, array) in enumerate(first):
        shape = moved_shape(kind, sizes[axis], array.shape)
        moved += 2 * array.size
        if index in inner_steps:
            scratch.append(pltpu.VMEM(shape, array.dtype))
        else:
            shapes.append(jax.ShapeDtypeStruct(shape, array.dtype))
        held(kind, axis, shape, array.dtype)
    scratch.extend(pltpu.VMEM(item.shape, item.dtype) for item in made)
    for kind, axis, source in second:
        item = source
        if isinstance(source, int):
            item = made[source]
            plan_second.append((kind, axis, source))
        else:
            seen += 1
            plan_second.append((kind, axis, -seen))
        shape = moved_shape(kind, sizes[axis], item.shape)
        second_shapes.append(jax.ShapeDtypeStruct(shape, item.dtype))
        held(kind, axis, shape, item.dtype)
    forward_shapes = []
    for index in forwards:
        kind, axis, array = first[index]
        shape = moved_shape(kind, sizes[axis], array.shape)[1:]
        forward_shapes.append(jax.ShapeDtypeStruct(shape, BF))
        scratch.append(pltpu.VMEM(shape, BF))
        held("a2a", "dp", shape, BF)
    hbm, vmem = pl.BlockSpec(memory_space=pl.ANY), pl.BlockSpec(memory_space=pltpu.VMEM)
    return pl.pallas_call(
        functools.partial(
            chain_kernel,
            tuple((kind, axis) for kind, axis, _ in first),
            tuple(plan_second),
            inner_steps,
            tuple(forwards),
            middle,
            (len(given), len(later), len(local), len(made)),
            sizes,
        ),
        out_shape=shapes + local_shapes + second_shapes + forward_shapes,
        in_specs=[hbm] * len(first) + [vmem] * len(given) + [hbm] * len(later),
        out_specs=[hbm] * len(shapes)
        + [vmem] * len(local_shapes)
        + [hbm] * (len(second_shapes) + len(forward_shapes)),
        scratch_shapes=scratch,
        compiler_params=pltpu.CompilerParams(
            collective_id=ident, has_side_effects=True, vmem_limit_bytes=VMEM_LIMIT
        ),
        cost_estimate=pl.CostEstimate(flops=0, bytes_accessed=64 * moved, transcendentals=0),
    )(*[array for _, _, array in first], *given, *later)


def patch_in_kernel(
    sizes, grad_ref, w_ref, rows_ref, packed_ref, gains_ref, out_rows_ref, grad_w_ref, out_packed_ref, out_gains_ref,
    leaving, grads, mine, paired, came, *sems,
):
    axes = ("dp", "mp")
    arrivals = hail(axes, {axis: lax.axis_index(axis) for axis in axes}, sizes)
    leaving[...] = right_product(grad_ref[...], w_ref[...]).astype(BF).reshape(leaving.shape)
    pl.semaphore_wait(pltpu.get_barrier_semaphore(), arrivals)
    moves = [
        Transfer("a2a", "dp", sizes["dp"], leaving, out_rows_ref, sems[:3]).start(),
        Transfer("agh", "dp", sizes["dp"], packed_ref, out_packed_ref, sems[3:6]).start(),
        Transfer("agh", "dp", sizes["dp"], gains_ref, out_gains_ref, sems[6:9]).start(),
    ]
    grads[...] = left_product(rows_ref[...], grad_ref[...]).astype(BF).reshape(grads.shape)
    added = Transfer("sum", "mp", sizes["mp"], grads, came, sems[9:], (mine, paired, None)).start()
    added.relay()
    for move in moves:
        move.relay()
    grad_w_ref[...] = added.total()
    for move in moves:
        move.finish()


def patch_in_backward(ident, grad, w, patch_rows, packed, gains, patches):
    sizes = {axis: lax.axis_size(axis) for axis in ("dp", "mp")}
    byte_cols = w.shape[0]
    slots = (sizes["dp"], patches, byte_cols)
    share = (byte_cols // sizes["mp"], D)
    half = (sizes["mp"] // 2,) + share
    hbm, vmem = pl.BlockSpec(memory_space=pl.ANY), pl.BlockSpec(memory_space=pltpu.VMEM)
    return pl.pallas_call(
        functools.partial(patch_in_kernel, sizes),
        out_shape=[
            jax.ShapeDtypeStruct(slots, BF),
            jax.ShapeDtypeStruct(share, F32),
            jax.ShapeDtypeStruct((sizes["dp"],) + packed.shape, F32),
            jax.ShapeDtypeStruct((sizes["dp"],) + gains.shape, F32),
        ],
        in_specs=[vmem] * 3 + [hbm] * 2,
        out_specs=[hbm, vmem, hbm, hbm],
        scratch_shapes=[
            pltpu.VMEM(slots, BF),
            pltpu.VMEM((sizes["mp"],) + share, BF),
            pltpu.VMEM(half, BF),
            pltpu.VMEM(half, BF),
            pltpu.VMEM(half, BF),
        ]
        + transfer_sems(sizes["dp"]) * 3
        + transfer_sems(sizes["mp"]),
        compiler_params=pltpu.CompilerParams(
            collective_id=ident, has_side_effects=True, vmem_limit_bytes=VMEM_LIMIT
        ),
        cost_estimate=pl.CostEstimate(
            flops=4 * grad.size * byte_cols, bytes_accessed=64 * grad.size, transcendentals=0
        ),
    )(grad, w, patch_rows, packed, gains)


def norm_step(summed, gain_ref):
    return [root_norm(summed, gain_ref[...]).astype(BF)], [summed]


def mixed_step(summed, squares_ref, global_in_ref):
    squares = squares_ref[0]
    for index in range(1, squares_ref.shape[0]):
        squares = squares + squares_ref[index]
    scale = lax.rsqrt(squares / INNER + EPSILON)
    return [(global_in_ref[...] + scale[:, :1] * summed).astype(BF), scale], [summed]


def grad_mixed_step(summed, unscaled_ref):
    low = summed.astype(BF)
    along = jnp.sum(low.astype(F32) * unscaled_ref[...], axis=1, keepdims=True)
    return [low, jnp.broadcast_to(along, (along.shape[0], LANE))], [summed]


def grad_norm_step(summed, global_in_ref, gain_ref, grad_out_ref):
    grad, gains = norm_back(global_in_ref[...], gain_ref[...], summed)
    gains = jnp.sum(gains, axis=0, keepdims=True)
    return [(grad_out_ref[...] + grad).astype(BF), jnp.broadcast_to(gains, (8, D))], []


def attend_forward_kernel(
    global_ref,
    w_out_ref,
    inputs_ref,
    gain_ref,
    feed_gain_ref,
    w_ref,
    local_ref,
    low_ref,
    qkv_ref,
    attended_ref,
    after_ref,
    feed_ref,
    probs_ref,
    leaving_ref,
    slots_ref,
    chunks_ref,
    *sems,
):
    rows = local_ref.shape[0]
    step = min(rows, 256)
    n_dp, patches, byte_cols = slots_ref.shape
    arrivals = hail(("dp",), {"dp": lax.axis_index("dp")}, {"dp": n_dp})
    leaving_ref[...] = product(global_ref[...], w_out_ref[...]).astype(BF).reshape(slots_ref.shape)
    pl.semaphore_wait(pltpu.get_barrier_semaphore(), arrivals)
    Transfer("a2a", "dp", n_dp, leaving_ref, slots_ref, sems).start().finish()
    for byte in range(PATCH):
        for chunk in range(D // LANE):
            column = byte * D + chunk * LANE
            there = slice(column % byte_cols, column % byte_cols + LANE)
            chunks_ref[chunk, pl.ds(byte, patches, stride=PATCH), :] = slots_ref[
                column // byte_cols, :, there
            ].astype(F32)
    mask = patch_mask(LANE)
    first = lax.broadcasted_iota(jnp.int32, (LANE, LANE), 1) < HEAD_A

    def some(index, _):
        at = pl.ds(pl.multiple_of(index * step, step), step)
        chunks = [chunks_ref[chunk, at, :] for chunk in range(D // LANE)]
        local = inputs_ref[at, :].astype(F32) + jnp.concatenate(chunks, axis=1)
        local_ref[at, :] = local
        low = root_norm(local, gain_ref[...]).astype(BF)
        low_ref[at, :] = low
        qkv_ref[at, :] = product(low, w_ref[:, : 3 * D]).astype(BF)

        def heads(inner, _):
            within = pl.ds(pl.multiple_of(index * step + inner * LANE, LANE), LANE)
            pairs = range(D // LANE)
            scores = []
            for pair in pairs:
                query = qkv_ref[within, pair * LANE : (pair + 1) * LANE]
                keyed = qkv_ref[within, D + pair * LANE : D + (pair + 1) * LANE]
                for half in (first, ~first):
                    scores.append(right_product(jnp.where(half, query, 0), keyed))
            probs = []
            for head, score in enumerate(scores):
                probs.append(patch_probs(score, mask).astype(BF))
                probs_ref[head, within, :] = probs[head]
            for pair in pairs:
                valued = qkv_ref[within, 2 * D + pair * LANE : 2 * D + (pair + 1) * LANE]
                attended_ref[within, pair * LANE : (pair + 1) * LANE] = jnp.where(
                    first, product(probs[2 * pair], valued), product(probs[2 * pair + 1], valued)
                ).astype(BF)
            return 0

        lax.fori_loop(0, step // LANE, heads, 0)
        after = local + product(attended_ref[at, :], w_ref[:, 3 * D :])
        after_ref[at, :] = after
        feed_ref[at, :] = root_norm(after, feed_gain_ref[...]).astype(BF)
        return 0

    lax.fori_loop(0, rows // step, some, 0)


def patch_mask(count):
    row = lax.broadcasted_iota(jnp.int32, (count, count), 0)
    column = lax.broadcasted_iota(jnp.int32, (count, count), 1)
    return (row // PATCH == column // PATCH) & (column <= row)


def patch_probs(scores, mask):
    scores = jnp.where(mask, scores * HEAD_A ** (-0.5), -1e30)
    expo = jnp.exp(scores - jnp.max(scores, axis=-1, keepdims=True))
    return expo / jnp.sum(expo, axis=-1, keepdims=True)


def attend_forward(ident, global_low, w_patch_out, inputs_low, norm_attend, norm_feed, w_attend):
    rows = inputs_low.shape[0]
    n_dp = lax.axis_size("dp")
    slots = (n_dp, rows // PATCH, w_patch_out.shape[1])
    return pl.pallas_call(
        attend_forward_kernel,
        out_shape=[
            jax.ShapeDtypeStruct((rows, D), F32),
            jax.ShapeDtypeStruct((rows, D), BF),
            jax.ShapeDtypeStruct((rows, 3 * D), BF),
            jax.ShapeDtypeStruct((rows, D), BF),
            jax.ShapeDtypeStruct((rows, D), F32),
            jax.ShapeDtypeStruct((rows, D), BF),
            jax.ShapeDtypeStruct((HEADS_A, rows, LANE), BF),
        ],
        in_specs=[pl.BlockSpec(memory_space=pltpu.VMEM)] * 6,
        out_specs=[pl.BlockSpec(memory_space=pltpu.VMEM)] * 7,
        scratch_shapes=[
            pltpu.VMEM(slots, BF),
            pltpu.VMEM(slots, BF),
            pltpu.VMEM((D // LANE, rows, LANE), F32),
        ]
        + transfer_sems(n_dp),
        compiler_params=pltpu.CompilerParams(
            collective_id=ident, has_side_effects=True, vmem_limit_bytes=VMEM_LIMIT
        ),
        cost_estimate=pl.CostEstimate(
            flops=2 * rows * D * 4 * D, bytes_accessed=24 * D * D, transcendentals=rows * 16 * LANE
        ),
    )(global_low, w_patch_out, inputs_low, norm_attend[None], norm_feed[None], w_attend)


def norm_back(values, gain, grad):
    scale = lax.rsqrt(jnp.mean(values * values, axis=-1, keepdims=True) + EPSILON)
    scaled = grad * gain
    along = jnp.mean(scaled * values, axis=-1, keepdims=True)
    return scale * scaled - values * (scale * scale * scale * along), grad * values * scale


def attend_backward_kernel(
    grad_feed_ref,
    grad_final_ref,
    local_ref,
    after_ref,
    low_ref,
    qkv_ref,
    attended_ref,
    probs_ref,
    gain_ref,
    feed_gain_ref,
    w_ref,
    grad_local_ref,
    grad_slots_ref,
    grad_w_ref,
    grad_more_ref,
    grad_gain_ref,
    grad_feed_gain_ref,
    grads_ref,
    chunks_ref,
    slots_ref,
    *sems,
):
    rows = local_ref.shape[0]
    step = min(rows, 256)
    n_dp, _, byte_cols = grad_slots_ref.shape
    arrivals = hail(("dp",), {"dp": lax.axis_index("dp")}, {"dp": n_dp})
    first = lax.broadcasted_iota(jnp.int32, (LANE, LANE), 1) < HEAD_A
    grad_gain_ref[...] = jnp.zeros_like(grad_gain_ref)
    grad_feed_gain_ref[...] = jnp.zeros_like(grad_feed_gain_ref)

    def some(index, _):
        at = pl.ds(pl.multiple_of(index * step, step), step)
        grad_after, gains = norm_back(after_ref[at, :], feed_gain_ref[...], grad_feed_ref[at, :])
        grad_feed_gain_ref[...] += jnp.sum(gains, axis=0, keepdims=True)
        grad_after = grad_after + grad_final_ref[at, :].astype(F32)
        grad_low = grad_after.astype(BF)
        grads_ref[at, 3 * D :] = grad_low
        grad_attended = right_product(grad_low, w_ref[:, 3 * D :]).astype(BF)
        grads_ref[at, :D] = grad_attended

        def heads(inner, _):
            within = pl.ds(pl.multiple_of(index * step + inner * LANE, LANE), LANE)
            pairs = range(D // LANE)

            def part(number, pair):
                return slice(number * D + pair * LANE, number * D + (pair + 1) * LANE)

            given = [grads_ref[within, part(0, pair)] for pair in pairs]
            grad_probs = []
            for pair in pairs:
                for half in (first, ~first):
                    grad_probs.append(
                        right_product(jnp.where(half, given[pair], 0), qkv_ref[within, part(2, pair)])
                    )
            grad_scores = []
            for head, grad in enumerate(grad_probs):
                probs = probs_ref[head, within, :].astype(F32)
                inside = jnp.sum(grad * probs, axis=-1, keepdims=True)
                grad_scores.append((probs * (grad - inside) * HEAD_A ** (-0.5)).astype(BF))
            for pair in pairs:
                query, keyed = qkv_ref[within, part(0, pair)], qkv_ref[within, part(1, pair)]
                two = (2 * pair, 2 * pair + 1)
                results = (
                    [product(grad_scores[head], keyed) for head in two],
                    [left_product(grad_scores[head], query) for head in two],
                    [left_product(probs_ref[head, within, :], given[pair]) for head in two],
                )
                for number in range(3):
                    grads_ref[within, part(number, pair)] = jnp.where(first, *results[number]).astype(BF)
            return 0

        lax.fori_loop(0, step // LANE, heads, 0)
        grad_normed = right_product(grads_ref[at, : 3 * D], w_ref[:, : 3 * D])
        grad_local, gains = norm_back(local_ref[at, :], gain_ref[...], grad_normed)
        grad_gain_ref[...] += jnp.sum(gains, axis=0, keepdims=True)
        grad_local = grad_after + grad_local
        grad_local_ref[at, :] = grad_local
        for chunk in range(D // LANE):
            chunks_ref[chunk, at, :] = grad_local[:, chunk * LANE : (chunk + 1) * LANE]
        return 0

    lax.fori_loop(0, rows // step, some, 0)
    for byte in range(PATCH):
        for chunk in range(D // LANE):
            slots_ref[byte, :, chunk * LANE : (chunk + 1) * LANE] = chunks_ref[
                chunk, pl.ds(byte, rows // PATCH, stride=PATCH), :
            ].astype(BF)
    shares = D // byte_cols

    def slot(peer):
        if shares == 1:
            return slots_ref.at[peer]
        column = pl.multiple_of(lax.rem(peer, shares) * byte_cols, byte_cols)
        return slots_ref.at[peer // shares, :, pl.ds(column, byte_cols)]

    pl.semaphore_wait(pltpu.get_barrier_semaphore(), arrivals)
    move = Transfer("a2a", "dp", n_dp, slot, grad_slots_ref, sems).start()

    n_mp, _, k_rows, _ = grad_w_ref.shape
    each = 256 // (n_mp * k_rows)

    def columns(index, _):
        at = pl.ds(pl.multiple_of(index * 256, 256), 256)
        for source, number, there in (
            (low_ref, 0, slice(0, 2 * D)),
            (low_ref, 2, slice(0, D)),
            (attended_ref, 3, slice(D, 2 * D)),
        ):
            width = there.stop - there.start
            target = grad_w_ref if number == 0 else grad_more_ref
            grad = left_product(source[:, at], grads_ref[:, number * D : number * D + width])
            grad = grad.astype(BF)
            for place in range(each):
                for owner in range(n_mp):
                    start = (place * n_mp + owner) * k_rows
                    target[owner, index * each + place, :, there] = grad[start : start + k_rows]
        return 0

    lax.fori_loop(0, D // 256, columns, 0)
    move.finish()


def attend_backward(ident, grad_feed, grad_final, local_in, after, low, qkv, attended, probs, gain, feed_gain, w):
    rows = local_in.shape[0]
    n_dp, n_mp = lax.axis_size("dp"), lax.axis_size("mp")
    vmem = pl.BlockSpec(memory_space=pltpu.VMEM)
    return pl.pallas_call(
        attend_backward_kernel,
        out_shape=[
            jax.ShapeDtypeStruct((rows, D), F32),
            jax.ShapeDtypeStruct((n_dp, rows // PATCH, PATCH * D // n_dp), BF),
            jax.ShapeDtypeStruct((n_mp, n_dp, D // (n_dp * n_mp), 2 * D), BF),
            jax.ShapeDtypeStruct((n_mp, n_dp, D // (n_dp * n_mp), 2 * D), BF),
            jax.ShapeDtypeStruct((1, D), F32),
            jax.ShapeDtypeStruct((1, D), F32),
        ],
        in_specs=[vmem] * 11,
        out_specs=[vmem, pl.BlockSpec(memory_space=pl.ANY)] + [vmem] * 4,
        scratch_shapes=[
            pltpu.VMEM((rows, 4 * D), BF),
            pltpu.VMEM((D // LANE, rows, LANE), F32),
            pltpu.VMEM((PATCH, rows // PATCH, D), BF),
        ]
        + transfer_sems(n_dp),
        compiler_params=pltpu.CompilerParams(
            collective_id=ident, has_side_effects=True, vmem_limit_bytes=VMEM_LIMIT
        ),
        cost_estimate=pl.CostEstimate(
            flops=4 * rows * D * 4 * D, bytes_accessed=40 * D * D, transcendentals=rows * 16 * LANE
        ),
    )(grad_feed, grad_final, local_in, after, low, qkv, attended, probs, gain[None], feed_gain[None], w)


def feed_kernel(
    n_mp,
    x_ref,
    c_ref,
    w_ref,
    out_ref,
    grad_feed_ref,
    grads_ref,
    held,
    hidden,
    grad_gate,
    grad_up,
    grad_held,
    paired,
    arrived,
    staged,
    own_sem,
    stage_sems,
    ag_send,
    ag_recv,
    pair_send,
    pair_recv,
    far_send,
    far_recv,
):
    rows = x_ref.shape[0]
    chips = n_mp // 2
    units = w_ref.shape[-1]
    here = lax.axis_index("mp")
    core = lax.rem(here, 2)
    twin = here + 1 - 2 * core
    pieces = 2
    size = rows // pieces
    greet(("mp",), {"mp": here}, {"mp": n_mp})

    def block(owner):
        return pl.ds(pl.multiple_of(owner * rows, rows), rows)

    def part(owner, piece):
        return pl.ds(pl.multiple_of(owner * rows + piece * size, size), size)

    def remote(source, target, send, recv, peer):
        copy = pltpu.make_async_remote_copy(
            src_ref=source,
            dst_ref=target,
            send_sem=send,
            recv_sem=recv,
            device_id={"mp": peer},
            device_id_type=MESH,
        )
        copy.start()
        return copy

    own = pltpu.make_async_copy(x_ref, held.at[block(here)], own_sem)
    own.start()
    far = [lax.rem(here + 2 * k, n_mp) for k in range(chips)]
    came = [lax.rem(here + n_mp - 2 * k, n_mp) for k in range(chips)]
    direct = {}
    near = remote(x_ref, held.at[block(here)], ag_send.at[0, 0], ag_recv.at[0, 0], twin)
    for piece in range(pieces):
        for k in range(1, chips):
            direct[k, piece] = remote(
                x_ref.at[part(0, piece)],
                held.at[part(here, piece)],
                ag_send.at[k, piece],
                ag_recv.at[k, piece],
                far[k],
            )

    def weight(number):
        return w_ref[:, number].reshape(D, units)

    stored, relays, pairs, sends = [], {}, {}, {}

    def work(owner, piece):
        number = len(stored)
        slot = number % 2
        if number >= 2:
            stored[number - 2].wait()
        at = part(owner, piece)
        x = held[at, :]
        gate = product(x, weight(0))
        up = product(x, weight(1))
        sigmoid = jax.nn.sigmoid(gate)
        silu = gate * sigmoid
        low = (silu * up).astype(BF)
        hidden[at, :] = low
        grad_hidden = product(c_ref[at, :], weight(2))
        gate_low = (grad_hidden * up * sigmoid * (1.0 + gate * (1.0 - sigmoid))).astype(BF)
        up_low = (grad_hidden * silu).astype(BF)
        grad_gate[at, :] = gate_low
        grad_up[at, :] = up_low
        staged[slot] = right_product(low, weight(2)).astype(BF)
        grad_held[at, :] = (
            right_product(gate_low, weight(0)) + right_product(up_low, weight(1))
        ).astype(BF)
        copy = pltpu.make_async_copy(staged.at[slot], out_ref.at[at], stage_sems.at[number])
        copy.start()
        stored.append(copy)

    def relay(k, piece):
        direct[k, piece].wait_recv()
        at = part(came[k], piece)
        relays[k, piece] = remote(
            held.at[at], held.at[at], ag_send.at[chips - 1 + k, piece], ag_recv.at[chips - 1 + k, piece], twin
        )

    def other(k):
        return came[k] + 1 - 2 * core

    def to_twin(k, piece):
        pairs[k, piece] = remote(
            grad_held.at[part(other(k), piece)],
            paired.at[k, part(0, piece)],
            pair_send.at[k, piece],
            pair_recv.at[k, piece],
            twin,
        )

    def onward(k, piece):
        pairs[k, piece].wait_recv()
        at = part(came[k], piece)
        both = grad_held[at, :].astype(F32) + paired[k, part(0, piece), :].astype(F32)
        grad_held[at, :] = both.astype(BF)
        if k:
            sends[k, piece] = remote(
                grad_held.at[at],
                arrived.at[k - 1, part(0, piece)],
                far_send.at[k - 1, piece],
                far_recv.at[k - 1, piece],
                came[k],
            )

    own.wait()
    for piece in range(pieces):
        work(here, piece)
    near.wait_recv()
    for piece in range(pieces):
        for k in range(1, chips):
            relay(k, piece)
        work(twin, piece)
        to_twin(0, piece)
        for k in range(1, chips):
            if piece:
                onward(k, piece - 1)
            relays[k, piece].wait_recv()
            work(other(k), piece)
            to_twin(k, piece)
            work(came[k], piece)

    def tiles(start, stop):
        def some(index, _):
            at = pl.ds(pl.multiple_of(index * LANE, LANE), LANE)
            x = held[:, at]
            each = grads_ref.shape[2]
            owners = pl.ds(index * (LANE // each), LANE // each)

            def store(number, value):
                grads_ref[owners, number] = value.astype(BF).reshape(LANE // each, each, units)

            store(0, left_product(x, grad_gate[...]))
            store(1, left_product(x, grad_up[...]))
            store(2, left_product(c_ref[:, at], hidden[...]))
            return 0

        lax.fori_loop(start, stop, some, 0)

    for k in range(1, chips):
        onward(k, pieces - 1)
    count = D // LANE
    tiles(0, count)
    for piece in range(pieces):
        onward(0, piece)
    total_here = grad_held[block(here), :].astype(F32)
    for k in range(1, chips):
        for piece in range(pieces):
            sends[k, piece].wait_recv()
        total_here = total_here + arrived[k - 1].astype(F32)
    grad_feed_ref[...] = total_here
    near.wait_send()
    for group in (direct, relays, pairs, sends):
        for copy in group.values():
            copy.wait_send()
    for copy in stored[-2:]:
        copy.wait()


def feed_section(ident, feed_low, grad_rows, weights):
    n_mp = lax.axis_size("mp")
    rows = feed_low.shape[0]
    every = rows * n_mp
    chips = n_mp // 2
    units = weights.shape[-1]
    dma = pltpu.SemaphoreType.DMA
    vmem = pl.BlockSpec(memory_space=pltpu.VMEM)
    return pl.pallas_call(
        functools.partial(feed_kernel, n_mp),
        out_shape=[
            jax.ShapeDtypeStruct((every, D), BF),
            jax.ShapeDtypeStruct((rows, D), F32),
            jax.ShapeDtypeStruct(weights.shape, BF),
        ],
        in_specs=[vmem] * 3,
        out_specs=[pl.BlockSpec(memory_space=pl.ANY), vmem, vmem],
        scratch_shapes=[
            pltpu.VMEM((every, D), BF),
            pltpu.VMEM((every, units), BF),
            pltpu.VMEM((every, units), BF),
            pltpu.VMEM((every, units), BF),
            pltpu.VMEM((every, D), BF),
            pltpu.VMEM((chips, rows, D), BF),
            pltpu.VMEM((chips - 1, rows, D), BF),
            pltpu.VMEM((2, rows // 2, D), BF),
            dma,
            dma((2 * n_mp,)),
            dma((n_mp - 1, 2)),
            dma((n_mp - 1, 2)),
            dma((chips, 2)),
            dma((chips, 2)),
            dma((chips - 1, 2)),
            dma((chips - 1, 2)),
        ],
        compiler_params=pltpu.CompilerParams(
            collective_id=ident, has_side_effects=True, vmem_limit_bytes=VMEM_LIMIT
        ),
        cost_estimate=pl.CostEstimate(
            flops=18 * every * D * units, bytes_accessed=30 * D * D, transcendentals=every * units
        ),
    )(feed_low, grad_rows, weights)


def product(left, right):
    return jnp.dot(left, right, preferred_element_type=F32)


def left_product(left, right):
    return lax.dot_general(left, right, (((0,), (0,)), ((), ())), preferred_element_type=F32)


def right_product(left, right):
    return lax.dot_general(left, right, (((1,), (1,)), ((), ())), preferred_element_type=F32)


def total(parts):
    return jnp.sum(parts.astype(F32), axis=0)


def root_norm(values, gain):
    return values * lax.rsqrt(jnp.mean(values * values, axis=-1, keepdims=True) + EPSILON) * gain


def shifted(values, steps):
    if steps == 0:
        return values
    row = lax.broadcasted_iota(jnp.int32, values.shape, 0)
    return jnp.where(row >= steps, pltpu.roll(values, steps, 0), 0.0)


def lifted(values, steps):
    if steps == 0:
        return values
    count = values.shape[0]
    row = lax.broadcasted_iota(jnp.int32, values.shape, 0)
    return jnp.where(row < count - steps, pltpu.roll(values, count - steps, 0), 0.0)


def running(values, move):
    steps = 1
    while steps < values.shape[0]:
        values = values + move(values, steps)
        steps *= 2
    return values


def softplus(values):
    return jnp.maximum(values, 0.0) + jnp.log1p(jnp.exp(-jnp.abs(values)))


class Mixer:
    def __init__(self, projected, inner, conv_weight, conv_bias, step_bias, decay_rate):
        self.inner = inner
        self.count = projected.shape[0]
        self.width = min(inner, LANE)
        self.per_group = self.width // HEAD_M
        self.tile = min(self.count, 256)
        edge = 2 * inner + 2 * STATE
        self.conv_input = projected[:, inner:edge]
        self.conv_weight = conv_weight
        summed = conv_bias + conv_weight[CONV - 1 : CONV] * self.conv_input
        for shift in range(1, CONV):
            row = CONV - 1 - shift
            summed = summed + conv_weight[row : row + 1] * shifted(self.conv_input, shift)
        self.sigmoid = jax.nn.sigmoid(summed)
        self.summed = summed
        self.activated = summed * self.sigmoid
        self.raw = projected[:, edge:] + step_bias
        self.step = softplus(self.raw)
        self.rate = jnp.exp(decay_rate)
        self.log_decay = running(self.step * -self.rate, shifted)
        self.log_decay_t = self.log_decay.T
        self.step_t = self.step.T
        low = self.activated.astype(BF)
        self.heads_low = low[:, :inner]
        self.input_low = low[:, inner : inner + STATE]
        self.output_low = low[:, inner + STATE :]
        lane = lax.broadcasted_iota(jnp.int32, (1, self.width), 1)
        self.lanes = [lane // HEAD_M == h for h in range(self.per_group)]

    def tiles(self):
        for start in range(0, self.count, self.tile):
            stop = start + self.tile
            scores = right_product(self.output_low[start:stop], self.input_low[:stop])
            row = lax.broadcasted_iota(jnp.int32, scores.shape, 0) + start
            causal = row >= lax.broadcasted_iota(jnp.int32, scores.shape, 1)
            yield start, stop, scores, causal

    def factor(self, head, start, stop, causal):
        spread = self.log_decay[start:stop, head : head + 1] - self.log_decay_t[head : head + 1, :stop]
        return jnp.exp(jnp.where(causal, spread, -1e30))

    def groups(self):
        return range(self.inner // self.width)

    def merged(self, parts):
        if len(parts) == 1:
            return parts[0]
        return jnp.where(self.lanes[0], parts[0], parts[1])


def mixer_forward_kernel(
    inner, normed_ref, w_ref, w_out_ref, conv_weight_ref, conv_bias_ref, step_bias_ref, decay_ref, skip_ref, gain_ref,
    projected_ref, values_ref, parts_ref, squares_ref,
):
    projected_ref[...] = product(normed_ref[...], w_ref[...])
    mixer = Mixer(
        projected_ref[...], inner, conv_weight_ref[...], conv_bias_ref[...], step_bias_ref[...], decay_ref[...]
    )
    for start, stop, scores, causal in mixer.tiles():
        for group in mixer.groups():
            at = slice(group * mixer.width, (group + 1) * mixer.width)
            parts = []
            for h in range(mixer.per_group):
                head = group * mixer.per_group + h
                weights = (
                    mixer.factor(head, start, stop, causal) * scores * mixer.step_t[head : head + 1, :stop]
                )
                parts.append(product(weights.astype(BF), mixer.heads_low[:stop, at]))
            values_ref[start:stop, at] = (
                mixer.merged(parts) + skip_ref[:, at] * mixer.activated[start:stop, at]
            )
    gate = projected_ref[:, :inner]
    gated = values_ref[...] * (gate * jax.nn.sigmoid(gate))
    squares = jnp.sum(gated * gated, axis=1, keepdims=True)
    squares_ref[...] = jnp.broadcast_to(squares, squares_ref.shape)
    parts_ref[...] = product((gated * gain_ref[...]).astype(BF), w_out_ref[...]).astype(BF)


def mixer_backward_kernel(
    inner,
    grad_ref,
    scales_ref,
    alongs_ref,
    normed_ref,
    projected_ref,
    values_ref,
    w_ref,
    w_out_ref,
    conv_weight_ref,
    conv_bias_ref,
    step_bias_ref,
    decay_ref,
    skip_ref,
    gain_ref,
    parts_ref,
    grad_w_ref,
    grad_w_out_ref,
    grad_conv_weight_ref,
    grad_conv_bias_ref,
    grad_heads_ref,
    grad_skip_ref,
    grad_gain_ref,
    grad_act_ref,
    columns_ref,
    grads_ref,
):
    mixer = Mixer(
        projected_ref[...], inner, conv_weight_ref[...], conv_bias_ref[...], step_bias_ref[...], decay_ref[...]
    )
    count = mixer.count
    edge = 2 * inner + 2 * STATE
    gate = projected_ref[:, :inner]
    sigmoid = jax.nn.sigmoid(gate)
    silu = gate * sigmoid
    values = values_ref[...]
    gated = values * silu
    scales = scales_ref[:, :1]
    grad = grad_ref[...]
    grad_w_out_ref[...] = left_product((gated * scales * gain_ref[...]).astype(BF), grad).astype(BF)
    grad_mixed = right_product(grad, w_out_ref[...])
    grad_gain_ref[...] = jnp.sum(grad_mixed * gated * scales, axis=0, keepdims=True)
    grad_gated = scales * gain_ref[...] * grad_mixed - gated * (scales**3 * alongs_ref[:, :1] / INNER)
    grad_values = grad_gated * silu
    grads_ref[:, :inner] = (grad_gated * values * (sigmoid * (1.0 + gate * (1.0 - sigmoid)))).astype(BF)
    heads_x = mixer.activated[:, :inner]
    grad_skip_ref[...] = jnp.sum(grad_values * heads_x, axis=0, keepdims=True)
    grad_act_ref[:, :inner] = grad_values * skip_ref[...]
    grad_act_ref[:, inner:] = jnp.zeros((count, 2 * STATE), F32)
    columns_ref[...] = jnp.zeros_like(columns_ref)
    grad_low = grad_values.astype(BF)
    lane = lax.broadcasted_iota(jnp.int32, (mixer.tile, LANE), 1)
    grad_decays = []
    for start, stop, scores, causal in mixer.tiles():
        grad_scores = jnp.zeros_like(scores)
        grad_decay = jnp.zeros((mixer.tile, LANE), F32)
        for group in mixer.groups():
            at = slice(group * mixer.width, (group + 1) * mixer.width)
            grad_group = grad_low[start:stop, at]
            parts = []
            for h in range(mixer.per_group):
                head = group * mixer.per_group + h
                row = slice(head, head + 1)
                factor = mixer.factor(head, start, stop, causal)
                step = mixer.step_t[row, :stop]
                unstepped = factor * scores
                grad_weights = right_product(
                    jnp.where(mixer.lanes[h], grad_group, 0), mixer.heads_low[:stop, at]
                )
                parts.append(left_product((unstepped * step).astype(BF), grad_group))
                grad_scores = grad_scores + grad_weights * factor * step
                grad_unstepped = grad_weights * unstepped
                columns_ref[row, :stop] += jnp.sum(grad_unstepped, axis=0, keepdims=True)
                summed = jnp.sum(grad_unstepped * step, axis=1, keepdims=True)
                grad_decay = jnp.where(lane == head, summed, grad_decay)
            grad_act_ref[:stop, at] += mixer.merged(parts)
        grad_decays.append(grad_decay)
        low = grad_scores.astype(BF)
        grad_act_ref[:stop, inner : inner + STATE] += left_product(low, mixer.output_low[start:stop])
        grad_act_ref[start:stop, inner + STATE :] += product(low, mixer.input_low[:stop])
    columns = columns_ref[...].T
    grad_decay = jnp.concatenate(grad_decays, axis=0) - mixer.step * columns
    onward = running(grad_decay, lifted)
    grad_step = columns - onward * mixer.rate
    grad_raw = grad_step * jax.nn.sigmoid(mixer.raw)
    grads_ref[:, edge:] = grad_raw.astype(BF)
    grad_heads_ref[0:1] = jnp.sum(grad_raw, axis=0, keepdims=True)
    grad_heads_ref[1:2] = -jnp.sum(onward * mixer.step, axis=0, keepdims=True) * mixer.rate
    grad_summed = grad_act_ref[...] * (mixer.sigmoid * (1.0 + mixer.summed * (1.0 - mixer.sigmoid)))
    grad_conv_bias_ref[...] = jnp.sum(grad_summed, axis=0, keepdims=True)
    grad_conv = jnp.zeros_like(grad_summed)
    for shift in range(CONV):
        row = slice(CONV - 1 - shift, CONV - shift)
        grad_conv = grad_conv + conv_weight_ref[row] * lifted(grad_summed, shift)
        grad_conv_weight_ref[row] = jnp.sum(
            grad_summed * shifted(mixer.conv_input, shift), axis=0, keepdims=True
        )
    grads_ref[:, inner:edge] = grad_conv.astype(BF)
    parts_ref[...] = right_product(grads_ref[...], w_ref[...]).astype(BF)
    grad_w_ref[...] = left_product(normed_ref[...], grads_ref[...]).astype(BF)


def whole_kernel(kernel, shapes, operands, scratch=(), flops=0):
    vmem = pl.BlockSpec(memory_space=pltpu.VMEM)
    moved = sum(x.size * x.dtype.itemsize for x in list(operands) + list(shapes))
    return pl.pallas_call(
        kernel,
        out_shape=shapes,
        in_specs=[vmem] * len(operands),
        out_specs=[vmem] * len(shapes),
        scratch_shapes=list(scratch),
        compiler_params=pltpu.CompilerParams(vmem_limit_bytes=VMEM_LIMIT),
        cost_estimate=pl.CostEstimate(flops=flops, bytes_accessed=3 * moved, transcendentals=0),
    )(*operands)


def own_columns(array, place, width):
    return lax.dynamic_slice_in_dim(array, place * width, width, axis=-1)


def tucked(row):
    return jnp.pad(row[:, None, :], ((0, 0), (0, 7), (0, -row.shape[1] % LANE)))


def body(
    byte_embeds,
    lengths,
    patch_in,
    mixer_in,
    mixer_out,
    patch_out,
    attend_in,
    attend_out,
    gate_weight,
    up_weight,
    down_weight,
    norm_global,
    conv_weight,
    conv_bias,
    step_bias,
    decay_rate,
    skip_gain,
    norm_gated,
    norm_attend,
    norm_feed,
    cotangent,
):
    n_dp, n_mp = lax.axis_size("dp"), lax.axis_size("mp")
    devices = n_dp * n_mp
    rows = byte_embeds.shape[1]
    patches = rows // PATCH
    count = patches * n_dp
    group = lax.axis_index("mp")
    place = lax.axis_index("dp")
    length = jnp.sum(jnp.where(jnp.arange(lengths.shape[0], dtype=jnp.int32) == group, lengths, 0))
    position = place * rows + jnp.arange(rows, dtype=jnp.int32)
    keep = (position < length).astype(F32)[:, None]
    inputs = byte_embeds[0].astype(F32) * keep

    heads = HEADS_M // n_dp
    inner = heads * HEAD_M
    byte_cols = PATCH * D // n_dp
    k_rows = D // devices
    step_pad = -heads % LANE
    cols = 2 * inner + 2 * STATE + heads + step_pad

    w_attend = lax.all_gather(
        jnp.concatenate([attend_in.reshape(k_rows, -1), attend_out.reshape(k_rows, -1)], axis=1),
        ("dp", "mp"),
        axis=0,
        tiled=True,
    )
    w_feed = lax.all_gather(jnp.stack([gate_weight, up_weight, down_weight.T]), "dp", axis=0)
    grad_final = (cotangent[0].astype(F32) * keep).astype(BF)

    mixer_rows = mixer_in.reshape(k_rows, PROJ)
    shared = mixer_rows[:, 2 * INNER : 2 * INNER + 2 * STATE]
    by_part = jnp.concatenate(
        [
            mixer_rows[:, :INNER].reshape(k_rows, n_dp, inner),
            mixer_rows[:, INNER : 2 * INNER].reshape(k_rows, n_dp, inner),
            jnp.broadcast_to(shared[:, None], (k_rows, n_dp, 2 * STATE)),
            mixer_rows[:, 2 * INNER + 2 * STATE :].reshape(k_rows, n_dp, heads),
            jnp.zeros((k_rows, n_dp, step_pad), BF),
        ],
        axis=2,
    ).transpose(1, 0, 2)
    out_by_part = patch_out.reshape(k_rows, n_dp, byte_cols).transpose(1, 0, 2)
    patch_rows = inputs.astype(BF).reshape(patches, n_dp, byte_cols).transpose(1, 0, 2)
    patch_rows, mixer_cols, w_patch_in = exchange(
        0,
        ("a2a", "dp", patch_rows),
        ("a2a", "dp", by_part),
        ("agh", "mp", patch_in.reshape(-1, D)),
    )
    patch_rows = patch_rows.reshape(count, byte_cols)
    w_patch_in = w_patch_in.reshape(byte_cols, D)
    parts = product(patch_rows, w_patch_in).reshape(n_dp, patches, D)
    row, lanes = jax.ShapeDtypeStruct((patches, D), F32), jax.ShapeDtypeStruct((patches, LANE), F32)
    row_low = jax.ShapeDtypeStruct((patches, D), BF)
    mixer_cols, global_in, normed, out_cols, w_mixer_out = chain(
        1,
        [("sum", "dp", parts), ("agh1", "mp", mixer_cols)],
        norm_step,
        [norm_global[None]],
        [row_low],
        [row],
        [("agh", "dp", 0), ("a2a", "dp", out_by_part), ("agh", "mp", mixer_out.reshape(-1, D))],
    )
    w_mixer_in = mixer_cols.reshape(D, cols)
    w_mixer_out = w_mixer_out.reshape(inner, D)
    normed = normed.reshape(count, D)

    def own_conv(array):
        return jnp.concatenate(
            [own_columns(array[..., :INNER], place, inner), array[..., INNER:]], axis=-1
        )

    def own_heads(array):
        return jnp.pad(own_columns(array, place, heads), (0, step_pad))[None]

    own_gain = own_columns(norm_gated, place, inner)[None]
    mixer_params = (
        own_conv(conv_weight),
        own_conv(conv_bias)[None],
        own_heads(step_bias),
        own_heads(decay_rate),
        jnp.repeat(own_columns(skip_gain, place, heads), HEAD_M)[None],
        own_gain,
    )
    projected, values, parts, squares = whole_kernel(
        functools.partial(mixer_forward_kernel, inner),
        [
            jax.ShapeDtypeStruct((count, cols), F32),
            jax.ShapeDtypeStruct((count, inner), F32),
            jax.ShapeDtypeStruct((count, D), BF),
            jax.ShapeDtypeStruct((count, LANE), F32),
        ],
        (normed, w_mixer_in, w_mixer_out) + mixer_params,
        flops=2 * count * D * (cols + inner),
    )
    out_cols, grad_feed_rows, unscaled, global_low, scales = chain(
        3,
        [
            ("sum", "dp", parts.reshape(n_dp, patches, D)),
            ("a2a", "dp", squares.reshape(n_dp, patches, LANE)),
            ("agh1", "mp", out_cols),
            ("agh", "mp", grad_final),
        ],
        mixed_step,
        [global_in],
        [row_low, lanes],
        [row],
        [("agh", "dp", 0), ("agh", "dp", 1)],
        extras=(1,),
    )
    w_patch_out = out_cols.reshape(D, byte_cols)
    global_low = global_low.reshape(count, D)
    scales = scales.reshape(count, LANE)

    local_in, attend_low, qkv, attended_low, after_attend, feed_low, probs = attend_forward(
        5, global_low, w_patch_out, inputs.astype(BF), norm_attend, norm_feed, w_attend
    )
    feed_parts, grad_feed_normed, grad_feed = feed_section(
        12, feed_low, grad_feed_rows.reshape(-1, D), w_feed
    )
    units = grad_feed.shape[-1]
    grad_feed = lax.psum_scatter(
        grad_feed.reshape(3 * D, units), "dp", scatter_dimension=0, tiled=True
    ).astype(F32)
    grad_gate, grad_up, grad_down = grad_feed.reshape(3, D // n_dp, units)
    grad_down = grad_down.T
    grad_local, grad_slots, grad_attend, grad_more, grad_norm_attend, grad_norm_feed = attend_backward(
        6,
        grad_feed_normed,
        grad_final,
        local_in,
        after_attend,
        attend_low,
        qkv,
        attended_low,
        probs,
        norm_attend,
        norm_feed,
        w_attend,
    )
    grad_norm_attend, grad_norm_feed = grad_norm_attend[0], grad_norm_feed[0]

    def owners(grad):
        return grad.astype(BF).reshape(n_dp, n_mp, -1, grad.shape[-1])

    grad_slots = grad_slots.reshape(count, byte_cols)
    grad_patch_out = owners(left_product(global_low, grad_slots))
    parts = right_product(grad_slots, w_patch_out).astype(BF).reshape(n_dp, patches, D)
    grad_attend, grad_more, grad_global_out, grad_mixer_low, alongs, grad_patch_out = chain(
        7,
        [
            ("sum", "dp", parts),
            ("sum1", "mp", grad_patch_out),
            ("sum", "mp", grad_attend),
            ("sum", "mp", grad_more),
        ],
        grad_mixed_step,
        [unscaled],
        [row_low, lanes],
        [row],
        [("agh", "dp", 0), ("agh", "dp", 1)],
        forwards=(1,),
    )
    grad_mixer_low = grad_mixer_low.reshape(count, D)
    alongs = alongs.reshape(count, LANE)
    conv_cols = inner + 2 * STATE
    (
        parts,
        grad_mixer_in,
        grad_mixer_out,
        grad_conv_weight,
        grad_conv_bias,
        grad_heads,
        grad_skip,
        grad_norm_gated,
    ) = whole_kernel(
        functools.partial(mixer_backward_kernel, inner),
        [
            jax.ShapeDtypeStruct((count, D), BF),
            jax.ShapeDtypeStruct((D, cols), BF),
            jax.ShapeDtypeStruct((inner, D), BF),
            jax.ShapeDtypeStruct((CONV, conv_cols), F32),
            jax.ShapeDtypeStruct((1, conv_cols), F32),
            jax.ShapeDtypeStruct((2, heads + step_pad), F32),
            jax.ShapeDtypeStruct((1, inner), F32),
            jax.ShapeDtypeStruct((1, inner), F32),
        ],
        (grad_mixer_low, scales, alongs, normed, projected, values, w_mixer_in, w_mixer_out)
        + mixer_params,
        scratch=(
            pltpu.VMEM((count, conv_cols), F32),
            pltpu.VMEM((LANE, count), F32),
            pltpu.VMEM((count, cols), BF),
        ),
        flops=4 * count * D * (cols + inner),
    )
    grad_conv_bias, grad_norm_gated = grad_conv_bias[0], grad_norm_gated[0]
    grad_step_bias, grad_decay_rate = grad_heads[0, :heads], grad_heads[1, :heads]
    grad_skip_gain = jnp.sum(grad_skip.reshape(heads, HEAD_M), axis=1)
    parts = parts.reshape(n_dp, patches, D)
    grad_mixer_in = owners(grad_mixer_in)
    def all_columns(part, whole):
        return lax.dynamic_update_slice_in_dim(
            jnp.zeros(part.shape[:-1] + (whole,), F32), part, place * part.shape[-1], axis=-1
        )

    small = [
        jnp.concatenate(
            [all_columns(grad_conv_weight[:, :inner], INNER), grad_conv_weight[:, inner:]], axis=1
        ),
        jnp.concatenate([all_columns(grad_conv_bias[:inner], INNER), grad_conv_bias[inner:]]),
        all_columns(grad_step_bias, HEADS_M),
        all_columns(grad_decay_rate, HEADS_M),
        all_columns(grad_skip_gain, HEADS_M),
        all_columns(grad_norm_gated, INNER),
        grad_norm_attend,
        grad_norm_feed,
    ]
    packed = jnp.concatenate([part.reshape(-1) for part in small])
    packed = jnp.pad(packed, (0, -packed.shape[0] % (8 * LANE))).reshape(-1, LANE)
    grad_mixer_out, feed_parts, grad_attend, packed, grad_global_low, gains, grad_more, grad_mixer_in = chain(
        9,
        [
            ("sum", "dp", parts),
            ("sum1", "mp", grad_mixer_in),
            ("sum", "mp", grad_mixer_out.reshape(n_mp, -1, D)),
            ("sum", "mp", feed_parts.reshape(n_mp, rows, D)),
            ("sum", "dp", total(grad_attend).astype(BF)),
            ("agh", "mp", packed),
        ],
        grad_norm_step,
        [global_in, norm_global[None], grad_global_out],
        [row_low, jax.ShapeDtypeStruct((8, D), F32)],
        [],
        [("agh", "dp", 0), ("agh", "mp", 1), ("sum", "dp", total(grad_more).astype(BF))],
        forwards=(1,),
    )
    grad_mixer_out = total(grad_mixer_out).reshape(-1)
    grad_attend, grad_more = total(grad_attend), total(grad_more)
    grad_global_low = grad_global_low.reshape(count, D)
    grad_patch_rows, grad_patch_in, packed, gains = patch_in_backward(
        11, grad_global_low, w_patch_in, patch_rows, total(packed), total(gains), patches
    )
    grad_patch_in = grad_patch_in.reshape(-1)
    grad_patch_rows = grad_patch_rows.astype(F32).transpose(1, 0, 2).reshape(rows, D)
    grad_bytes = ((grad_local + grad_patch_rows) * keep).astype(BF)[None]
    out_bytes = ((after_attend + total(feed_parts)) * keep).astype(BF)[None]
    grad_patch_out = grad_patch_out.astype(F32).transpose(1, 0, 2).reshape(-1)
    grad_mixer_in = grad_mixer_in.astype(F32).transpose(1, 0, 2)
    edges = (inner, 2 * inner, 2 * inner + 2 * STATE, 2 * inner + 2 * STATE + heads)
    grad_mixer_in = jnp.concatenate(
        [
            grad_mixer_in[:, :, : edges[0]].reshape(k_rows, INNER),
            grad_mixer_in[:, :, edges[0] : edges[1]].reshape(k_rows, INNER),
            jnp.sum(grad_mixer_in[:, :, edges[1] : edges[2]], axis=1),
            grad_mixer_in[:, :, edges[2] : edges[3]].reshape(k_rows, HEADS_M),
        ],
        axis=1,
    ).reshape(-1)
    packed = total(packed).reshape(-1)
    summed, start = [], 0
    for part in small:
        summed.append(packed[start : start + part.size].reshape(part.shape))
        start += part.size
    return (
        out_bytes,
        grad_bytes,
        grad_patch_in,
        grad_mixer_in,
        grad_mixer_out,
        grad_patch_out,
        jnp.concatenate([grad_attend, grad_more[:, :D]], axis=1).reshape(-1),
        grad_more[:, D:].reshape(-1),
        grad_gate,
        grad_up,
        grad_down,
        total(gains)[0],
        *summed,
    )


def solution(mesh):
    flat = P(("dp", "mp"))
    split = P("mp", "dp", None)
    return jax.shard_map(
        body,
        mesh=mesh,
        in_specs=(split, P())
        + (flat,) * 6
        + (P("dp", "mp"), P("dp", "mp"), P("mp", "dp"))
        + (P(),) * 9
        + (split,),
        out_specs=(split, split)
        + (flat,) * 6
        + (P("dp", "mp"), P("dp", "mp"), P("mp", "dp"))
        + (P(),) * 9,
        check_vma=False,
    )
```
